128 devices in a mesh: row: 8 (over x, z_hi), col: 16 (over y, z_lo, core).
Axes of the slice: x: 4, y: 4, z: 4 (z_hi: 2, z_lo: 2; z = z_hi * 2 + z_lo), core: 2. Of those that a mesh axis runs over, the one named last changes fastest.
Arguments:
- pair: bfloat16 [1024, 65536], P('row', 'col'), may hold values from -6 to 6
- tile_mask: int32 [16, 16], replicated, may hold values from 0 to 1, as said below
- w_first: bfloat16 [3, 3, 64, 64], replicated, may hold values from -0.25 to 0.25
- b_first: float32 [64], replicated, may hold values from -3 to 3
- w_second: bfloat16 [3, 3, 64, 64], replicated, may hold values from -0.25 to 0.25
- b_second: float32 [64], replicated, may hold values from -3 to 3
- norm_gain: float32 [64], replicated, may hold values from 0.5 to 1.5
- w_proj: bfloat16 [64, 384], replicated, may hold values from -0.75 to 0.75
Outputs:
- update: bfloat16 [1024, 384], P(('row', 'col'))
The draws below stay inside these ranges and needn't reach their ends.
Inputs may be any that keep to these rules, and one draw needn't show every extreme that they name: tile_mask is symmetric and its diagonal is 1; it is constant on blocks of tiles that belong to one pair of chains.
All inputs are finite; a program needn't handle non-finite values.
Results may differ from the reference program's by a relative error of at most 0.015.
Values may be sent and summed in bfloat16 or wider, within the bound.
A program may use at most 64 MiB of HBM per device.

```python
import jax
import jax.numpy as jnp
from jax import lax

TILE = 64
C = 64
OUT = 384
L = 1024
NT = 16


def draw_tile_mask(key, part):
    chain_key, link_key = jax.random.split(jax.random.fold_in(key, 11))
    breaks = (jax.random.randint(chain_key, (NT,), 0, 3) == 0).astype(jnp.int32)
    breaks = breaks.at[0].set(0)
    chain_ids = jnp.cumsum(breaks).astype(jnp.int32)
    links = jnp.triu(jax.random.randint(link_key, (NT, NT), 0, 2).astype(jnp.int32))
    linked = jnp.maximum(links, links.T)
    linked = jnp.maximum(linked, jnp.eye(NT, dtype=jnp.int32))
    return linked[chain_ids[:, None], chain_ids[None, :]].astype(jnp.int32)


def levels(own_key, extent, cuts, low, top_value):
    def one(axis_at, parts):
        steps = jax.random.uniform(jax.random.fold_in(jax.random.fold_in(own_key, 6), axis_at), (parts,), jnp.float32, low / len(cuts), top_value / len(cuts))
        return jnp.repeat(jnp.exp(steps), extent[axis_at] // parts).reshape((-1,) + (1,) * (len(extent) - axis_at - 1))

    gain = one(*cuts[0])
    for cut in cuts[1:]:
        gain = gain * one(*cut)
    return gain


def scatter_about(rng, extent, width, reach, pieces=(), held_as=jnp.bfloat16):
    values = width * jax.random.normal(rng, extent, jnp.float32)
    if pieces:
        values = values * levels(rng, extent, pieces, -0.22, 0.18)
    return jnp.clip(values, -reach, reach).astype(held_as)


def setup_inputs(seed: int = 0) -> dict:
    arg_keys = jax.random.split(jax.random.key(seed), 9)
    return {
        "pair": scatter_about(arg_keys[0], (L, L * C), 1.0, 6.0, ((0, 8), (1, 16))),
        "tile_mask": draw_tile_mask(jax.random.fold_in(arg_keys[8], 71), 0),
        "w_first": scatter_about(arg_keys[2], (3, 3, C, C), (9 * C) ** -0.5, 0.25),
        "b_first": scatter_about(arg_keys[3], (C,), 0.5, 3.0, (), jnp.float32),
        "w_second": scatter_about(arg_keys[4], (3, 3, C, C), (9 * C) ** -0.5, 0.25),
        "b_second": scatter_about(arg_keys[5], (C,), 0.5, 3.0, (), jnp.float32),
        "norm_gain": jnp.clip(jax.random.uniform(arg_keys[6], (C,), jnp.float32, 0.5, 1.5), 0.5, 1.5),
        "w_proj": scatter_about(arg_keys[7], (C, OUT), C ** -0.5, 0.75),
    }


EPSILON = 1e-05

def dilated(field, kernel, dilation):
    return lax.conv_general_dilated(field[None], kernel.astype(jnp.float32), (1, 1), ((0, 0), (dilation, dilation)), rhs_dilation=(dilation, dilation), dimension_numbers=('NHWC', 'HWIO', 'NHWC'), precision=lax.Precision.HIGHEST)[0]

def reference(pair, tile_mask, w_first, b_first, w_second, b_second, norm_gain, w_proj):
    pair_cells = pair.reshape(L, L, C)
    cell_mask = jnp.repeat(jnp.repeat(tile_mask.astype(jnp.float32), TILE, axis=0), TILE, axis=1)
    padded = jnp.pad(pair_cells, ((6, 6), (0, 0), (0, 0)))
    mask_pad = jnp.pad(cell_mask, ((6, 6), (0, 0)))

    def stripe_step(col_total, tile_index):
        top_row = (tile_index * TILE).astype(jnp.int32)
        zero = jnp.zeros((), jnp.int32)
        window = lax.dynamic_slice(padded, (top_row, zero, zero), (TILE + 12, L, C)).astype(jnp.float32)
        first_out = dilated(window, w_first, 2) + b_first
        outer_mask = lax.dynamic_slice(mask_pad, (top_row + 2, zero), (TILE + 8, L))
        hidden = (outer_mask[:, :, None] * jax.nn.elu(first_out)).astype(jnp.bfloat16)
        hidden = lax.optimization_barrier(hidden)
        second_out = dilated(hidden.astype(jnp.float32), w_second, 4) + b_second
        inner_mask = lax.dynamic_slice(mask_pad, (top_row + 6, zero), (TILE, L))
        result = (inner_mask[:, :, None] * (window[6:6 + TILE] + second_out)).astype(jnp.bfloat16)
        row_part = lax.optimization_barrier(jnp.sum(result, axis=1, dtype=jnp.float32))
        return (col_total + lax.optimization_barrier(jnp.sum(result, axis=0, dtype=jnp.float32)), row_part)
    col_total, row_parts = lax.scan(stripe_step, jnp.zeros((L, C), jnp.float32), jnp.arange(NT, dtype=jnp.int32))
    pooled = row_parts.reshape(L, C) + col_total
    center = lax.optimization_barrier(jnp.mean(pooled, axis=1, keepdims=True))
    spread = lax.optimization_barrier(jnp.mean((pooled - center) ** 2, axis=1, keepdims=True))
    normed = ((pooled - center) / jnp.sqrt(spread + EPSILON) * norm_gain).astype(jnp.bfloat16)
    return jnp.dot(normed, w_proj, preferred_element_type=jnp.float32).astype(jnp.bfloat16)
```

```python
import functools

import jax
import jax.numpy as jnp
from jax import lax
from jax.experimental import pallas as pl
from jax.experimental.pallas import tpu as pltpu
from jax.sharding import PartitionSpec as P

TILE = 64
EPSILON = 1e-05
MESH = pl.DeviceIdType.MESH
F32 = jnp.float32
BF16 = jnp.bfloat16

ROWS = 128
PAIRS = 32
EDGE = 16
GROUPS = 16
OWN = 128
LANES = PAIRS * 128


def elu(v):
    return jnp.where(v > 0, v, jnp.exp(jnp.minimum(v, 0.0)) - 1.0)


def kernel(
    n_row, n_col,
    pair, mask, w1, b1, w2, b2, gain, wp,
    out,
    xe, xm, xp, hb, wt1, wt2, bias, hs, xs, racc, cacc, csum, rsend, csend, rrecv, crecv, total, res,
    load_sem, halo_send, halo_recv, row_send, row_recv, col_send, col_recv,
):
    r = lax.axis_index("row")
    c = lax.axis_index("col")
    me = r * n_col + c
    n_all = n_row * n_col

    load = pltpu.make_async_copy(pair, xe.at[pl.ds(EDGE, ROWS), pl.ds(OWN, LANES)], load_sem)
    load.start()

    barrier = pltpu.get_barrier_semaphore()

    def greet(tr, tc):
        same = jnp.logical_and(tr == r, tc == c)

        @pl.when(jnp.logical_not(same))
        def _():
            pl.semaphore_signal(barrier, inc=1, device_id=(tr, tc), device_id_type=MESH)

    up, down = lax.rem(r + n_row - 1, n_row), lax.rem(r + 1, n_row)
    left, right = lax.rem(c + n_col - 1, n_col), lax.rem(c + 1, n_col)
    top, bottom = pl.ds(0, EDGE), pl.ds(ROWS - EDGE, EDGE)
    first, last = pl.ds(0, 128), pl.ds(LANES - 128, 128)
    above, below, whole = pl.ds(0, EDGE), pl.ds(EDGE + ROWS, EDGE), pl.ds(EDGE, ROWS)
    before, after, inside = pl.ds(0, 128), pl.ds(OWN + LANES, 128), pl.ds(OWN, LANES)
    every, every_row = pl.ds(0, LANES), pl.ds(0, ROWS)
    halos = [
        (up, c, top, every, below, inside),
        (down, c, bottom, every, above, inside),
        (r, left, every_row, first, whole, after),
        (r, right, every_row, last, whole, before),
        (up, left, top, first, below, after),
        (up, right, top, last, below, before),
        (down, left, bottom, first, above, after),
        (down, right, bottom, last, above, before),
    ]
    for halo in halos:
        pl.semaphore_signal(barrier, inc=1, device_id=(halo[0], halo[1]), device_id_type=MESH)

    @pl.loop(1, n_col)
    def _(k):
        pl.semaphore_signal(
            barrier, inc=1, device_id=(r, lax.rem(c + k, n_col)), device_id_type=MESH
        )

    for edge, other in ((0, up), (n_col - 1, down)):
        @pl.when(c == edge)
        def _():
            @pl.loop(0, n_col)
            def _(k):
                pl.semaphore_signal(barrier, inc=1, device_id=(other, k), device_id_type=MESH)

    block = me // 8
    part = lax.rem(me, 8)

    @pl.loop(0, n_row)
    def _(k):
        greet(k, block)

    for edge, step in ((0, n_col - 1), (7, 1)):
        @pl.when(part == edge)
        def _():
            @pl.loop(0, n_row)
            def _(k):
                greet(k, lax.rem(block + step, n_col))

    zero = jnp.zeros((64, 64), BF16)
    wt1[...] = jnp.zeros_like(wt1)
    for a in range(3):
        for b in range(3):
            w = w1[a, b]
            doubled = jnp.concatenate(
                [jnp.concatenate([w, zero], axis=1), jnp.concatenate([zero, w], axis=1)], axis=0
            )
            for n in range(2):
                wt1[pl.ds(a * 512 + (b + n) * 128, 128), pl.ds(n * 128, 128)] = doubled
            w = w2[a, b]
            wt2[pl.ds((a * 3 + b) * 128, 128), :] = jnp.concatenate(
                [jnp.concatenate([w, zero], axis=1), jnp.concatenate([zero, w], axis=1)], axis=0
            )
    bias_one = jnp.concatenate([b1[...]] * 4, axis=1)
    bias_two = jnp.concatenate([b2[...]] * 2, axis=1)

    def tile(t, v):
        ti = 2 * r - 1 + t
        tj = c + v
        ok = (ti >= 0) & (ti < 2 * n_row) & (tj >= 0) & (tj < n_col)
        value = mask[jnp.clip(ti, 0, 2 * n_row - 1), jnp.clip(tj, 0, n_col - 1)]
        return jnp.where(ok, value, 0).astype(F32)

    mt = [[tile(t, v) for v in (0, -1, 1)] for t in range(4)]

    def by_row(rows, v):
        return jnp.where(
            rows < 0, mt[0][v], jnp.where(rows < 64, mt[1][v], jnp.where(rows < 128, mt[2][v], mt[3][v]))
        )

    to_self = lax.rem(me - 8 * c + 1 + n_all, n_all) < 10
    pl.semaphore_wait(barrier, 8 + (n_col - 1) + 2 + 10 - jnp.where(to_self, 1, 0))
    copies = []
    for k, (tr, tc, src_rows, src_lanes, dst_rows, dst_lanes) in enumerate(halos):
        copy = pltpu.make_async_remote_copy(
            src_ref=pair.at[src_rows, src_lanes],
            dst_ref=xe.at[dst_rows, dst_lanes],
            send_sem=halo_send.at[k],
            recv_sem=halo_recv.at[k],
            device_id=(tr, tc),
            device_id_type=MESH,
        )
        copy.start()
        copies.append(copy)

    load.wait()

    def shift(r0, lanes):
        window = xe[pl.ds(r0, 48), lanes]
        xm[pl.ds(r0, 16), lanes] = window[14:30]
        xp[pl.ds(r0, 16), lanes] = window[18:34]

    def taps(r0, rows, g):
        lanes = pl.ds(g * 256, 512)
        return jnp.concatenate(
            [xm[pl.ds(r0, rows), lanes], xe[pl.ds(EDGE + r0, rows), lanes], xp[pl.ds(r0, rows), lanes]],
            axis=1,
        )

    def hidden(r0, rows, groups):
        lhs = jnp.concatenate([taps(r0, rows, g) for g in groups], axis=0)
        h = elu(jnp.dot(lhs, wt1[...], preferred_element_type=F32) + bias_one)
        parts = [h[k * rows : (k + 1) * rows] for k in range(len(groups))]
        for g, piece in zip(groups, parts):
            hb[pl.ds(r0, rows), pl.ds(g * 256, 256)] = piece.astype(BF16)
        return parts

    def fold(parts):
        both = functools.reduce(jnp.add, parts)
        return both[:, :128] + both[:, 128:]

    def sum_x(r0):
        cells = xe[pl.ds(EDGE + r0, 16), pl.ds(OWN, LANES)].astype(F32)
        xs[pl.ds(r0, 16), :] = functools.reduce(
            jnp.add, [cells[:, p * 128 : (p + 1) * 128] for p in range(PAIRS)]
        )

    @pl.loop(0, 6)
    def _(k):
        r0 = pl.multiple_of(16 + 16 * k, 16)
        shift(r0, pl.ds(OWN, LANES))
        hs[1, pl.ds(r0, 16), :] = fold(hidden(r0, 16, range(1, GROUPS - 1)))
        sum_x(r0)

    for copy in copies:
        copy.wait()

    @pl.when(r == 0)
    def _():
        xe[above, :] = jnp.zeros((EDGE, xe.shape[1]), BF16)

    @pl.when(r == n_row - 1)
    def _():
        xe[below, :] = jnp.zeros((EDGE, xe.shape[1]), BF16)

    @pl.when(c == 0)
    def _():
        xe[:, before] = jnp.zeros((xe.shape[0], 128), BF16)

    @pl.when(c == n_col - 1)
    def _():
        xe[:, after] = jnp.zeros((xe.shape[0], 128), BF16)

    for r0 in range(16, ROWS - 16, 16):
        shift(r0, before)
        shift(r0, after)

    @pl.loop(0, 2)
    def _(k):
        r0 = pl.multiple_of((ROWS - 16) * k, 16)
        shift(r0, pl.ds(0, xe.shape[1]))
        parts = hidden(r0, 16, range(GROUPS))
        hs[0, pl.ds(r0, 16), :] = fold(parts[:1])
        hs[1, pl.ds(r0, 16), :] = fold(parts[1:-1])
        hs[2, pl.ds(r0, 16), :] = fold(parts[-1:])
        sum_x(r0)

    parts = hidden(16, ROWS - 32, (0, GROUPS - 1))
    hs[0, pl.ds(16, ROWS - 32), :] = fold(parts[:1])
    hs[2, pl.ds(16, ROWS - 32), :] = fold(parts[1:])

    def split(values):
        high = values.astype(BF16)
        return jnp.concatenate([high, (values - high.astype(F32)).astype(BF16)], axis=0)

    rows = lax.broadcasted_iota(jnp.int32, (ROWS, 128), 0)
    own = by_row(rows, 0)
    sum_l, sum_m, sum_r = (hs[k] * own for k in range(3))
    racc[...] = jnp.zeros_like(racc)
    racc[pl.ds(8, ROWS), :] = (xs[...] + 32.0 * bias_two) * own
    for a in range(3):
        out_rows = rows - 4 * (a - 1)
        m0, ml, mr = (by_row(out_rows, v) for v in range(3))
        lhs = split(
            jnp.concatenate(
                [
                    m0 * (sum_l + sum_m) + mr * sum_r,
                    m0 * (sum_l + sum_m + sum_r),
                    m0 * (sum_m + sum_r) + ml * sum_l,
                ],
                axis=1,
            )
        )
        both = jnp.dot(lhs, wt2[pl.ds(a * 384, 384), :], preferred_element_type=F32)
        racc[pl.ds(8 - 4 * (a - 1), ROWS), :] += both[:ROWS] + both[ROWS:]
    racc[...] = racc[...] + pltpu.roll(racc[...], 64, 1)
    half = lax.broadcasted_iota(jnp.int32, (72, 128), 1) < 64
    paired = jnp.where(half, racc[pl.ds(0, 72, stride=2), :], racc[pl.ds(1, 72, stride=2), :])
    for k in range(18):
        rsend[k] = paired[4 * k : 4 * k + 4]

    @pl.loop(0, 18)
    def _(k):
        target = lax.rem(me - c - 1 + k + n_all, n_all)
        slot = jnp.where((k == 0) | (k == 17), n_col + c, c)

        @pl.when(target == me)
        def _():
            pltpu.make_async_copy(rsend.at[k], rrecv.at[slot], row_recv.at[slot]).start()

        @pl.when(target != me)
        def _():
            pltpu.make_async_remote_copy(
                src_ref=rsend.at[k], dst_ref=rrecv.at[slot], send_sem=row_send.at[k],
                recv_sem=row_recv.at[slot], device_id=(target // n_col, lax.rem(target, n_col)),
                device_id_type=MESH,
            ).start()

    combos = [(a, v) for a in range(3) for v in range(3)]
    at = lax.broadcasted_iota(jnp.int32, (16, 128), 1)
    which = lax.broadcasted_iota(jnp.int32, (16, 128), 0)
    own_at = by_row(at, 0)
    pick = jnp.zeros((16, 128), F32)
    for k, (a, v) in enumerate(combos):
        pick = jnp.where(which == k, by_row(at - 4 * (a - 1), v), pick)
    pick = jnp.concatenate([pick * own_at, jnp.where(which == 9, own_at, 0.0)], axis=1).astype(BF16)
    for g in range(GROUPS):
        cells = jnp.concatenate(
            [hb[:, pl.ds(g * 256, 256)], xe[pl.ds(EDGE, ROWS), pl.ds(OWN + g * 256, 256)]], axis=0
        )
        sums = jnp.dot(pick, cells, preferred_element_type=F32)
        csum[pl.ds(g * 32, 16), :] = sums[:, :128]
        csum[pl.ds(g * 32 + 16, 16), :] = sums[:, 128:]

    def column(k):
        return csum[pl.ds(k, PAIRS, stride=16), :]

    at_pair = lax.broadcasted_iota(jnp.int32, (PAIRS, 128), 0)
    cacc[...] = jnp.zeros_like(cacc)
    cacc[pl.ds(8, PAIRS), :] = column(9) + bias_two * (64.0 * (mt[1][0] + mt[2][0]))
    for b in range(3):
        pieces = []
        for a in range(3):
            value = column(3 * a)
            if b == 0:
                value = jnp.where(at_pair >= PAIRS - 2, column(3 * a + 2), value)
            if b == 2:
                value = jnp.where(at_pair < 2, column(3 * a + 1), value)
            pieces.append(value)
        weights = jnp.concatenate([wt2[pl.ds((a * 3 + b) * 128, 128), :] for a in range(3)], axis=0)
        both = jnp.dot(split(jnp.concatenate(pieces, axis=1)), weights, preferred_element_type=F32)
        cacc[pl.ds(8 - 2 * (b - 1), PAIRS), :] += both[:PAIRS] + both[PAIRS:]
    columns = cacc[pl.ds(4, 40), :]
    for k in range(10):
        csend[k] = columns[4 * k : 4 * k + 4]

    @pl.loop(0, 10)
    def _(k):
        target = lax.rem(8 * c - 1 + k + n_all, n_all)
        slot = jnp.where((k == 0) | (k == 9), n_row + r, r)

        @pl.when(target == me)
        def _():
            pltpu.make_async_copy(csend.at[k], crecv.at[slot], col_recv.at[slot]).start()

        @pl.when(target != me)
        def _():
            pltpu.make_async_remote_copy(
                src_ref=csend.at[k], dst_ref=crecv.at[slot], send_sem=col_send.at[k],
                recv_sem=col_recv.at[slot], device_id=(target // n_col, lax.rem(target, n_col)),
                device_id_type=MESH,
            ).start()

    def arrived(buffer, sem, first_slot, count):
        for k in range(first_slot, first_slot + count):
            pltpu.make_async_copy(buffer.at[k], buffer.at[k], sem.at[k]).wait()
        return jnp.sum(buffer[pl.ds(first_slot, count)], axis=0)

    total[...] = arrived(rrecv, row_recv, 0, n_col) + arrived(crecv, col_recv, 0, n_row)

    @pl.when((c == 0) | (c == n_col - 1))
    def _():
        total[...] += arrived(rrecv, row_recv, n_col, n_col)

    @pl.when((part == 0) | (part == 7))
    def _():
        total[...] += arrived(crecv, col_recv, n_row, n_row)

    sums = total[...]
    res[pl.ds(0, 4, stride=2), :] = sums
    res[pl.ds(1, 4, stride=2), :] = pltpu.roll(sums, 64, 1)
    pooled = res[:, :64]
    center = jnp.mean(pooled, axis=1, keepdims=True)
    spread = jnp.mean((pooled - center) ** 2, axis=1, keepdims=True)
    normed = ((pooled - center) / jnp.sqrt(spread + EPSILON) * gain[...]).astype(BF16)
    out[...] = jnp.dot(normed, wp[...], preferred_element_type=F32).astype(BF16)

    @pl.loop(0, 18)
    def _(k):
        @pl.when(lax.rem(me - c - 1 + k + n_all, n_all) != me)
        def _():
            pltpu.make_async_copy(rsend.at[k], rsend.at[k], row_send.at[k]).wait()

    @pl.loop(0, 10)
    def _(k):
        @pl.when(lax.rem(8 * c - 1 + k + n_all, n_all) != me)
        def _():
            pltpu.make_async_copy(csend.at[k], csend.at[k], col_send.at[k]).wait()


def body(pair, tile_mask, w_first, b_first, w_second, b_second, norm_gain, w_proj):
    n_row, n_col = lax.axis_size("row"), lax.axis_size("col")
    vmem = pl.BlockSpec(memory_space=pltpu.VMEM)
    return pl.pallas_call(
        functools.partial(kernel, n_row, n_col),
        out_shape=jax.ShapeDtypeStruct((8, w_proj.shape[1]), BF16),
        in_specs=[pl.BlockSpec(memory_space=pl.ANY), pl.BlockSpec(memory_space=pltpu.SMEM)] + [vmem] * 6,
        out_specs=vmem,
        scratch_shapes=[
            pltpu.VMEM((ROWS + 2 * EDGE, LANES + 256), BF16),
            pltpu.VMEM((ROWS, LANES + 256), BF16),
            pltpu.VMEM((ROWS, LANES + 256), BF16),
            pltpu.VMEM((ROWS, LANES), BF16),
            pltpu.VMEM((1536, 256), BF16),
            pltpu.VMEM((1152, 128), BF16),
            pltpu.VMEM((8, 256), F32),
            pltpu.VMEM((3, ROWS, 128), F32),
            pltpu.VMEM((ROWS, 128), F32),
            pltpu.VMEM((144, 128), F32),
            pltpu.VMEM((48, 128), F32),
            pltpu.VMEM((512, 128), F32),
            pltpu.VMEM((18, 4, 128), F32),
            pltpu.VMEM((10, 4, 128), F32),
            pltpu.VMEM((32, 4, 128), F32),
            pltpu.VMEM((16, 4, 128), F32),
            pltpu.VMEM((4, 128), F32),
            pltpu.VMEM((8, 128), F32),
            pltpu.SemaphoreType.DMA,
            pltpu.SemaphoreType.DMA((8,)),
            pltpu.SemaphoreType.DMA((8,)),
            pltpu.SemaphoreType.DMA((18,)),
            pltpu.SemaphoreType.DMA((32,)),
            pltpu.SemaphoreType.DMA((10,)),
            pltpu.SemaphoreType.DMA((16,)),
        ],
        compiler_params=pltpu.CompilerParams(
            collective_id=0, has_side_effects=True, vmem_limit_bytes=40 * 1024 * 1024
        ),
        name="block",
    )(
        pair, tile_mask, w_first, b_first.reshape(1, -1), w_second, b_second.reshape(1, -1),
        norm_gain.reshape(1, -1), w_proj,
    )


def solution(mesh):
    return jax.shard_map(
        body,
        mesh=mesh,
        in_specs=(P("row", "col"), P(), P(), P(), P(), P(), P(), P()),
        out_specs=P(("row", "col"), None),
        check_vma=False,
    )
```

```python
import functools

import jax
import jax.numpy as jnp
from jax import lax
from jax.experimental import pallas as pl
from jax.experimental.pallas import tpu as pltpu
from jax.sharding import PartitionSpec as P

TILE = 64
EPSILON = 1e-05
MESH = pl.DeviceIdType.MESH
F32 = jnp.float32
BF16 = jnp.bfloat16

ROWS = 128
PAIRS = 32
EDGE = 16
GROUPS = 16
OWN = 128
LANES = PAIRS * 128


def elu(v):
    return jnp.where(v > 0, v, jnp.exp(jnp.minimum(v, 0.0)) - 1.0)


def kernel(
    n_row, n_col,
    pair, mask_in, w1_in, b1_in, w2_in, b2_in, gain_in, wp_in,
    out,
    mask, w1, b1, w2, b2, gain, wp, xe, xm, xp, hb, wt1, wt2, hs, xs, racc, cacc, csum, packed, landed, rsend, csend, rrecv, crecv, total, res,
    load_sem, small_sem, halo_send, halo_recv, row_send, row_recv, col_send, col_recv,
):
    r = lax.axis_index("row")
    c = lax.axis_index("col")
    me = r * n_col + c
    n_all = n_row * n_col

    loads = [
        pltpu.make_async_copy(
            pair.at[pl.ds(start, size)], xe.at[pl.ds(EDGE + start, size), pl.ds(OWN, LANES)], load_sem.at[k]
        )
        for k, (start, size) in enumerate(((0, EDGE), (ROWS - EDGE, EDGE), (EDGE, ROWS - 2 * EDGE)))
    ]
    for copy in loads:
        copy.start()
    small = [(mask_in, mask), (w1_in, w1), (w2_in, w2), (b1_in, b1), (b2_in, b2), (gain_in, gain), (wp_in, wp)]
    small = [
        pltpu.make_async_copy(src, dst, small_sem.at[k]) for k, (src, dst) in enumerate(small)
    ]
    for copy in small:
        copy.start()

    barrier = pltpu.get_barrier_semaphore()

    def greet(tr, tc):
        same = jnp.logical_and(tr == r, tc == c)

        @pl.when(jnp.logical_not(same))
        def _():
            pl.semaphore_signal(barrier, inc=1, device_id=(tr, tc), device_id_type=MESH)

    up, down = lax.rem(r + n_row - 1, n_row), lax.rem(r + 1, n_row)
    left, right = lax.rem(c + n_col - 1, n_col), lax.rem(c + 1, n_col)
    top, bottom = pl.ds(0, EDGE), pl.ds(ROWS - EDGE, EDGE)
    first, last = pl.ds(0, 128), pl.ds(LANES - 128, 128)
    above, below, whole = pl.ds(0, EDGE), pl.ds(EDGE + ROWS, EDGE), pl.ds(EDGE, ROWS)
    before, after = pl.ds(0, 128), pl.ds(OWN + LANES, 128)
    halos = [
        (up, c, packed.at[0], landed.at[1]),
        (down, c, packed.at[1], landed.at[0]),
        (r, left, pair.at[:, first], xe.at[whole, after]),
        (r, right, pair.at[:, last], xe.at[whole, before]),
        (up, left, pair.at[top, first], xe.at[below, after]),
        (up, right, pair.at[top, last], xe.at[below, before]),
        (down, left, pair.at[bottom, first], xe.at[above, after]),
        (down, right, pair.at[bottom, last], xe.at[above, before]),
    ]
    for halo in halos:
        pl.semaphore_signal(barrier, inc=1, device_id=(halo[0], halo[1]), device_id_type=MESH)

    @pl.loop(1, n_col)
    def _(k):
        pl.semaphore_signal(
            barrier, inc=1, device_id=(r, lax.rem(c + k, n_col)), device_id_type=MESH
        )

    for edge, other in ((0, up), (n_col - 1, down)):
        @pl.when(c == edge)
        def _():
            @pl.loop(0, n_col)
            def _(k):
                pl.semaphore_signal(barrier, inc=1, device_id=(other, k), device_id_type=MESH)

    block = me // 8
    part = lax.rem(me, 8)

    @pl.loop(0, n_row)
    def _(k):
        greet(k, block)

    for edge, step in ((0, n_col - 1), (7, 1)):
        @pl.when(part == edge)
        def _():
            @pl.loop(0, n_row)
            def _(k):
                greet(k, lax.rem(block + step, n_col))

    to_self = lax.rem(me - 8 * c + 1 + n_all, n_all) < 10
    pl.semaphore_wait(barrier, 8 + (n_col - 1) + 2 + 10 - jnp.where(to_self, 1, 0))
    copies = []

    def send(k):
        tr, tc, src, dst = halos[k]
        copy = pltpu.make_async_remote_copy(
            src_ref=src, dst_ref=dst, send_sem=halo_send.at[k], recv_sem=halo_recv.at[k],
            device_id=(tr, tc), device_id_type=MESH,
        )
        copy.start()
        copies.append(copy)

    for k in range(2, 8):
        send(k)

    for k, row in ((0, 0), (1, EDGE - 2)):
        loads[k].wait()
        cells = jnp.concatenate(
            [xe[pl.ds(EDGE + (ROWS - EDGE) * k, EDGE), pl.ds(OWN + 512 * p, 512)] for p in range(8)], axis=0
        )
        i = lax.broadcasted_iota(jnp.int32, (16, 128), 0)
        j = lax.broadcasted_iota(jnp.int32, (16, 128), 1)
        select = jnp.where(j == (i // 2) * 16 + row + i % 2, 1.0, 0.0).astype(BF16)
        packed[k] = jnp.dot(select, cells, preferred_element_type=F32).astype(BF16)
        send(k)

    for copy in small:
        copy.wait()

    zero = jnp.zeros((64, 64), BF16)
    wt1[...] = jnp.zeros_like(wt1)
    for a in range(3):
        for b in range(3):
            w = w1[a, b]
            doubled = jnp.concatenate(
                [jnp.concatenate([w, zero], axis=1), jnp.concatenate([zero, w], axis=1)], axis=0
            )
            for n in range(2):
                wt1[pl.ds(a * 512 + (b + n) * 128, 128), pl.ds(n * 128, 128)] = doubled
            w = w2[a, b]
            wt2[pl.ds((a * 3 + b) * 128, 128), :] = jnp.concatenate(
                [jnp.concatenate([w, zero], axis=1), jnp.concatenate([zero, w], axis=1)], axis=0
            )
    bias_one = jnp.concatenate([b1[...]] * 4, axis=1)
    bias_two = jnp.concatenate([b2[...]] * 2, axis=1)

    def tile(t, v):
        ti = 2 * r - 1 + t
        tj = c + v
        ok = (ti >= 0) & (ti < 2 * n_row) & (tj >= 0) & (tj < n_col)
        value = mask[jnp.clip(ti, 0, 2 * n_row - 1), jnp.clip(tj, 0, n_col - 1)]
        return jnp.where(ok, value, 0).astype(F32)

    mt = [[tile(t, v) for v in (0, -1, 1)] for t in range(4)]

    def by_row(rows, v):
        return jnp.where(
            rows < 0, mt[0][v], jnp.where(rows < 64, mt[1][v], jnp.where(rows < 128, mt[2][v], mt[3][v]))
        )

    loads[2].wait()

    def shift(r0, lanes):
        window = xe[pl.ds(r0, 48), lanes]
        xm[pl.ds(r0, 16), lanes] = window[14:30]
        xp[pl.ds(r0, 16), lanes] = window[18:34]

    def taps(r0, rows, g):
        lanes = pl.ds(g * 256, 512)
        return jnp.concatenate(
            [xm[pl.ds(r0, rows), lanes], xe[pl.ds(EDGE + r0, rows), lanes], xp[pl.ds(r0, rows), lanes]],
            axis=1,
        )

    def hidden(r0, rows, groups):
        lhs = jnp.concatenate([taps(r0, rows, g) for g in groups], axis=0)
        h = elu(jnp.dot(lhs, wt1[...], preferred_element_type=F32) + bias_one)
        parts = [h[k * rows : (k + 1) * rows] for k in range(len(groups))]
        for g, piece in zip(groups, parts):
            hb[pl.ds(r0, rows), pl.ds(g * 256, 256)] = piece.astype(BF16)
        return parts

    def fold(parts):
        both = functools.reduce(jnp.add, parts)
        return both[:, :128] + both[:, 128:]

    def sum_x(r0):
        cells = xe[pl.ds(EDGE + r0, 16), pl.ds(OWN, LANES)].astype(F32)
        xs[pl.ds(r0, 16), :] = functools.reduce(
            jnp.add, [cells[:, p * 128 : (p + 1) * 128] for p in range(PAIRS)]
        )

    @pl.loop(0, 6)
    def _(k):
        r0 = pl.multiple_of(16 + 16 * k, 16)
        shift(r0, pl.ds(OWN, LANES))
        hs[1, pl.ds(r0, 16), :] = fold(hidden(r0, 16, range(1, GROUPS - 1)))
        sum_x(r0)

    for copy in copies:
        copy.wait()

    i = lax.broadcasted_iota(jnp.int32, (128, 16), 0)
    j = lax.broadcasted_iota(jnp.int32, (128, 16), 1)
    for k, (row, place) in enumerate(((EDGE - 2, above), (0, below))):
        at_row = i % 16 - row
        select = jnp.where((at_row >= 0) & (at_row < 2) & (j == (i // 16) * 2 + at_row), 1.0, 0.0)
        cells = jnp.dot(select.astype(BF16), landed[k], preferred_element_type=F32).astype(BF16)
        for p in range(8):
            xe[place, pl.ds(OWN + 512 * p, 512)] = cells[16 * p : 16 * p + 16]

    @pl.when(r == 0)
    def _():
        xe[above, :] = jnp.zeros((EDGE, xe.shape[1]), BF16)

    @pl.when(r == n_row - 1)
    def _():
        xe[below, :] = jnp.zeros((EDGE, xe.shape[1]), BF16)

    @pl.when(c == 0)
    def _():
        xe[:, before] = jnp.zeros((xe.shape[0], 128), BF16)

    @pl.when(c == n_col - 1)
    def _():
        xe[:, after] = jnp.zeros((xe.shape[0], 128), BF16)

    for r0 in range(16, ROWS - 16, 16):
        shift(r0, before)
        shift(r0, after)

    @pl.loop(0, 2)
    def _(k):
        r0 = pl.multiple_of((ROWS - 16) * k, 16)
        shift(r0, pl.ds(0, xe.shape[1]))
        parts = hidden(r0, 16, range(GROUPS))
        hs[0, pl.ds(r0, 16), :] = fold(parts[:1])
        hs[1, pl.ds(r0, 16), :] = fold(parts[1:-1])
        hs[2, pl.ds(r0, 16), :] = fold(parts[-1:])
        sum_x(r0)

    parts = hidden(16, ROWS - 32, (0, GROUPS - 1))
    hs[0, pl.ds(16, ROWS - 32), :] = fold(parts[:1])
    hs[2, pl.ds(16, ROWS - 32), :] = fold(parts[1:])

    def split(values):
        high = values.astype(BF16)
        return jnp.concatenate([high, (values - high.astype(F32)).astype(BF16)], axis=0)

    rows = lax.broadcasted_iota(jnp.int32, (ROWS, 128), 0)
    own = by_row(rows, 0)
    sum_l, sum_m, sum_r = (hs[k] * own for k in range(3))
    racc[...] = jnp.zeros_like(racc)
    racc[pl.ds(8, ROWS), :] = (xs[...] + 32.0 * bias_two) * own
    for a in range(3):
        out_rows = rows - 4 * (a - 1)
        m0, ml, mr = (by_row(out_rows, v) for v in range(3))
        lhs = split(
            jnp.concatenate(
                [
                    m0 * (sum_l + sum_m) + mr * sum_r,
                    m0 * (sum_l + sum_m + sum_r),
                    m0 * (sum_m + sum_r) + ml * sum_l,
                ],
                axis=1,
            )
        )
        both = jnp.dot(lhs, wt2[pl.ds(a * 384, 384), :], preferred_element_type=F32)
        racc[pl.ds(8 - 4 * (a - 1), ROWS), :] += both[:ROWS] + both[ROWS:]
    racc[...] = racc[...] + pltpu.roll(racc[...], 64, 1)
    half = lax.broadcasted_iota(jnp.int32, (72, 128), 1) < 64
    paired = jnp.where(half, racc[pl.ds(0, 72, stride=2), :], racc[pl.ds(1, 72, stride=2), :])
    for k in range(18):
        rsend[k] = paired[4 * k : 4 * k + 4]

    @pl.loop(0, 18)
    def _(k):
        target = lax.rem(me - c - 1 + k + n_all, n_all)
        slot = jnp.where((k == 0) | (k == 17), n_col + c, c)

        @pl.when(target == me)
        def _():
            pltpu.make_async_copy(rsend.at[k], rrecv.at[slot], row_recv.at[slot]).start()

        @pl.when(target != me)
        def _():
            pltpu.make_async_remote_copy(
                src_ref=rsend.at[k], dst_ref=rrecv.at[slot], send_sem=row_send.at[k],
                recv_sem=row_recv.at[slot], device_id=(target // n_col, lax.rem(target, n_col)),
                device_id_type=MESH,
            ).start()

    combos = [(a, v) for a in range(3) for v in range(3)]
    at = lax.broadcasted_iota(jnp.int32, (16, 128), 1)
    which = lax.broadcasted_iota(jnp.int32, (16, 128), 0)
    own_at = by_row(at, 0)
    pick = jnp.zeros((16, 128), F32)
    for k, (a, v) in enumerate(combos):
        pick = jnp.where(which == k, by_row(at - 4 * (a - 1), v), pick)
    pick = jnp.concatenate([pick * own_at, jnp.where(which == 9, own_at, 0.0)], axis=1).astype(BF16)
    for g in range(GROUPS):
        cells = jnp.concatenate(
            [hb[:, pl.ds(g * 256, 256)], xe[pl.ds(EDGE, ROWS), pl.ds(OWN + g * 256, 256)]], axis=0
        )
        sums = jnp.dot(pick, cells, preferred_element_type=F32)
        csum[pl.ds(g * 32, 16), :] = sums[:, :128]
        csum[pl.ds(g * 32 + 16, 16), :] = sums[:, 128:]

    def column(k):
        return csum[pl.ds(k, PAIRS, stride=16), :]

    at_pair = lax.broadcasted_iota(jnp.int32, (PAIRS, 128), 0)
    cacc[...] = jnp.zeros_like(cacc)
    cacc[pl.ds(8, PAIRS), :] = column(9) + bias_two * (64.0 * (mt[1][0] + mt[2][0]))
    for b in range(3):
        pieces = []
        for a in range(3):
            value = column(3 * a)
            if b == 0:
                value = jnp.where(at_pair >= PAIRS - 2, column(3 * a + 2), value)
            if b == 2:
                value = jnp.where(at_pair < 2, column(3 * a + 1), value)
            pieces.append(value)
        weights = jnp.concatenate([wt2[pl.ds((a * 3 + b) * 128, 128), :] for a in range(3)], axis=0)
        both = jnp.dot(split(jnp.concatenate(pieces, axis=1)), weights, preferred_element_type=F32)
        cacc[pl.ds(8 - 2 * (b - 1), PAIRS), :] += both[:PAIRS] + both[PAIRS:]
    columns = cacc[pl.ds(4, 40), :]
    for k in range(10):
        csend[k] = columns[4 * k : 4 * k + 4]

    @pl.loop(0, 10)
    def _(k):
        target = lax.rem(8 * c - 1 + k + n_all, n_all)
        slot = jnp.where((k == 0) | (k == 9), n_row + r, r)

        @pl.when(target == me)
        def _():
            pltpu.make_async_copy(csend.at[k], crecv.at[slot], col_recv.at[slot]).start()

        @pl.when(target != me)
        def _():
            pltpu.make_async_remote_copy(
                src_ref=csend.at[k], dst_ref=crecv.at[slot], send_sem=col_send.at[k],
                recv_sem=col_recv.at[slot], device_id=(target // n_col, lax.rem(target, n_col)),
                device_id_type=MESH,
            ).start()

    def arrived(buffer, sem, first_slot, count):
        for k in range(first_slot, first_slot + count):
            pltpu.make_async_copy(buffer.at[k], buffer.at[k], sem.at[k]).wait()
        return jnp.sum(buffer[pl.ds(first_slot, count)], axis=0)

    total[...] = arrived(rrecv, row_recv, 0, n_col) + arrived(crecv, col_recv, 0, n_row)

    @pl.when((c == 0) | (c == n_col - 1))
    def _():
        total[...] += arrived(rrecv, row_recv, n_col, n_col)

    @pl.when((part == 0) | (part == 7))
    def _():
        total[...] += arrived(crecv, col_recv, n_row, n_row)

    sums = total[...]
    res[pl.ds(0, 4, stride=2), :] = sums
    res[pl.ds(1, 4, stride=2), :] = pltpu.roll(sums, 64, 1)
    pooled = res[:, :64]
    center = jnp.mean(pooled, axis=1, keepdims=True)
    spread = jnp.mean((pooled - center) ** 2, axis=1, keepdims=True)
    normed = ((pooled - center) / jnp.sqrt(spread + EPSILON) * gain[...]).astype(BF16)
    out[...] = jnp.dot(normed, wp[...], preferred_element_type=F32).astype(BF16)

    @pl.loop(0, 18)
    def _(k):
        @pl.when(lax.rem(me - c - 1 + k + n_all, n_all) != me)
        def _():
            pltpu.make_async_copy(rsend.at[k], rsend.at[k], row_send.at[k]).wait()

    @pl.loop(0, 10)
    def _(k):
        @pl.when(lax.rem(8 * c - 1 + k + n_all, n_all) != me)
        def _():
            pltpu.make_async_copy(csend.at[k], csend.at[k], col_send.at[k]).wait()


def body(pair, tile_mask, w_first, b_first, w_second, b_second, norm_gain, w_proj):
    n_row, n_col = lax.axis_size("row"), lax.axis_size("col")
    hbm = pl.BlockSpec(memory_space=pltpu.HBM)
    return pl.pallas_call(
        functools.partial(kernel, n_row, n_col),
        out_shape=jax.ShapeDtypeStruct((8, w_proj.shape[1]), BF16),
        in_specs=[hbm] * 8,
        out_specs=pl.BlockSpec(memory_space=pltpu.VMEM),
        scratch_shapes=[
            pltpu.SMEM(tile_mask.shape, jnp.int32),
            pltpu.VMEM(w_first.shape, BF16),
            pltpu.VMEM((1, 64), F32),
            pltpu.VMEM(w_second.shape, BF16),
            pltpu.VMEM((1, 64), F32),
            pltpu.VMEM((1, 64), F32),
            pltpu.VMEM(w_proj.shape, BF16),
            pltpu.VMEM((ROWS + 2 * EDGE, LANES + 256), BF16),
            pltpu.VMEM((ROWS, LANES + 256), BF16),
            pltpu.VMEM((ROWS, LANES + 256), BF16),
            pltpu.VMEM((ROWS, LANES), BF16),
            pltpu.VMEM((1536, 256), BF16),
            pltpu.VMEM((1152, 128), BF16),
            pltpu.VMEM((3, ROWS, 128), F32),
            pltpu.VMEM((ROWS, 128), F32),
            pltpu.VMEM((144, 128), F32),
            pltpu.VMEM((48, 128), F32),
            pltpu.VMEM((512, 128), F32),
            pltpu.VMEM((2, 16, 512), BF16),
            pltpu.VMEM((2, 16, 512), BF16),
            pltpu.VMEM((18, 4, 128), F32),
            pltpu.VMEM((10, 4, 128), F32),
            pltpu.VMEM((32, 4, 128), F32),
            pltpu.VMEM((16, 4, 128), F32),
            pltpu.VMEM((4, 128), F32),
            pltpu.VMEM((8, 128), F32),
            pltpu.SemaphoreType.DMA((3,)),
            pltpu.SemaphoreType.DMA((7,)),
            pltpu.SemaphoreType.DMA((8,)),
            pltpu.SemaphoreType.DMA((8,)),
            pltpu.SemaphoreType.DMA((18,)),
            pltpu.SemaphoreType.DMA((32,)),
            pltpu.SemaphoreType.DMA((10,)),
            pltpu.SemaphoreType.DMA((16,)),
        ],
        compiler_params=pltpu.CompilerParams(
            collective_id=0, has_side_effects=True, vmem_limit_bytes=64 * 1024 * 1024 - 65536
        ),
        name="block",
    )(
        pair, tile_mask, w_first, b_first.reshape(1, -1), w_second, b_second.reshape(1, -1),
        norm_gain.reshape(1, -1), w_proj,
    )


def solution(mesh):
    return jax.shard_map(
        body,
        mesh=mesh,
        in_specs=(P("row", "col"), P(), P(), P(), P(), P(), P(), P()),
        out_specs=P(("row", "col"), None),
        check_vma=False,
    )
```

```python
import functools

import jax
import jax.numpy as jnp
from jax import lax
from jax.experimental import pallas as pl
from jax.experimental.pallas import tpu as pltpu
from jax.sharding import PartitionSpec as P

TILE = 64
EPSILON = 1e-05
MESH = pl.DeviceIdType.MESH
F32 = jnp.float32
BF16 = jnp.bfloat16

ROWS = 128
PAIRS = 32
EDGE = 16
GROUPS = 16
OWN = 128
LANES = PAIRS * 128


def elu(v):
    return jnp.where(v > 0, v, jnp.exp(jnp.minimum(v, 0.0)) - 1.0)


def kernel(
    n_row, n_col,
    pair, mask_in, w1_in, b1_in, w2_in, b2_in, gain_in, wp_in,
    out,
    mask, w1, b1, w2, b2, gain, wp, xe, xm, xp, hb, wt1, wt2, hs, xs, racc, cacc, csum, packed, landed, rsend, csend, rrecv, crecv, total, res,
    ready, load_sem, small_sem, halo_send, halo_recv, row_send, row_recv, col_send, col_recv,
):
    r = lax.axis_index("row")
    c = lax.axis_index("col")
    me = r * n_col + c
    n_all = n_row * n_col

    loads = [
        pltpu.make_async_copy(
            pair.at[pl.ds(start, size)], xe.at[pl.ds(EDGE + start, size), pl.ds(OWN, LANES)], load_sem.at[k]
        )
        for k, (start, size) in enumerate(((0, EDGE), (ROWS - EDGE, EDGE), (EDGE, ROWS - 2 * EDGE)))
    ]
    small = [(mask_in, mask), (w1_in, w1), (w2_in, w2), (b1_in, b1), (b2_in, b2), (gain_in, gain), (wp_in, wp)]
    small = [
        pltpu.make_async_copy(src, dst, small_sem.at[k]) for k, (src, dst) in enumerate(small)
    ]
    barrier = pltpu.get_barrier_semaphore()

    def greet(semaphore, tr, tc):
        pl.semaphore_signal(semaphore, inc=1, device_id=(tr, tc), device_id_type=MESH)

    up, down = lax.rem(r + n_row - 1, n_row), lax.rem(r + 1, n_row)
    left, right = lax.rem(c + n_col - 1, n_col), lax.rem(c + 1, n_col)
    top, bottom = pl.ds(0, EDGE), pl.ds(ROWS - EDGE, EDGE)
    first, last = pl.ds(0, 128), pl.ds(LANES - 128, 128)
    above, below, whole = pl.ds(0, EDGE), pl.ds(EDGE + ROWS, EDGE), pl.ds(EDGE, ROWS)
    before, after = pl.ds(0, 128), pl.ds(OWN + LANES, 128)
    halos = [
        (up, c, packed.at[0], landed.at[1]),
        (down, c, packed.at[1], landed.at[0]),
        (r, left, pair.at[:, first], xe.at[whole, after]),
        (r, right, pair.at[:, last], xe.at[whole, before]),
        (up, left, pair.at[top, first], xe.at[below, after]),
        (up, right, pair.at[top, last], xe.at[below, before]),
        (down, left, pair.at[bottom, first], xe.at[above, after]),
        (down, right, pair.at[bottom, last], xe.at[above, before]),
    ]
    for k in range(1, n_row):
        greet(barrier, lax.rem(r + k, n_row), c)
    for halo in halos[4:]:
        greet(barrier, halo[0], halo[1])
    for k in range(1, n_col):
        greet(barrier, r, lax.rem(c + k, n_col))
    for copy in loads + small:
        copy.start()
    part = lax.rem(me, 8)

    for k, row in ((0, 0), (1, EDGE - 2)):
        loads[k].wait()
        cells = jnp.concatenate(
            [xe[pl.ds(EDGE + (ROWS - EDGE) * k, EDGE), pl.ds(OWN + 512 * p, 512)] for p in range(8)], axis=0
        )
        i = lax.broadcasted_iota(jnp.int32, (16, 128), 0)
        j = lax.broadcasted_iota(jnp.int32, (16, 128), 1)
        select = jnp.where(j == (i // 2) * 16 + row + i % 2, 1.0, 0.0).astype(BF16)
        packed[k] = jnp.dot(select, cells, preferred_element_type=F32).astype(BF16)

    pl.semaphore_wait(barrier, (n_row - 1) + 4 + (n_col - 1))
    copies = []
    for k in (0, 1, 4, 5, 6, 7, 2, 3):
        tr, tc, src, dst = halos[k]
        copy = pltpu.make_async_remote_copy(
            src_ref=src, dst_ref=dst, send_sem=halo_send.at[k], recv_sem=halo_recv.at[k],
            device_id=(tr, tc), device_id_type=MESH,
        )
        copy.start()
        copies.append(copy)
    for k in range(1, n_col):
        greet(ready, r, lax.rem(c + k, n_col))

    for copy in small:
        copy.wait()

    zero = jnp.zeros((64, 64), BF16)
    wt1[...] = jnp.zeros_like(wt1)
    for a in range(3):
        for b in range(3):
            w = w1[a, b]
            doubled = jnp.concatenate(
                [jnp.concatenate([w, zero], axis=1), jnp.concatenate([zero, w], axis=1)], axis=0
            )
            for n in range(2):
                wt1[pl.ds(a * 512 + (b + n) * 128, 128), pl.ds(n * 128, 128)] = doubled
            w = w2[a, b]
            wt2[pl.ds((a * 3 + b) * 128, 128), :] = jnp.concatenate(
                [jnp.concatenate([w, zero], axis=1), jnp.concatenate([zero, w], axis=1)], axis=0
            )
    bias_one = jnp.concatenate([b1[...]] * 4, axis=1)
    bias_two = jnp.concatenate([b2[...]] * 2, axis=1)

    def tile(t, v):
        ti = 2 * r - 1 + t
        tj = c + v
        ok = (ti >= 0) & (ti < 2 * n_row) & (tj >= 0) & (tj < n_col)
        value = mask[jnp.clip(ti, 0, 2 * n_row - 1), jnp.clip(tj, 0, n_col - 1)]
        return jnp.where(ok, value, 0).astype(F32)

    mt = [[tile(t, v) for v in (0, -1, 1)] for t in range(4)]

    def by_row(rows, v):
        return jnp.where(
            rows < 0, mt[0][v], jnp.where(rows < 64, mt[1][v], jnp.where(rows < 128, mt[2][v], mt[3][v]))
        )

    loads[2].wait()

    def shift(r0, lanes):
        window = xe[pl.ds(r0, 48), lanes]
        xm[pl.ds(r0, 16), lanes] = window[14:30]
        xp[pl.ds(r0, 16), lanes] = window[18:34]

    def taps(r0, rows, g):
        lanes = pl.ds(g * 256, 512)
        return jnp.concatenate(
            [xm[pl.ds(r0, rows), lanes], xe[pl.ds(EDGE + r0, rows), lanes], xp[pl.ds(r0, rows), lanes]],
            axis=1,
        )

    def hidden(r0, rows, groups):
        lhs = jnp.concatenate([taps(r0, rows, g) for g in groups], axis=0)
        h = elu(jnp.dot(lhs, wt1[...], preferred_element_type=F32) + bias_one)
        parts = [h[k * rows : (k + 1) * rows] for k in range(len(groups))]
        for g, piece in zip(groups, parts):
            hb[pl.ds(r0, rows), pl.ds(g * 256, 256)] = piece.astype(BF16)
        return parts

    def fold(parts):
        both = functools.reduce(jnp.add, parts)
        return both[:, :128] + both[:, 128:]

    def sum_x(r0):
        cells = xe[pl.ds(EDGE + r0, 16), pl.ds(OWN, LANES)].astype(F32)
        xs[pl.ds(r0, 16), :] = functools.reduce(
            jnp.add, [cells[:, p * 128 : (p + 1) * 128] for p in range(PAIRS)]
        )

    @pl.loop(0, 6)
    def _(k):
        r0 = pl.multiple_of(16 + 16 * k, 16)
        shift(r0, pl.ds(OWN, LANES))
        hs[1, pl.ds(r0, 16), :] = fold(hidden(r0, 16, range(1, GROUPS - 1)))
        sum_x(r0)

    at = lax.broadcasted_iota(jnp.int32, (16, 128), 1)
    own_at = by_row(at, 0)
    for g in range(GROUPS):
        sums = jnp.dot(
            own_at.astype(BF16), xe[pl.ds(EDGE, ROWS), pl.ds(OWN + g * 256, 256)], preferred_element_type=F32
        )
        csum[pl.ds(g * 32, 16), :] = sums[:, :128]
        csum[pl.ds(g * 32 + 16, 16), :] = sums[:, 128:]
    cacc[...] = jnp.zeros_like(cacc)
    cacc[pl.ds(8, PAIRS), :] = csum[pl.ds(0, PAIRS, stride=16), :] + bias_two * (
        64.0 * (mt[1][0] + mt[2][0])
    )
    sum_x(0)
    sum_x(ROWS - 16)

    for copy in copies:
        copy.wait()

    i = lax.broadcasted_iota(jnp.int32, (128, 16), 0)
    j = lax.broadcasted_iota(jnp.int32, (128, 16), 1)
    for k, (row, place) in enumerate(((EDGE - 2, above), (0, below))):
        at_row = i % 16 - row
        select = jnp.where((at_row >= 0) & (at_row < 2) & (j == (i // 16) * 2 + at_row), 1.0, 0.0)
        cells = jnp.dot(select.astype(BF16), landed[k], preferred_element_type=F32).astype(BF16)
        for p in range(8):
            xe[place, pl.ds(OWN + 512 * p, 512)] = cells[16 * p : 16 * p + 16]

    @pl.when(r == 0)
    def _():
        xe[above, :] = jnp.zeros((EDGE, xe.shape[1]), BF16)

    @pl.when(r == n_row - 1)
    def _():
        xe[below, :] = jnp.zeros((EDGE, xe.shape[1]), BF16)

    @pl.when(c == 0)
    def _():
        xe[:, before] = jnp.zeros((xe.shape[0], 128), BF16)

    @pl.when(c == n_col - 1)
    def _():
        xe[:, after] = jnp.zeros((xe.shape[0], 128), BF16)

    for r0 in range(16, ROWS - 16, 16):
        shift(r0, before)
        shift(r0, after)

    @pl.loop(0, 2)
    def _(k):
        r0 = pl.multiple_of((ROWS - 16) * k, 16)
        shift(r0, pl.ds(0, xe.shape[1]))
        parts = hidden(r0, 16, range(GROUPS))
        hs[0, pl.ds(r0, 16), :] = fold(parts[:1])
        hs[1, pl.ds(r0, 16), :] = fold(parts[1:-1])
        hs[2, pl.ds(r0, 16), :] = fold(parts[-1:])

    parts = hidden(16, ROWS - 32, (0, GROUPS - 1))
    hs[0, pl.ds(16, ROWS - 32), :] = fold(parts[:1])
    hs[2, pl.ds(16, ROWS - 32), :] = fold(parts[1:])

    def split(values):
        high = values.astype(BF16)
        return jnp.concatenate([high, (values - high.astype(F32)).astype(BF16)], axis=0)

    combos = [(a, v) for a in range(3) for v in range(3)]
    which = lax.broadcasted_iota(jnp.int32, (16, 128), 0)
    pick = jnp.zeros((16, 128), F32)
    for k, (a, v) in enumerate(combos):
        pick = jnp.where(which == k, by_row(at - 4 * (a - 1), v), pick)
    pick = (pick * own_at).astype(BF16)
    for g in range(GROUPS):
        sums = jnp.dot(pick, hb[:, pl.ds(g * 256, 256)], preferred_element_type=F32)
        csum[pl.ds(g * 32, 16), :] = sums[:, :128]
        csum[pl.ds(g * 32 + 16, 16), :] = sums[:, 128:]

    def column(k):
        return csum[pl.ds(k, PAIRS, stride=16), :]

    at_pair = lax.broadcasted_iota(jnp.int32, (PAIRS, 128), 0)
    for b in range(3):
        pieces = []
        for a in range(3):
            value = column(3 * a)
            if b == 0:
                value = jnp.where(at_pair >= PAIRS - 2, column(3 * a + 2), value)
            if b == 2:
                value = jnp.where(at_pair < 2, column(3 * a + 1), value)
            pieces.append(value)
        weights = jnp.concatenate([wt2[pl.ds((a * 3 + b) * 128, 128), :] for a in range(3)], axis=0)
        both = jnp.dot(split(jnp.concatenate(pieces, axis=1)), weights, preferred_element_type=F32)
        cacc[pl.ds(8 - 2 * (b - 1), PAIRS), :] += both[:PAIRS] + both[PAIRS:]
    columns = cacc[pl.ds(4, 40), :]
    for k in range(10):
        csend[k] = columns[4 * k : 4 * k + 4]

    pl.semaphore_wait(ready, n_col - 1)

    @pl.loop(0, 10)
    def _(k):
        target = lax.rem(8 * c - 1 + k + n_all, n_all)
        slot = jnp.where((k == 0) | (k == 9), n_row + r, r)

        @pl.when(target == me)
        def _():
            pltpu.make_async_copy(csend.at[k], crecv.at[slot], col_recv.at[slot]).start()

        @pl.when(target != me)
        def _():
            pltpu.make_async_remote_copy(
                src_ref=csend.at[k], dst_ref=crecv.at[slot], send_sem=col_send.at[k],
                recv_sem=col_recv.at[slot], device_id=(target // n_col, lax.rem(target, n_col)),
                device_id_type=MESH,
            ).start()

    rows = lax.broadcasted_iota(jnp.int32, (ROWS, 128), 0)
    own = by_row(rows, 0)
    sum_l, sum_m, sum_r = (hs[k] * own for k in range(3))
    racc[...] = jnp.zeros_like(racc)
    racc[pl.ds(8, ROWS), :] = (xs[...] + 32.0 * bias_two) * own
    for a in range(3):
        out_rows = rows - 4 * (a - 1)
        m0, ml, mr = (by_row(out_rows, v) for v in range(3))
        lhs = split(
            jnp.concatenate(
                [
                    m0 * (sum_l + sum_m) + mr * sum_r,
                    m0 * (sum_l + sum_m + sum_r),
                    m0 * (sum_m + sum_r) + ml * sum_l,
                ],
                axis=1,
            )
        )
        both = jnp.dot(lhs, wt2[pl.ds(a * 384, 384), :], preferred_element_type=F32)
        racc[pl.ds(8 - 4 * (a - 1), ROWS), :] += both[:ROWS] + both[ROWS:]
    racc[...] = racc[...] + pltpu.roll(racc[...], 64, 1)
    half = lax.broadcasted_iota(jnp.int32, (72, 128), 1) < 64
    paired = jnp.where(half, racc[pl.ds(0, 72, stride=2), :], racc[pl.ds(1, 72, stride=2), :])
    for k in range(18):
        rsend[k] = paired[4 * k : 4 * k + 4]

    @pl.loop(0, 18)
    def _(k):
        target = lax.rem(me - c - 1 + k + n_all, n_all)
        slot = jnp.where((k == 0) | (k == 17), n_col + c, c)

        @pl.when(target == me)
        def _():
            pltpu.make_async_copy(rsend.at[k], rrecv.at[slot], row_recv.at[slot]).start()

        @pl.when(target != me)
        def _():
            pltpu.make_async_remote_copy(
                src_ref=rsend.at[k], dst_ref=rrecv.at[slot], send_sem=row_send.at[k],
                recv_sem=row_recv.at[slot], device_id=(target // n_col, lax.rem(target, n_col)),
                device_id_type=MESH,
            ).start()

    def arrived(buffer, sem, first_slot, count):
        for k in range(first_slot, first_slot + count):
            pltpu.make_async_copy(buffer.at[k], buffer.at[k], sem.at[k]).wait()
        return jnp.sum(buffer[pl.ds(first_slot, count)], axis=0)

    total[...] = arrived(rrecv, row_recv, 0, n_col) + arrived(crecv, col_recv, 0, n_row)

    @pl.when((c == 0) | (c == n_col - 1))
    def _():
        total[...] += arrived(rrecv, row_recv, n_col, n_col)

    @pl.when((part == 0) | (part == 7))
    def _():
        total[...] += arrived(crecv, col_recv, n_row, n_row)

    sums = total[...]
    res[pl.ds(0, 4, stride=2), :] = sums
    res[pl.ds(1, 4, stride=2), :] = pltpu.roll(sums, 64, 1)
    pooled = res[:, :64]
    center = jnp.mean(pooled, axis=1, keepdims=True)
    spread = jnp.mean((pooled - center) ** 2, axis=1, keepdims=True)
    normed = ((pooled - center) / jnp.sqrt(spread + EPSILON) * gain[...]).astype(BF16)
    out[...] = jnp.dot(normed, wp[...], preferred_element_type=F32).astype(BF16)

    @pl.loop(0, 18)
    def _(k):
        @pl.when(lax.rem(me - c - 1 + k + n_all, n_all) != me)
        def _():
            pltpu.make_async_copy(rsend.at[k], rsend.at[k], row_send.at[k]).wait()

    @pl.loop(0, 10)
    def _(k):
        @pl.when(lax.rem(8 * c - 1 + k + n_all, n_all) != me)
        def _():
            pltpu.make_async_copy(csend.at[k], csend.at[k], col_send.at[k]).wait()


def body(pair, tile_mask, w_first, b_first, w_second, b_second, norm_gain, w_proj):
    n_row, n_col = lax.axis_size("row"), lax.axis_size("col")
    hbm = pl.BlockSpec(memory_space=pltpu.HBM)
    return pl.pallas_call(
        functools.partial(kernel, n_row, n_col),
        out_shape=jax.ShapeDtypeStruct((8, w_proj.shape[1]), BF16),
        in_specs=[hbm] * 8,
        out_specs=pl.BlockSpec(memory_space=pltpu.VMEM),
        scratch_shapes=[
            pltpu.SMEM(tile_mask.shape, jnp.int32),
            pltpu.VMEM(w_first.shape, BF16),
            pltpu.VMEM((1, 64), F32),
            pltpu.VMEM(w_second.shape, BF16),
            pltpu.VMEM((1, 64), F32),
            pltpu.VMEM((1, 64), F32),
            pltpu.VMEM(w_proj.shape, BF16),
            pltpu.VMEM((ROWS + 2 * EDGE, LANES + 256), BF16),
            pltpu.VMEM((ROWS, LANES + 256), BF16),
            pltpu.VMEM((ROWS, LANES + 256), BF16),
            pltpu.VMEM((ROWS, LANES), BF16),
            pltpu.VMEM((1536, 256), BF16),
            pltpu.VMEM((1152, 128), BF16),
            pltpu.VMEM((3, ROWS, 128), F32),
            pltpu.VMEM((ROWS, 128), F32),
            pltpu.VMEM((144, 128), F32),
            pltpu.VMEM((48, 128), F32),
            pltpu.VMEM((512, 128), F32),
            pltpu.VMEM((2, 16, 512), BF16),
            pltpu.VMEM((2, 16, 512), BF16),
            pltpu.VMEM((18, 4, 128), F32),
            pltpu.VMEM((10, 4, 128), F32),
            pltpu.VMEM((32, 4, 128), F32),
            pltpu.VMEM((16, 4, 128), F32),
            pltpu.VMEM((4, 128), F32),
            pltpu.VMEM((8, 128), F32),
            pltpu.SemaphoreType.REGULAR,
            pltpu.SemaphoreType.DMA((3,)),
            pltpu.SemaphoreType.DMA((7,)),
            pltpu.SemaphoreType.DMA((8,)),
            pltpu.SemaphoreType.DMA((8,)),
            pltpu.SemaphoreType.DMA((18,)),
            pltpu.SemaphoreType.DMA((32,)),
            pltpu.SemaphoreType.DMA((10,)),
            pltpu.SemaphoreType.DMA((16,)),
        ],
        compiler_params=pltpu.CompilerParams(
            collective_id=0, has_side_effects=True, vmem_limit_bytes=64 * 1024 * 1024 - 65536
        ),
        name="block",
    )(
        pair, tile_mask, w_first, b_first.reshape(1, -1), w_second, b_second.reshape(1, -1),
        norm_gain.reshape(1, -1), w_proj,
    )


def solution(mesh):
    return jax.shard_map(
        body,
        mesh=mesh,
        in_specs=(P("row", "col"), P(), P(), P(), P(), P(), P(), P()),
        out_specs=P(("row", "col"), None),
        check_vma=False,
    )
```

```python
import functools

import jax
import jax.numpy as jnp
from jax import lax
from jax.experimental import pallas as pl
from jax.experimental.pallas import tpu as pltpu
from jax.sharding import PartitionSpec as P

TILE = 64
EPSILON = 1e-05
MESH = pl.DeviceIdType.MESH
F32 = jnp.float32
BF16 = jnp.bfloat16

ROWS = 128
PAIRS = 32
EDGE = 16
GROUPS = 16
OWN = 128
LANES = PAIRS * 128


def elu(v):
    return jnp.where(v > 0, v, jnp.exp(jnp.minimum(v, 0.0)) - 1.0)


def kernel(
    n_row, n_col,
    pair, mask_in, w1_in, b1_in, w2_in, b2_in, gain_in, wp_in,
    out,
    mask, w1, b1, w2, b2, gain, wp, xe, xm, xp, hb, wt1, wt2, hs, xs, racc, cacc, csum, packed, landed, rsend, csend, rrecv, crecv, total, res,
    ready, load_sem, small_sem, halo_send, halo_recv, row_send, row_recv, col_send, col_recv,
):
    r = lax.axis_index("row")
    c = lax.axis_index("col")
    me = r * n_col + c
    n_all = n_row * n_col

    loads = [
        pltpu.make_async_copy(
            pair.at[pl.ds(start, size)], xe.at[pl.ds(EDGE + start, size), pl.ds(OWN, LANES)], load_sem.at[k]
        )
        for k, (start, size) in enumerate(((0, EDGE), (ROWS - EDGE, EDGE), (EDGE, ROWS - 2 * EDGE)))
    ]
    small = [(mask_in, mask), (w1_in, w1), (w2_in, w2), (b1_in, b1), (b2_in, b2), (gain_in, gain), (wp_in, wp)]
    small = [
        pltpu.make_async_copy(src, dst, small_sem.at[k]) for k, (src, dst) in enumerate(small)
    ]
    barrier = pltpu.get_barrier_semaphore()

    def greet(semaphore, tr, tc):
        pl.semaphore_signal(semaphore, inc=1, device_id=(tr, tc), device_id_type=MESH)

    up, down = lax.rem(r + n_row - 1, n_row), lax.rem(r + 1, n_row)
    left, right = lax.rem(c + n_col - 1, n_col), lax.rem(c + 1, n_col)
    above, below, whole = pl.ds(0, EDGE), pl.ds(EDGE + ROWS, EDGE), pl.ds(EDGE, ROWS)
    before, after = pl.ds(0, 128), pl.ds(OWN + LANES, 128)
    first, last = pl.ds(OWN, 128), pl.ds(OWN + LANES - 128, 128)
    top, bottom = pl.ds(EDGE, EDGE), pl.ds(ROWS, EDGE)
    halos = [
        (up, c, packed.at[0], landed.at[1]),
        (down, c, packed.at[1], landed.at[0]),
        (r, left, xe.at[whole, first], xe.at[whole, after]),
        (r, right, xe.at[whole, last], xe.at[whole, before]),
        (up, left, xe.at[top, first], xe.at[below, after]),
        (up, right, xe.at[top, last], xe.at[below, before]),
        (down, left, xe.at[bottom, first], xe.at[above, after]),
        (down, right, xe.at[bottom, last], xe.at[above, before]),
    ]
    for k in range(1, n_row):
        greet(barrier, lax.rem(r + k, n_row), c)
    for halo in halos[4:]:
        greet(barrier, halo[0], halo[1])
    for k in range(1, n_col):
        greet(barrier, r, lax.rem(c + k, n_col))
    for copy in loads + small:
        copy.start()
    part = lax.rem(me, 8)

    for k, row in ((0, 0), (1, EDGE - 2)):
        loads[k].wait()
        cells = jnp.concatenate(
            [xe[pl.ds(EDGE + (ROWS - EDGE) * k, EDGE), pl.ds(OWN + 512 * p, 512)] for p in range(8)], axis=0
        )
        i = lax.broadcasted_iota(jnp.int32, (16, 128), 0)
        j = lax.broadcasted_iota(jnp.int32, (16, 128), 1)
        select = jnp.where(j == (i // 2) * 16 + row + i % 2, 1.0, 0.0).astype(BF16)
        packed[k] = jnp.dot(select, cells, preferred_element_type=F32).astype(BF16)

    loads[2].wait()
    pl.semaphore_wait(barrier, (n_row - 1) + 4 + (n_col - 1))
    copies = []
    for k in (0, 1, 4, 5, 6, 7, 2, 3):
        tr, tc, src, dst = halos[k]
        copy = pltpu.make_async_remote_copy(
            src_ref=src, dst_ref=dst, send_sem=halo_send.at[k], recv_sem=halo_recv.at[k],
            device_id=(tr, tc), device_id_type=MESH,
        )
        copy.start()
        copies.append(copy)
    for k in range(1, n_col):
        greet(ready, r, lax.rem(c + k, n_col))

    for copy in small:
        copy.wait()

    zero = jnp.zeros((64, 64), BF16)
    wt1[...] = jnp.zeros_like(wt1)
    for a in range(3):
        for b in range(3):
            w = w1[a, b]
            doubled = jnp.concatenate(
                [jnp.concatenate([w, zero], axis=1), jnp.concatenate([zero, w], axis=1)], axis=0
            )
            for n in range(2):
                wt1[pl.ds(a * 512 + (b + n) * 128, 128), pl.ds(n * 128, 128)] = doubled
            w = w2[a, b]
            wt2[pl.ds((a * 3 + b) * 128, 128), :] = jnp.concatenate(
                [jnp.concatenate([w, zero], axis=1), jnp.concatenate([zero, w], axis=1)], axis=0
            )
    bias_one = jnp.concatenate([b1[...]] * 4, axis=1)
    bias_two = jnp.concatenate([b2[...]] * 2, axis=1)

    def tile(t, v):
        ti = 2 * r - 1 + t
        tj = c + v
        ok = (ti >= 0) & (ti < 2 * n_row) & (tj >= 0) & (tj < n_col)
        value = mask[jnp.clip(ti, 0, 2 * n_row - 1), jnp.clip(tj, 0, n_col - 1)]
        return jnp.where(ok, value, 0).astype(F32)

    mt = [[tile(t, v) for v in (0, -1, 1)] for t in range(4)]

    def by_row(rows, v):
        return jnp.where(
            rows < 0, mt[0][v], jnp.where(rows < 64, mt[1][v], jnp.where(rows < 128, mt[2][v], mt[3][v]))
        )

    def shift(r0, lanes):
        window = xe[pl.ds(r0, 48), lanes]
        xm[pl.ds(r0, 16), lanes] = window[14:30]
        xp[pl.ds(r0, 16), lanes] = window[18:34]

    def taps(r0, rows, g):
        lanes = pl.ds(g * 256, 512)
        return jnp.concatenate(
            [xm[pl.ds(r0, rows), lanes], xe[pl.ds(EDGE + r0, rows), lanes], xp[pl.ds(r0, rows), lanes]],
            axis=1,
        )

    def hidden(r0, rows, groups):
        lhs = jnp.concatenate([taps(r0, rows, g) for g in groups], axis=0)
        h = elu(jnp.dot(lhs, wt1[...], preferred_element_type=F32) + bias_one)
        parts = [h[k * rows : (k + 1) * rows] for k in range(len(groups))]
        for g, piece in zip(groups, parts):
            hb[pl.ds(r0, rows), pl.ds(g * 256, 256)] = piece.astype(BF16)
        return parts

    def fold(parts):
        both = functools.reduce(jnp.add, parts)
        return both[:, :128] + both[:, 128:]

    def sum_x(r0):
        cells = xe[pl.ds(EDGE + r0, 16), pl.ds(OWN, LANES)].astype(F32)
        xs[pl.ds(r0, 16), :] = functools.reduce(
            jnp.add, [cells[:, p * 128 : (p + 1) * 128] for p in range(PAIRS)]
        )

    @pl.loop(0, 6)
    def _(k):
        r0 = pl.multiple_of(16 + 16 * k, 16)
        shift(r0, pl.ds(OWN, LANES))
        hs[1, pl.ds(r0, 16), :] = fold(hidden(r0, 16, range(1, GROUPS - 1)))
        sum_x(r0)

    at = lax.broadcasted_iota(jnp.int32, (16, 128), 1)
    own_at = by_row(at, 0)
    for g in range(GROUPS):
        sums = jnp.dot(
            own_at.astype(BF16), xe[pl.ds(EDGE, ROWS), pl.ds(OWN + g * 256, 256)], preferred_element_type=F32
        )
        csum[pl.ds(g * 32, 16), :] = sums[:, :128]
        csum[pl.ds(g * 32 + 16, 16), :] = sums[:, 128:]
    cacc[...] = jnp.zeros_like(cacc)
    cacc[pl.ds(8, PAIRS), :] = csum[pl.ds(0, PAIRS, stride=16), :] + bias_two * (
        64.0 * (mt[1][0] + mt[2][0])
    )
    sum_x(0)
    sum_x(ROWS - 16)

    for copy in copies:
        copy.wait()

    i = lax.broadcasted_iota(jnp.int32, (128, 16), 0)
    j = lax.broadcasted_iota(jnp.int32, (128, 16), 1)
    for k, (row, place) in enumerate(((EDGE - 2, above), (0, below))):
        at_row = i % 16 - row
        select = jnp.where((at_row >= 0) & (at_row < 2) & (j == (i // 16) * 2 + at_row), 1.0, 0.0)
        cells = jnp.dot(select.astype(BF16), landed[k], preferred_element_type=F32).astype(BF16)
        for p in range(8):
            xe[place, pl.ds(OWN + 512 * p, 512)] = cells[16 * p : 16 * p + 16]

    @pl.when(r == 0)
    def _():
        xe[above, :] = jnp.zeros((EDGE, xe.shape[1]), BF16)

    @pl.when(r == n_row - 1)
    def _():
        xe[below, :] = jnp.zeros((EDGE, xe.shape[1]), BF16)

    @pl.when(c == 0)
    def _():
        xe[:, before] = jnp.zeros((xe.shape[0], 128), BF16)

    @pl.when(c == n_col - 1)
    def _():
        xe[:, after] = jnp.zeros((xe.shape[0], 128), BF16)

    for r0 in range(16, ROWS - 16, 16):
        shift(r0, before)
        shift(r0, after)

    @pl.loop(0, 2)
    def _(k):
        r0 = pl.multiple_of((ROWS - 16) * k, 16)
        shift(r0, pl.ds(0, xe.shape[1]))
        parts = hidden(r0, 16, range(GROUPS))
        hs[0, pl.ds(r0, 16), :] = fold(parts[:1])
        hs[1, pl.ds(r0, 16), :] = fold(parts[1:-1])
        hs[2, pl.ds(r0, 16), :] = fold(parts[-1:])

    parts = hidden(16, ROWS - 32, (0, GROUPS - 1))
    hs[0, pl.ds(16, ROWS - 32), :] = fold(parts[:1])
    hs[2, pl.ds(16, ROWS - 32), :] = fold(parts[1:])

    def split(values):
        high = values.astype(BF16)
        return jnp.concatenate([high, (values - high.astype(F32)).astype(BF16)], axis=0)

    combos = [(a, v) for a in range(3) for v in range(3)]
    which = lax.broadcasted_iota(jnp.int32, (16, 128), 0)
    pick = jnp.zeros((16, 128), F32)
    for k, (a, v) in enumerate(combos):
        pick = jnp.where(which == k, by_row(at - 4 * (a - 1), v), pick)
    pick = (pick * own_at).astype(BF16)
    for g in range(GROUPS):
        sums = jnp.dot(pick, hb[:, pl.ds(g * 256, 256)], preferred_element_type=F32)
        csum[pl.ds(g * 32, 16), :] = sums[:, :128]
        csum[pl.ds(g * 32 + 16, 16), :] = sums[:, 128:]

    def column(k):
        return csum[pl.ds(k, PAIRS, stride=16), :]

    at_pair = lax.broadcasted_iota(jnp.int32, (PAIRS, 128), 0)
    for b in range(3):
        pieces = []
        for a in range(3):
            value = column(3 * a)
            if b == 0:
                value = jnp.where(at_pair >= PAIRS - 2, column(3 * a + 2), value)
            if b == 2:
                value = jnp.where(at_pair < 2, column(3 * a + 1), value)
            pieces.append(value)
        weights = jnp.concatenate([wt2[pl.ds((a * 3 + b) * 128, 128), :] for a in range(3)], axis=0)
        both = jnp.dot(split(jnp.concatenate(pieces, axis=1)), weights, preferred_element_type=F32)
        cacc[pl.ds(8 - 2 * (b - 1), PAIRS), :] += both[:PAIRS] + both[PAIRS:]
    columns = cacc[pl.ds(4, 40), :]
    for k in range(10):
        csend[k] = columns[4 * k : 4 * k + 4]

    pl.semaphore_wait(ready, n_col - 1)

    @pl.loop(0, 10)
    def _(k):
        target = lax.rem(8 * c - 1 + k + n_all, n_all)
        slot = jnp.where((k == 0) | (k == 9), n_row + r, r)

        @pl.when(target == me)
        def _():
            pltpu.make_async_copy(csend.at[k], crecv.at[slot], col_recv.at[slot]).start()

        @pl.when(target != me)
        def _():
            pltpu.make_async_remote_copy(
                src_ref=csend.at[k], dst_ref=crecv.at[slot], send_sem=col_send.at[k],
                recv_sem=col_recv.at[slot], device_id=(target // n_col, lax.rem(target, n_col)),
                device_id_type=MESH,
            ).start()

    rows = lax.broadcasted_iota(jnp.int32, (ROWS, 128), 0)
    own = by_row(rows, 0)
    sum_l, sum_m, sum_r = (hs[k] * own for k in range(3))
    racc[...] = jnp.zeros_like(racc)
    racc[pl.ds(8, ROWS), :] = (xs[...] + 32.0 * bias_two) * own
    for a in range(3):
        out_rows = rows - 4 * (a - 1)
        m0, ml, mr = (by_row(out_rows, v) for v in range(3))
        lhs = split(
            jnp.concatenate(
                [
                    m0 * (sum_l + sum_m) + mr * sum_r,
                    m0 * (sum_l + sum_m + sum_r),
                    m0 * (sum_m + sum_r) + ml * sum_l,
                ],
                axis=1,
            )
        )
        both = jnp.dot(lhs, wt2[pl.ds(a * 384, 384), :], preferred_element_type=F32)
        racc[pl.ds(8 - 4 * (a - 1), ROWS), :] += both[:ROWS] + both[ROWS:]
    racc[...] = racc[...] + pltpu.roll(racc[...], 64, 1)
    half = lax.broadcasted_iota(jnp.int32, (72, 128), 1) < 64
    paired = jnp.where(half, racc[pl.ds(0, 72, stride=2), :], racc[pl.ds(1, 72, stride=2), :])
    for k in range(18):
        rsend[k] = paired[4 * k : 4 * k + 4]

    @pl.loop(0, 18)
    def _(k):
        target = lax.rem(me - c - 1 + k + n_all, n_all)
        slot = jnp.where((k == 0) | (k == 17), n_col + c, c)

        @pl.when(target == me)
        def _():
            pltpu.make_async_copy(rsend.at[k], rrecv.at[slot], row_recv.at[slot]).start()

        @pl.when(target != me)
        def _():
            pltpu.make_async_remote_copy(
                src_ref=rsend.at[k], dst_ref=rrecv.at[slot], send_sem=row_send.at[k],
                recv_sem=row_recv.at[slot], device_id=(target // n_col, lax.rem(target, n_col)),
                device_id_type=MESH,
            ).start()

    def arrived(buffer, sem, first_slot, count):
        for k in range(first_slot, first_slot + count):
            pltpu.make_async_copy(buffer.at[k], buffer.at[k], sem.at[k]).wait()
        return jnp.sum(buffer[pl.ds(first_slot, count)], axis=0)

    total[...] = arrived(rrecv, row_recv, 0, n_col) + arrived(crecv, col_recv, 0, n_row)

    @pl.when((c == 0) | (c == n_col - 1))
    def _():
        total[...] += arrived(rrecv, row_recv, n_col, n_col)

    @pl.when((part == 0) | (part == 7))
    def _():
        total[...] += arrived(crecv, col_recv, n_row, n_row)

    sums = total[...]
    res[pl.ds(0, 4, stride=2), :] = sums
    res[pl.ds(1, 4, stride=2), :] = pltpu.roll(sums, 64, 1)
    pooled = res[:, :64]
    center = jnp.mean(pooled, axis=1, keepdims=True)
    spread = jnp.mean((pooled - center) ** 2, axis=1, keepdims=True)
    normed = ((pooled - center) / jnp.sqrt(spread + EPSILON) * gain[...]).astype(BF16)
    out[...] = jnp.dot(normed, wp[...], preferred_element_type=F32).astype(BF16)

    @pl.loop(0, 18)
    def _(k):
        @pl.when(lax.rem(me - c - 1 + k + n_all, n_all) != me)
        def _():
            pltpu.make_async_copy(rsend.at[k], rsend.at[k], row_send.at[k]).wait()

    @pl.loop(0, 10)
    def _(k):
        @pl.when(lax.rem(8 * c - 1 + k + n_all, n_all) != me)
        def _():
            pltpu.make_async_copy(csend.at[k], csend.at[k], col_send.at[k]).wait()


def body(pair, tile_mask, w_first, b_first, w_second, b_second, norm_gain, w_proj):
    n_row, n_col = lax.axis_size("row"), lax.axis_size("col")
    hbm = pl.BlockSpec(memory_space=pltpu.HBM)
    return pl.pallas_call(
        functools.partial(kernel, n_row, n_col),
        out_shape=pltpu.VMEM((8, w_proj.shape[1]), BF16),
        in_specs=[hbm] * 8,
        out_specs=pl.BlockSpec(memory_space=pltpu.VMEM),
        scratch_shapes=[
            pltpu.SMEM(tile_mask.shape, jnp.int32),
            pltpu.VMEM(w_first.shape, BF16),
            pltpu.VMEM((1, 64), F32),
            pltpu.VMEM(w_second.shape, BF16),
            pltpu.VMEM((1, 64), F32),
            pltpu.VMEM((1, 64), F32),
            pltpu.VMEM(w_proj.shape, BF16),
            pltpu.VMEM((ROWS + 2 * EDGE, LANES + 256), BF16),
            pltpu.VMEM((ROWS, LANES + 256), BF16),
            pltpu.VMEM((ROWS, LANES + 256), BF16),
            pltpu.VMEM((ROWS, LANES), BF16),
            pltpu.VMEM((1536, 256), BF16),
            pltpu.VMEM((1152, 128), BF16),
            pltpu.VMEM((3, ROWS, 128), F32),
            pltpu.VMEM((ROWS, 128), F32),
            pltpu.VMEM((144, 128), F32),
            pltpu.VMEM((48, 128), F32),
            pltpu.VMEM((512, 128), F32),
            pltpu.VMEM((2, 16, 512), BF16),
            pltpu.VMEM((2, 16, 512), BF16),
            pltpu.VMEM((18, 4, 128), F32),
            pltpu.VMEM((10, 4, 128), F32),
            pltpu.VMEM((32, 4, 128), F32),
            pltpu.VMEM((16, 4, 128), F32),
            pltpu.VMEM((4, 128), F32),
            pltpu.VMEM((8, 128), F32),
            pltpu.SemaphoreType.REGULAR,
            pltpu.SemaphoreType.DMA((3,)),
            pltpu.SemaphoreType.DMA((7,)),
            pltpu.SemaphoreType.DMA((8,)),
            pltpu.SemaphoreType.DMA((8,)),
            pltpu.SemaphoreType.DMA((18,)),
            pltpu.SemaphoreType.DMA((32,)),
            pltpu.SemaphoreType.DMA((10,)),
            pltpu.SemaphoreType.DMA((16,)),
        ],
        compiler_params=pltpu.CompilerParams(
            collective_id=0, has_side_effects=True, vmem_limit_bytes=48 * 1024 * 1024
        ),
        name="block",
    )(
        *(pltpu.with_memory_space_constraint(v, pltpu.HBM) for v in (
        pair, tile_mask, w_first, b_first.reshape(1, -1), w_second, b_second.reshape(1, -1),
        norm_gain.reshape(1, -1), w_proj,
    )))


def solution(mesh):
    return jax.shard_map(
        body,
        mesh=mesh,
        in_specs=(P("row", "col"), P(), P(), P(), P(), P(), P(), P()),
        out_specs=P(("row", "col"), None),
        check_vma=False,
    )
```

```python
import functools

import jax
import jax.numpy as jnp
from jax import lax
from jax.experimental import pallas as pl
from jax.experimental.pallas import tpu as pltpu
from jax.sharding import PartitionSpec as P

TILE = 64
EPSILON = 1e-05
MESH = pl.DeviceIdType.MESH
F32 = jnp.float32
BF16 = jnp.bfloat16

ROWS = 128
PAIRS = 32
EDGE = 16
GROUPS = 16
OWN = 128
LANES = PAIRS * 128


def elu(v):
    return jnp.where(v > 0, v, jnp.exp(jnp.minimum(v, 0.0)) - 1.0)


def kernel(
    n_row, n_col,
    pair, mask_in, w1_in, b1_in, w2_in, b2_in, gain_in, wp_in,
    out,
    mask, w1, b1, w2, b2, gain, wp, xe, xm, xp, hb, wt1, wt2, hs, xs, racc, cacc, csum, compact, landed, side, side_pre, edge_pre, gather, rsend, csend, rrecv, crecv, res,
    ready, load_sem, small_sem, halo_send, halo_recv, row_send, row_recv, col_send, col_recv,
):
    r = lax.axis_index("row")
    c = lax.axis_index("col")
    me = r * n_col + c
    n_all = n_row * n_col

    loads = [
        pltpu.make_async_copy(
            pair.at[pl.ds(start, size)], xe.at[pl.ds(EDGE + start, size), pl.ds(OWN, LANES)], load_sem.at[k]
        )
        for k, (start, size) in enumerate(((0, EDGE), (ROWS - EDGE, EDGE), (EDGE, ROWS - 2 * EDGE)))
    ]
    small = [(mask_in, mask), (w1_in, w1), (w2_in, w2), (b1_in, b1), (b2_in, b2), (gain_in, gain), (wp_in, wp)]
    small = [
        pltpu.make_async_copy(src, dst, small_sem.at[k]) for k, (src, dst) in enumerate(small)
    ]
    barrier = pltpu.get_barrier_semaphore()

    def greet(semaphore, tr, tc):
        pl.semaphore_signal(semaphore, inc=1, device_id=(tr, tc), device_id_type=MESH)

    up, down = lax.rem(r + n_row - 1, n_row), lax.rem(r + 1, n_row)
    left, right = lax.rem(c + n_col - 1, n_col), lax.rem(c + 1, n_col)
    above, below, whole = pl.ds(0, EDGE), pl.ds(EDGE + ROWS, EDGE), pl.ds(EDGE, ROWS)
    before, after = pl.ds(0, 128), pl.ds(OWN + LANES, 128)
    first, last = pl.ds(OWN, 128), pl.ds(OWN + LANES - 128, 128)
    top, bottom = pl.ds(EDGE, EDGE), pl.ds(ROWS, EDGE)
    inner, low, high = pl.ds(EDGE, ROWS), pl.ds(0, EDGE), pl.ds(EDGE + ROWS, EDGE)
    halos = [
        (up, c, compact.at[0, pl.ds(16, 32)], landed.at[1, pl.ds(16, 32)]),
        (down, c, compact.at[3, pl.ds(16, 32)], landed.at[0, pl.ds(16, 32)]),
        (r, left, xe.at[whole, first], side.at[1, inner]),
        (r, right, xe.at[whole, last], side.at[0, inner]),
        (up, left, xe.at[top, first], side.at[1, high]),
        (up, right, xe.at[top, last], side.at[0, high]),
        (down, left, xe.at[bottom, first], side.at[1, low]),
        (down, right, xe.at[bottom, last], side.at[0, low]),
    ]
    for k in range(1, n_row):
        greet(barrier, lax.rem(r + k, n_row), c)
    for halo in halos[4:]:
        greet(barrier, halo[0], halo[1])
    for k in range(1, n_col):
        greet(barrier, r, lax.rem(c + k, n_col))
    for copy in loads + small:
        copy.start()
    part = lax.rem(me, 8)

    xe[above, :] = jnp.zeros((EDGE, xe.shape[1]), BF16)
    xe[below, :] = jnp.zeros((EDGE, xe.shape[1]), BF16)
    xe[whole, before] = jnp.zeros((ROWS, 128), BF16)
    xe[whole, after] = jnp.zeros((ROWS, 128), BF16)
    for k in range(2):
        landed[k, pl.ds(0, 16), :] = jnp.zeros((16, 256), BF16)
        landed[k, pl.ds(48, 16), :] = jnp.zeros((16, 256), BF16)
    for k in range(4):
        compact[k, pl.ds(0, 16), :] = jnp.zeros((16, 256), BF16)
        compact[k, pl.ds(48, 16), :] = jnp.zeros((16, 256), BF16)

    row_edge = (c == 0) | (c == n_col - 1)
    col_edge = (part == 0) | (part == 7)

    @pl.when(jnp.logical_not(row_edge))
    def _():
        rrecv[pl.ds(n_col, n_col)] = jnp.zeros((n_col, 4, 128), F32)

    @pl.when(jnp.logical_not(col_edge))
    def _():
        crecv[pl.ds(n_row, n_row)] = jnp.zeros((n_row, 4, 128), F32)

    i = lax.broadcasted_iota(jnp.int32, (64, 256), 0)
    j = lax.broadcasted_iota(jnp.int32, (64, 256), 1)
    for k in range(2):
        loads[k].wait()
        cells = jnp.concatenate(
            [xe[pl.ds(EDGE + (ROWS - EDGE) * k, EDGE), pl.ds(OWN + 256 * g, 256)] for g in range(GROUPS)], axis=0
        )
        row = (EDGE - 4) * k + (i // 32) * 2 + i % 2
        select = jnp.where(j == (i % 32 // 2) * 16 + row, 1.0, 0.0).astype(BF16)
        both = jnp.dot(select, cells, preferred_element_type=F32).astype(BF16)
        compact[2 * k, pl.ds(16, 32), :] = both[:32]
        compact[2 * k + 1, pl.ds(16, 32), :] = both[32:]

    loads[2].wait()
    pl.semaphore_wait(barrier, (n_row - 1) + 4 + (n_col - 1))
    copies = []
    for k in (0, 1, 4, 5, 6, 7, 2, 3):
        tr, tc, src, dst = halos[k]
        copy = pltpu.make_async_remote_copy(
            src_ref=src, dst_ref=dst, send_sem=halo_send.at[k], recv_sem=halo_recv.at[k],
            device_id=(tr, tc), device_id_type=MESH,
        )
        copy.start()
        copies.append(copy)
    for k in range(1, n_col):
        greet(ready, r, lax.rem(c + k, n_col))

    for copy in small:
        copy.wait()

    zero = jnp.zeros((64, 64), BF16)
    wt1[...] = jnp.zeros_like(wt1)
    for a in range(3):
        for b in range(3):
            w = w1[a, b]
            doubled = jnp.concatenate(
                [jnp.concatenate([w, zero], axis=1), jnp.concatenate([zero, w], axis=1)], axis=0
            )
            for n in range(2):
                wt1[pl.ds(a * 512 + (b + n) * 128, 128), pl.ds(n * 128, 128)] = doubled
            w = w2[a, b]
            wt2[pl.ds((a * 3 + b) * 128, 128), :] = jnp.concatenate(
                [jnp.concatenate([w, zero], axis=1), jnp.concatenate([zero, w], axis=1)], axis=0
            )
    bias_one = jnp.concatenate([b1[...]] * 4, axis=1)
    bias_two = jnp.concatenate([b2[...]] * 2, axis=1)

    def tile(t, v):
        ti = 2 * r - 1 + t
        tj = c + v
        ok = (ti >= 0) & (ti < 2 * n_row) & (tj >= 0) & (tj < n_col)
        value = mask[jnp.clip(ti, 0, 2 * n_row - 1), jnp.clip(tj, 0, n_col - 1)]
        return jnp.where(ok, value, 0).astype(F32)

    mt = [[tile(t, v) for v in (0, -1, 1)] for t in range(4)]

    def by_row(rows, v):
        return jnp.where(
            rows < 0, mt[0][v], jnp.where(rows < 64, mt[1][v], jnp.where(rows < 128, mt[2][v], mt[3][v]))
        )

    def expand(buffer, k):
        window = buffer[k]
        return jnp.concatenate([window[14:46, 128:], window[16:48], window[18:50, :128]], axis=1)

    def fold(parts):
        both = functools.reduce(jnp.add, parts)
        return both[:, :128] + both[:, 128:]

    def split(values):
        high_part = values.astype(BF16)
        return jnp.concatenate([high_part, (values - high_part.astype(F32)).astype(BF16)], axis=0)

    @pl.loop(0, ROWS // 16)
    def _(k):
        r0 = pl.multiple_of(16 * k, 16)
        window = xe[pl.ds(r0, 48), :]
        xm[...] = window[14:30]
        xp[...] = window[18:34]
        lhs = []
        for g in range(GROUPS):
            lanes = pl.ds(g * 256, 512)
            lhs.append(jnp.concatenate([xm[:, lanes], xe[pl.ds(EDGE + r0, 16), lanes], xp[:, lanes]], axis=1))
        pre = jnp.dot(jnp.concatenate(lhs, axis=0), wt1[...], preferred_element_type=F32) + bias_one
        side_pre[0, pl.ds(r0, 16), :] = pre[:16, :128]
        side_pre[1, pl.ds(r0, 16), :] = pre[-16:, 128:]
        h = elu(pre)
        parts = [h[16 * g : 16 * g + 16] for g in range(GROUPS)]
        for g, piece in enumerate(parts):
            hb[pl.ds(r0, 16), pl.ds(g * 256, 256)] = piece.astype(BF16)
        at_row = r0 + lax.broadcasted_iota(jnp.int32, (16, 128), 0)
        final = (at_row >= 2) & (at_row < ROWS - 2)
        for n, value in enumerate((parts[0][:, 128:], fold(parts[1:-1]), parts[-1][:, :128])):
            hs[n, pl.ds(r0, 16), :] = jnp.where(final, value, 0.0)
        cells = xe[pl.ds(EDGE + r0, 16), pl.ds(OWN, LANES)].astype(F32)
        xs[pl.ds(r0, 16), :] = functools.reduce(
            jnp.add, [cells[:, p * 128 : (p + 1) * 128] for p in range(PAIRS)]
        )

    for k in range(2):
        lhs = jnp.concatenate([expand(compact, 2 * k), expand(compact, 2 * k + 1)], axis=1)
        edge_pre[k] = (
            jnp.dot(lhs, wt1[pl.ds(512 * (1 - k), 1024), :], preferred_element_type=F32) + bias_one
        )

    combos = [(a, v) for a in range(3) for v in range(3)]
    at = lax.broadcasted_iota(jnp.int32, (16, 128), 1)
    which = lax.broadcasted_iota(jnp.int32, (16, 128), 0)
    own_at = by_row(at, 0)
    pick = jnp.zeros((16, 128), F32)
    for k, (a, v) in enumerate(combos):
        pick = jnp.where(which == k, by_row(at - 4 * (a - 1), v), pick)
    pick = pick * own_at
    inside = jnp.where((at >= 2) & (at < ROWS - 2), pick, 0.0)
    weights = jnp.concatenate([inside, jnp.where(which == 9, own_at, 0.0)], axis=1).astype(BF16)
    pick = pick.astype(BF16)
    for g in range(GROUPS):
        cells = jnp.concatenate(
            [hb[:, pl.ds(g * 256, 256)], xe[pl.ds(EDGE, ROWS), pl.ds(OWN + g * 256, 256)]], axis=0
        )
        sums = jnp.dot(weights, cells, preferred_element_type=F32)
        csum[pl.ds(g * 32, 16), :] = sums[:, :128]
        csum[pl.ds(g * 32 + 16, 16), :] = sums[:, 128:]
    cacc[...] = jnp.zeros_like(cacc)
    cacc[pl.ds(8, PAIRS), :] = csum[pl.ds(9, PAIRS, stride=16), :] + bias_two * (
        64.0 * (mt[1][0] + mt[2][0])
    )

    i = lax.broadcasted_iota(jnp.int32, (112, 128), 0)
    j = lax.broadcasted_iota(jnp.int32, (112, 128), 1)
    lower = j // 64
    pair_at = j % 32 // 2 * 2 + j // 32 % 2
    by_column = (lower == i // 32) & (pair_at == i % 32) & (pair_at > 0) & (pair_at < PAIRS - 1)
    kind = (i - 64) // 16
    in_kind = ((kind == 0) & (pair_at >= 2) & (pair_at < PAIRS - 2)) | (
        (kind > 0) & (pair_at == jnp.where(kind == 1, 1, PAIRS - 2))
    )
    by_line = in_kind & (lower == (i // 8) % 2) & (j % 2 + 6 * lower == i % 8)
    gather[...] = jnp.where(((i < 64) & by_column) | ((i >= 64) & by_line), 1.0, 0.0).astype(BF16)

    for copy in copies:
        copy.wait()

    @pl.when(r == 0)
    def _():
        side[:, low] = jnp.zeros((2, EDGE, 128), BF16)

    @pl.when(r == n_row - 1)
    def _():
        side[:, high] = jnp.zeros((2, EDGE, 128), BF16)

    edges = []
    for k, present in ((0, r > 0), (1, r < n_row - 1)):
        term = jnp.dot(expand(landed, k), wt1[pl.ds(1024 * k, 512), :], preferred_element_type=F32)
        edges.append(jnp.where(present, term, 0.0))
    line = lax.broadcasted_iota(jnp.int32, (8, 128), 0)
    flat = []
    for k, present in ((0, c > 0), (1, c < n_col - 1)):
        window = side[k]
        lhs = jnp.concatenate([window[14:142], window[16:144], window[18:146]], axis=1)
        taps = jnp.concatenate([wt1[pl.ds(a * 512 + 256 * k, 128), pl.ds(0, 128)] for a in range(3)], axis=0)
        term = jnp.dot(lhs, taps, preferred_element_type=F32)
        value = side_pre[k] + jnp.where(present, term, 0.0)
        if k == 0:
            head, tail = edges[0][:8, :128], pltpu.roll(edges[1][:8, :128], 6, 0)
        else:
            head, tail = pltpu.roll(edges[0][24:, 128:], 2, 0), edges[1][24:, 128:]
        value = jnp.concatenate(
            [
                value[:8] + jnp.where(line < 2, head, 0.0),
                value[8:120],
                value[120:] + jnp.where(line >= 6, tail, 0.0),
            ],
            axis=0,
        )
        flat.append(elu(value))
    sums = jnp.dot(
        pick, jnp.concatenate([v.astype(BF16) for v in flat], axis=1), preferred_element_type=F32
    )
    csum[pl.ds(0, 16), :] = sums[:, :128]
    csum[pl.ds(16 * (PAIRS - 1), 16), :] = sums[:, 128:]
    edges = [elu(edge_pre[k] + edges[k]).astype(BF16) for k in range(2)]
    cells = jnp.concatenate([edges[0][:, :128], edges[0][:, 128:], edges[1][:, :128], edges[1][:, 128:]], axis=0)
    found = jnp.dot(gather[...], cells, preferred_element_type=F32)

    def column(a, v):
        upper = mt[1][0] * (mt[0][v] if a == 2 else mt[1][v])
        under = mt[2][0] * (mt[3][v] if a == 0 else mt[2][v])
        return csum[pl.ds(3 * a + v, PAIRS, stride=16), :] + upper * found[:32] + under * found[32:64]

    at_pair = lax.broadcasted_iota(jnp.int32, (PAIRS, 128), 0)
    for b in range(3):
        pieces = []
        for a in range(3):
            value = column(a, 0)
            if b == 0:
                value = jnp.where(at_pair >= PAIRS - 2, column(a, 2), value)
            if b == 2:
                value = jnp.where(at_pair < 2, column(a, 1), value)
            pieces.append(value)
        weights = jnp.concatenate([wt2[pl.ds((a * 3 + b) * 128, 128), :] for a in range(3)], axis=0)
        both = jnp.dot(split(jnp.concatenate(pieces, axis=1)), weights, preferred_element_type=F32)
        cacc[pl.ds(8 - 2 * (b - 1), PAIRS), :] += both[:PAIRS] + both[PAIRS:]
    columns = cacc[pl.ds(4, 40), :]
    for k in range(10):
        csend[k] = columns[4 * k : 4 * k + 4]

    def post(src, dst, send_sem, recv_sem, tr, tc):
        mine = (tr == r) & (tc == c)

        @pl.when(mine)
        def _():
            pltpu.make_async_copy(src, dst, recv_sem).start()

        @pl.when(jnp.logical_not(mine))
        def _():
            pltpu.make_async_remote_copy(
                src_ref=src, dst_ref=dst, send_sem=send_sem, recv_sem=recv_sem, device_id=(tr, tc),
                device_id_type=MESH,
            ).start()

    def col_target(k):
        target = lax.rem(8 * c - 1 + k + n_all, n_all)
        return target // n_col, lax.rem(target, n_col)

    pl.semaphore_wait(ready, n_col - 1)
    for k in range(10):
        slot = r + n_row if k in (0, 9) else r
        post(csend.at[k], crecv.at[slot], col_send.at[k], col_recv.at[slot], *col_target(k))

    for k in range(2):
        hs[2 * k] += flat[k]
    for k, n in enumerate((1, 0, 2)):
        hs[n, pl.ds(0, 8), :] += found[64 + 16 * k : 72 + 16 * k]
        hs[n, pl.ds(ROWS - 8, 8), :] += found[72 + 16 * k : 80 + 16 * k]
    rows = lax.broadcasted_iota(jnp.int32, (ROWS, 128), 0)
    own = by_row(rows, 0)
    sum_l, sum_m, sum_r = (hs[k] * own for k in range(3))
    racc[...] = jnp.zeros_like(racc)
    racc[pl.ds(8, ROWS), :] = (xs[...] + 32.0 * bias_two) * own
    for a in range(3):
        out_rows = rows - 4 * (a - 1)
        m0, ml, mr = (by_row(out_rows, v) for v in range(3))
        lhs = split(
            jnp.concatenate(
                [
                    m0 * (sum_l + sum_m) + mr * sum_r,
                    m0 * (sum_l + sum_m + sum_r),
                    m0 * (sum_m + sum_r) + ml * sum_l,
                ],
                axis=1,
            )
        )
        both = jnp.dot(lhs, wt2[pl.ds(a * 384, 384), :], preferred_element_type=F32)
        racc[pl.ds(8 - 4 * (a - 1), ROWS), :] += both[:ROWS] + both[ROWS:]
    racc[...] = racc[...] + pltpu.roll(racc[...], 64, 1)
    half = lax.broadcasted_iota(jnp.int32, (72, 128), 1) < 64
    paired = jnp.where(half, racc[pl.ds(0, 72, stride=2), :], racc[pl.ds(1, 72, stride=2), :])
    for k in range(18):
        rsend[k] = paired[4 * k : 4 * k + 4]


    rrecv[c] = rsend[c + 1]
    for k in range(1, n_col):
        tc = lax.rem(c + k, n_col)
        pltpu.make_async_remote_copy(
            src_ref=rsend.at[tc + 1], dst_ref=rrecv.at[c], send_sem=row_send.at[k], recv_sem=row_recv.at[c],
            device_id=(r, tc), device_id_type=MESH,
        ).start()
    for k, tr, tc in ((0, up, n_col - 1), (17, down, 0)):
        pltpu.make_async_remote_copy(
            src_ref=rsend.at[k], dst_ref=rrecv.at[n_col + c], send_sem=row_send.at[k],
            recv_sem=row_recv.at[n_col + c], device_id=(tr, tc), device_id_type=MESH,
        ).start()

    def arrived(buffer, sem, slot):
        pltpu.make_async_copy(buffer.at[slot], buffer.at[slot], sem.at[slot]).wait()

    for k in range(1, n_col):
        arrived(rrecv, row_recv, lax.rem(c + k, n_col))

    @pl.when(row_edge)
    def _():
        for k in range(n_col):
            arrived(rrecv, row_recv, n_col + k)

    for k in range(n_row):
        arrived(crecv, col_recv, k)

    @pl.when(col_edge)
    def _():
        for k in range(n_row):
            arrived(crecv, col_recv, n_row + k)

    sums = jnp.sum(rrecv[...], axis=0) + jnp.sum(crecv[...], axis=0)
    res[pl.ds(0, 4, stride=2), :] = sums
    res[pl.ds(1, 4, stride=2), :] = pltpu.roll(sums, 64, 1)
    pooled = res[:, :64]
    center = jnp.mean(pooled, axis=1, keepdims=True)
    spread = jnp.mean((pooled - center) ** 2, axis=1, keepdims=True)
    normed = ((pooled - center) / jnp.sqrt(spread + EPSILON) * gain[...]).astype(BF16)
    out[...] = jnp.dot(normed, wp[...], preferred_element_type=F32).astype(BF16)

    for k in range(18):
        if k != n_col:
            pltpu.make_async_copy(rsend.at[k], rsend.at[k], row_send.at[k]).wait()
    for k in range(10):
        tr, tc = col_target(k)

        @pl.when((tr != r) | (tc != c))
        def _():
            pltpu.make_async_copy(csend.at[k], csend.at[k], col_send.at[k]).wait()


def body(pair, tile_mask, w_first, b_first, w_second, b_second, norm_gain, w_proj):
    n_row, n_col = lax.axis_size("row"), lax.axis_size("col")
    hbm = pl.BlockSpec(memory_space=pltpu.HBM)
    return pl.pallas_call(
        functools.partial(kernel, n_row, n_col),
        out_shape=pltpu.VMEM((8, w_proj.shape[1]), BF16),
        in_specs=[hbm] * 8,
        out_specs=pl.BlockSpec(memory_space=pltpu.VMEM),
        scratch_shapes=[
            pltpu.SMEM(tile_mask.shape, jnp.int32),
            pltpu.VMEM(w_first.shape, BF16),
            pltpu.VMEM((1, 64), F32),
            pltpu.VMEM(w_second.shape, BF16),
            pltpu.VMEM((1, 64), F32),
            pltpu.VMEM((1, 64), F32),
            pltpu.VMEM(w_proj.shape, BF16),
            pltpu.VMEM((ROWS + 2 * EDGE, LANES + 256), BF16),
            pltpu.VMEM((16, LANES + 256), BF16),
            pltpu.VMEM((16, LANES + 256), BF16),
            pltpu.VMEM((ROWS, LANES), BF16),
            pltpu.VMEM((1536, 256), BF16),
            pltpu.VMEM((1152, 128), BF16),
            pltpu.VMEM((3, ROWS, 128), F32),
            pltpu.VMEM((ROWS, 128), F32),
            pltpu.VMEM((144, 128), F32),
            pltpu.VMEM((48, 128), F32),
            pltpu.VMEM((512, 128), F32),
            pltpu.VMEM((4, 64, 256), BF16),
            pltpu.VMEM((2, 64, 256), BF16),
            pltpu.VMEM((2, ROWS + 2 * EDGE, 128), BF16),
            pltpu.VMEM((2, ROWS, 128), F32),
            pltpu.VMEM((2, 32, 256), F32),
            pltpu.VMEM((112, 128), BF16),
            pltpu.VMEM((18, 4, 128), F32),
            pltpu.VMEM((10, 4, 128), F32),
            pltpu.VMEM((32, 4, 128), F32),
            pltpu.VMEM((16, 4, 128), F32),
            pltpu.VMEM((8, 128), F32),
            pltpu.SemaphoreType.REGULAR,
            pltpu.SemaphoreType.DMA((3,)),
            pltpu.SemaphoreType.DMA((7,)),
            pltpu.SemaphoreType.DMA((8,)),
            pltpu.SemaphoreType.DMA((8,)),
            pltpu.SemaphoreType.DMA((18,)),
            pltpu.SemaphoreType.DMA((32,)),
            pltpu.SemaphoreType.DMA((10,)),
            pltpu.SemaphoreType.DMA((16,)),
        ],
        compiler_params=pltpu.CompilerParams(
            collective_id=0, has_side_effects=True, vmem_limit_bytes=48 * 1024 * 1024
        ),
        name="block",
    )(
        *(pltpu.with_memory_space_constraint(v, pltpu.HBM) for v in (
        pair, tile_mask, w_first, b_first.reshape(1, -1), w_second, b_second.reshape(1, -1),
        norm_gain.reshape(1, -1), w_proj,
    )))


def solution(mesh):
    return jax.shard_map(
        body,
        mesh=mesh,
        in_specs=(P("row", "col"), P(), P(), P(), P(), P(), P(), P()),
        out_specs=P(("row", "col"), None),
        check_vma=False,
    )
```

```python
import functools

import jax
import jax.numpy as jnp
from jax import lax
from jax.experimental import pallas as pl
from jax.experimental.pallas import tpu as pltpu
from jax.sharding import PartitionSpec as P

TILE = 64
EPSILON = 1e-05
MESH = pl.DeviceIdType.MESH
F32 = jnp.float32
BF16 = jnp.bfloat16

ROWS = 128
PAIRS = 32
EDGE = 16
GROUPS = 16
OWN = 128
LANES = PAIRS * 128


def elu(v):
    return jnp.where(v > 0, v, jnp.exp(jnp.minimum(v, 0.0)) - 1.0)


def kernel(
    n_row, n_col,
    pair, mask_in, w1_in, b1_in, w2_in, b2_in, gain_in, wp_in,
    out,
    mask, w1, b1, w2, b2, gain, wp, xe, xm, xp, hb, wt1, wt2, hs, xs, racc, cacc, csum, compact, landed, side, side_pre, edge_pre, gather, rsend, csend, rrecv, crecv, res,
    ready, load_sem, small_sem, halo_send, halo_recv, row_send, row_recv, col_send, col_recv,
):
    r = lax.axis_index("row")
    c = lax.axis_index("col")
    me = r * n_col + c
    n_all = n_row * n_col

    loads = [
        pltpu.make_async_copy(
            pair.at[pl.ds(start, size)], xe.at[pl.ds(EDGE + start, size), pl.ds(OWN, LANES)], load_sem.at[k]
        )
        for k, (start, size) in enumerate(((0, EDGE), (ROWS - EDGE, EDGE), (EDGE, ROWS - 2 * EDGE)))
    ]
    small = [(mask_in, mask), (w1_in, w1), (w2_in, w2), (b1_in, b1), (b2_in, b2), (gain_in, gain), (wp_in, wp)]
    small = [
        pltpu.make_async_copy(src, dst, small_sem.at[k]) for k, (src, dst) in enumerate(small)
    ]
    barrier = pltpu.get_barrier_semaphore()

    def greet(semaphore, tr, tc):
        pl.semaphore_signal(semaphore, inc=1, device_id=(tr, tc), device_id_type=MESH)

    up, down = lax.rem(r + n_row - 1, n_row), lax.rem(r + 1, n_row)
    left, right = lax.rem(c + n_col - 1, n_col), lax.rem(c + 1, n_col)
    above, below, whole = pl.ds(0, EDGE), pl.ds(EDGE + ROWS, EDGE), pl.ds(EDGE, ROWS)
    before, after = pl.ds(0, 128), pl.ds(OWN + LANES, 128)
    first, last = pl.ds(OWN, 128), pl.ds(OWN + LANES - 128, 128)
    top, bottom = pl.ds(EDGE, EDGE), pl.ds(ROWS, EDGE)
    inner, low, high = pl.ds(EDGE, ROWS), pl.ds(0, EDGE), pl.ds(EDGE + ROWS, EDGE)
    has_up, has_down, has_left, has_right = r > 0, r < n_row - 1, c > 0, c < n_col - 1
    halos = [
        (has_up, up, c, compact.at[0, pl.ds(16, 32)], landed.at[1, pl.ds(16, 32)]),
        (has_down, down, c, compact.at[3, pl.ds(16, 32)], landed.at[0, pl.ds(16, 32)]),
        (has_left, r, left, xe.at[whole, first], side.at[1, inner]),
        (has_right, r, right, xe.at[whole, last], side.at[0, inner]),
        (has_up & has_left, up, left, xe.at[top, first], side.at[1, high]),
        (has_up & has_right, up, right, xe.at[top, last], side.at[0, high]),
        (has_down & has_left, down, left, xe.at[bottom, first], side.at[1, low]),
        (has_down & has_right, down, right, xe.at[bottom, last], side.at[0, low]),
    ]
    for k in range(1, n_row):
        greet(barrier, lax.rem(r + k, n_row), c)
    for present, tr, tc, _, _ in halos[4:]:
        @pl.when(present)
        def _():
            greet(barrier, tr, tc)

    for k in range(1, n_col):
        greet(barrier, r, lax.rem(c + k, n_col))
    for copy in loads + small:
        copy.start()
    part = lax.rem(me, 8)

    xe[above, :] = jnp.zeros((EDGE, xe.shape[1]), BF16)
    xe[below, :] = jnp.zeros((EDGE, xe.shape[1]), BF16)
    xe[whole, before] = jnp.zeros((ROWS, 128), BF16)
    xe[whole, after] = jnp.zeros((ROWS, 128), BF16)
    for k in range(2):
        landed[k, pl.ds(0, 16), :] = jnp.zeros((16, 256), BF16)
        landed[k, pl.ds(48, 16), :] = jnp.zeros((16, 256), BF16)
    for k in range(4):
        compact[k, pl.ds(0, 16), :] = jnp.zeros((16, 256), BF16)
        compact[k, pl.ds(48, 16), :] = jnp.zeros((16, 256), BF16)

    for k, present, place in ((0, has_up, low), (1, has_down, high)):
        @pl.when(jnp.logical_not(present))
        def _():
            landed[k, pl.ds(16, 32), :] = jnp.zeros((32, 256), BF16)
            side[:, place] = jnp.zeros((2, EDGE, 128), BF16)

    for k, present in ((0, has_left), (1, has_right)):
        @pl.when(jnp.logical_not(present))
        def _():
            side[k] = jnp.zeros((ROWS + 2 * EDGE, 128), BF16)

    row_edge = ((c == 0) & has_up) | ((c == n_col - 1) & has_down)
    col_edge = ((part == 0) & (me > 0)) | ((part == 7) & (me < n_all - 1))

    @pl.when(jnp.logical_not(row_edge))
    def _():
        rrecv[pl.ds(n_col, n_col)] = jnp.zeros((n_col, 4, 128), F32)

    @pl.when(jnp.logical_not(col_edge))
    def _():
        crecv[pl.ds(n_row, n_row)] = jnp.zeros((n_row, 4, 128), F32)

    i = lax.broadcasted_iota(jnp.int32, (64, 256), 0)
    j = lax.broadcasted_iota(jnp.int32, (64, 256), 1)
    for k in range(2):
        loads[k].wait()
        cells = jnp.concatenate(
            [xe[pl.ds(EDGE + (ROWS - EDGE) * k, EDGE), pl.ds(OWN + 256 * g, 256)] for g in range(GROUPS)], axis=0
        )
        row = (EDGE - 4) * k + (i // 32) * 2 + i % 2
        select = jnp.where(j == (i % 32 // 2) * 16 + row, 1.0, 0.0).astype(BF16)
        both = jnp.dot(select, cells, preferred_element_type=F32).astype(BF16)
        compact[2 * k, pl.ds(16, 32), :] = both[:32]
        compact[2 * k + 1, pl.ds(16, 32), :] = both[32:]

    loads[2].wait()
    corners = (has_up.astype(jnp.int32) + has_down.astype(jnp.int32)) * (
        has_left.astype(jnp.int32) + has_right.astype(jnp.int32)
    )
    pl.semaphore_wait(barrier, (n_row - 1) + (n_col - 1) + corners)
    copies = []
    for k in (0, 1, 4, 5, 6, 7, 2, 3):
        present, tr, tc, src, dst = halos[k]
        copy = pltpu.make_async_remote_copy(
            src_ref=src, dst_ref=dst, send_sem=halo_send.at[k], recv_sem=halo_recv.at[k],
            device_id=(tr, tc), device_id_type=MESH,
        )
        copies.append((present, k, copy))

        @pl.when(present)
        def _():
            copy.start()

    for k in range(1, n_col):
        greet(ready, r, lax.rem(c + k, n_col))

    for copy in small:
        copy.wait()

    zero = jnp.zeros((64, 64), BF16)
    wt1[...] = jnp.zeros_like(wt1)
    for a in range(3):
        for b in range(3):
            w = w1[a, b]
            doubled = jnp.concatenate(
                [jnp.concatenate([w, zero], axis=1), jnp.concatenate([zero, w], axis=1)], axis=0
            )
            for n in range(2):
                wt1[pl.ds(a * 512 + (b + n) * 128, 128), pl.ds(n * 128, 128)] = doubled
            w = w2[a, b]
            wt2[pl.ds((a * 3 + b) * 128, 128), :] = jnp.concatenate(
                [jnp.concatenate([w, zero], axis=1), jnp.concatenate([zero, w], axis=1)], axis=0
            )
    bias_one = jnp.concatenate([b1[...]] * 4, axis=1)
    bias_two = jnp.concatenate([b2[...]] * 2, axis=1)

    def tile(t, v):
        ti = 2 * r - 1 + t
        tj = c + v
        ok = (ti >= 0) & (ti < 2 * n_row) & (tj >= 0) & (tj < n_col)
        value = mask[jnp.clip(ti, 0, 2 * n_row - 1), jnp.clip(tj, 0, n_col - 1)]
        return jnp.where(ok, value, 0).astype(F32)

    mt = [[tile(t, v) for v in (0, -1, 1)] for t in range(4)]

    def by_row(rows, v):
        return jnp.where(
            rows < 0, mt[0][v], jnp.where(rows < 64, mt[1][v], jnp.where(rows < 128, mt[2][v], mt[3][v]))
        )

    def expand(buffer, k):
        window = buffer[k]
        return jnp.concatenate([window[14:46, 128:], window[16:48], window[18:50, :128]], axis=1)

    def fold(parts):
        both = functools.reduce(jnp.add, parts)
        return both[:, :128] + both[:, 128:]

    def split(values):
        high_part = values.astype(BF16)
        return jnp.concatenate([high_part, (values - high_part.astype(F32)).astype(BF16)], axis=0)

    @pl.loop(0, ROWS // 16)
    def _(k):
        r0 = pl.multiple_of(16 * k, 16)
        window = xe[pl.ds(r0, 48), :]
        xm[...] = window[14:30]
        xp[...] = window[18:34]
        lhs = []
        for g in range(GROUPS):
            lanes = pl.ds(g * 256, 512)
            lhs.append(jnp.concatenate([xm[:, lanes], xe[pl.ds(EDGE + r0, 16), lanes], xp[:, lanes]], axis=1))
        pre = jnp.dot(jnp.concatenate(lhs, axis=0), wt1[...], preferred_element_type=F32) + bias_one
        side_pre[0, pl.ds(r0, 16), :] = pre[:16, :128]
        side_pre[1, pl.ds(r0, 16), :] = pre[-16:, 128:]
        h = elu(pre)
        parts = [h[16 * g : 16 * g + 16] for g in range(GROUPS)]
        for g, piece in enumerate(parts):
            hb[pl.ds(r0, 16), pl.ds(g * 256, 256)] = piece.astype(BF16)
        at_row = r0 + lax.broadcasted_iota(jnp.int32, (16, 128), 0)
        final = (at_row >= 2) & (at_row < ROWS - 2)
        for n, value in enumerate((parts[0][:, 128:], fold(parts[1:-1]), parts[-1][:, :128])):
            hs[n, pl.ds(r0, 16), :] = jnp.where(final, value, 0.0)
        cells = xe[pl.ds(EDGE + r0, 16), pl.ds(OWN, LANES)].astype(F32)
        xs[pl.ds(r0, 16), :] = functools.reduce(
            jnp.add, [cells[:, p * 128 : (p + 1) * 128] for p in range(PAIRS)]
        )

    for k in range(2):
        lhs = jnp.concatenate([expand(compact, 2 * k), expand(compact, 2 * k + 1)], axis=1)
        edge_pre[k] = (
            jnp.dot(lhs, wt1[pl.ds(512 * (1 - k), 1024), :], preferred_element_type=F32) + bias_one
        )

    combos = [(a, v) for a in range(3) for v in range(3)]
    at = lax.broadcasted_iota(jnp.int32, (16, 128), 1)
    which = lax.broadcasted_iota(jnp.int32, (16, 128), 0)
    own_at = by_row(at, 0)
    pick = jnp.zeros((16, 128), F32)
    for k, (a, v) in enumerate(combos):
        pick = jnp.where(which == k, by_row(at - 4 * (a - 1), v), pick)
    pick = pick * own_at
    inside = jnp.where((at >= 2) & (at < ROWS - 2), pick, 0.0)
    weights = jnp.concatenate([inside, jnp.where(which == 9, own_at, 0.0)], axis=1).astype(BF16)
    pick = pick.astype(BF16)
    for g in range(GROUPS):
        cells = jnp.concatenate(
            [hb[:, pl.ds(g * 256, 256)], xe[pl.ds(EDGE, ROWS), pl.ds(OWN + g * 256, 256)]], axis=0
        )
        sums = jnp.dot(weights, cells, preferred_element_type=F32)
        csum[pl.ds(g * 32, 16), :] = sums[:, :128]
        csum[pl.ds(g * 32 + 16, 16), :] = sums[:, 128:]
    cacc[...] = jnp.zeros_like(cacc)
    cacc[pl.ds(8, PAIRS), :] = csum[pl.ds(9, PAIRS, stride=16), :] + bias_two * (
        64.0 * (mt[1][0] + mt[2][0])
    )

    i = lax.broadcasted_iota(jnp.int32, (112, 128), 0)
    j = lax.broadcasted_iota(jnp.int32, (112, 128), 1)
    lower = j // 64
    pair_at = j % 32 // 2 * 2 + j // 32 % 2
    by_column = (lower == i // 32) & (pair_at == i % 32) & (pair_at > 0) & (pair_at < PAIRS - 1)
    kind = (i - 64) // 16
    in_kind = ((kind == 0) & (pair_at >= 2) & (pair_at < PAIRS - 2)) | (
        (kind > 0) & (pair_at == jnp.where(kind == 1, 1, PAIRS - 2))
    )
    by_line = in_kind & (lower == (i // 8) % 2) & (j % 2 + 6 * lower == i % 8)
    gather[...] = jnp.where(((i < 64) & by_column) | ((i >= 64) & by_line), 1.0, 0.0).astype(BF16)

    sender = (has_down, has_up, has_right, has_left, has_down & has_right, has_down & has_left,
              has_up & has_right, has_up & has_left)
    for _, k, copy in copies:
        @pl.when(sender[k])
        def _():
            copy.wait_recv()

    edges = []
    for k in range(2):
        edges.append(jnp.dot(expand(landed, k), wt1[pl.ds(1024 * k, 512), :], preferred_element_type=F32))
    line = lax.broadcasted_iota(jnp.int32, (8, 128), 0)
    flat = []
    for k in range(2):
        window = side[k]
        lhs = jnp.concatenate([window[14:142], window[16:144], window[18:146]], axis=1)
        taps = jnp.concatenate([wt1[pl.ds(a * 512 + 256 * k, 128), pl.ds(0, 128)] for a in range(3)], axis=0)
        term = jnp.dot(lhs, taps, preferred_element_type=F32)
        value = side_pre[k] + term
        if k == 0:
            head, tail = edges[0][:8, :128], pltpu.roll(edges[1][:8, :128], 6, 0)
        else:
            head, tail = pltpu.roll(edges[0][24:, 128:], 2, 0), edges[1][24:, 128:]
        value = jnp.concatenate(
            [
                value[:8] + jnp.where(line < 2, head, 0.0),
                value[8:120],
                value[120:] + jnp.where(line >= 6, tail, 0.0),
            ],
            axis=0,
        )
        flat.append(elu(value))
    sums = jnp.dot(
        pick, jnp.concatenate([v.astype(BF16) for v in flat], axis=1), preferred_element_type=F32
    )
    csum[pl.ds(0, 16), :] = sums[:, :128]
    csum[pl.ds(16 * (PAIRS - 1), 16), :] = sums[:, 128:]
    edges = [elu(edge_pre[k] + edges[k]).astype(BF16) for k in range(2)]
    cells = jnp.concatenate([edges[0][:, :128], edges[0][:, 128:], edges[1][:, :128], edges[1][:, 128:]], axis=0)
    found = jnp.dot(gather[...], cells, preferred_element_type=F32)

    def column(a, v):
        upper = mt[1][0] * (mt[0][v] if a == 2 else mt[1][v])
        under = mt[2][0] * (mt[3][v] if a == 0 else mt[2][v])
        return csum[pl.ds(3 * a + v, PAIRS, stride=16), :] + upper * found[:32] + under * found[32:64]

    at_pair = lax.broadcasted_iota(jnp.int32, (PAIRS, 128), 0)
    for b in range(3):
        pieces = []
        for a in range(3):
            value = column(a, 0)
            if b == 0:
                value = jnp.where(at_pair >= PAIRS - 2, column(a, 2), value)
            if b == 2:
                value = jnp.where(at_pair < 2, column(a, 1), value)
            pieces.append(value)
        weights = jnp.concatenate([wt2[pl.ds((a * 3 + b) * 128, 128), :] for a in range(3)], axis=0)
        both = jnp.dot(split(jnp.concatenate(pieces, axis=1)), weights, preferred_element_type=F32)
        cacc[pl.ds(8 - 2 * (b - 1), PAIRS), :] += both[:PAIRS] + both[PAIRS:]
    columns = cacc[pl.ds(4, 40), :]
    for k in range(10):
        csend[k] = columns[4 * k : 4 * k + 4]

    def post(src, dst, send_sem, recv_sem, tr, tc):
        mine = (tr == r) & (tc == c)

        @pl.when(mine)
        def _():
            pltpu.make_async_copy(src, dst, recv_sem).start()

        @pl.when(jnp.logical_not(mine))
        def _():
            pltpu.make_async_remote_copy(
                src_ref=src, dst_ref=dst, send_sem=send_sem, recv_sem=recv_sem, device_id=(tr, tc),
                device_id_type=MESH,
            ).start()

    def col_target(k):
        target = lax.rem(8 * c - 1 + k + n_all, n_all)
        return target // n_col, lax.rem(target, n_col)

    pl.semaphore_wait(ready, n_col - 1)
    for k in range(1, 9):
        post(csend.at[k], crecv.at[r], col_send.at[k], col_recv.at[r], *col_target(k))
    for k, present in ((0, has_left), (9, has_right)):
        @pl.when(present)
        def _():
            post(
                csend.at[k], crecv.at[n_row + r], col_send.at[k], col_recv.at[n_row + r], *col_target(k)
            )

    for k in range(2):
        hs[2 * k] += flat[k]
    for k, n in enumerate((1, 0, 2)):
        hs[n, pl.ds(0, 8), :] += found[64 + 16 * k : 72 + 16 * k]
        hs[n, pl.ds(ROWS - 8, 8), :] += found[72 + 16 * k : 80 + 16 * k]
    rows = lax.broadcasted_iota(jnp.int32, (ROWS, 128), 0)
    own = by_row(rows, 0)
    sum_l, sum_m, sum_r = (hs[k] * own for k in range(3))
    racc[...] = jnp.zeros_like(racc)
    racc[pl.ds(8, ROWS), :] = (xs[...] + 32.0 * bias_two) * own
    for a in range(3):
        out_rows = rows - 4 * (a - 1)
        m0, ml, mr = (by_row(out_rows, v) for v in range(3))
        lhs = split(
            jnp.concatenate(
                [
                    m0 * (sum_l + sum_m) + mr * sum_r,
                    m0 * (sum_l + sum_m + sum_r),
                    m0 * (sum_m + sum_r) + ml * sum_l,
                ],
                axis=1,
            )
        )
        both = jnp.dot(lhs, wt2[pl.ds(a * 384, 384), :], preferred_element_type=F32)
        racc[pl.ds(8 - 4 * (a - 1), ROWS), :] += both[:ROWS] + both[ROWS:]
    racc[...] = racc[...] + pltpu.roll(racc[...], 64, 1)
    half = lax.broadcasted_iota(jnp.int32, (72, 128), 1) < 64
    paired = jnp.where(half, racc[pl.ds(0, 72, stride=2), :], racc[pl.ds(1, 72, stride=2), :])
    for k in range(18):
        rsend[k] = paired[4 * k : 4 * k + 4]


    for k, present, tr, tc in ((0, has_up, up, n_col - 1), (17, has_down, down, 0)):
        @pl.when(present)
        def _():
            pltpu.make_async_remote_copy(
                src_ref=rsend.at[k], dst_ref=rrecv.at[n_col + c], send_sem=row_send.at[k],
                recv_sem=row_recv.at[n_col + c], device_id=(tr, tc), device_id_type=MESH,
            ).start()

    rrecv[c] = rsend[c + 1]
    for k in range(1, n_col):
        tc = lax.rem(c + k, n_col)
        pltpu.make_async_remote_copy(
            src_ref=rsend.at[tc + 1], dst_ref=rrecv.at[c], send_sem=row_send.at[k], recv_sem=row_recv.at[c],
            device_id=(r, tc), device_id_type=MESH,
        ).start()

    def arrived(buffer, sem, slot):
        pltpu.make_async_copy(buffer.at[slot], buffer.at[slot], sem.at[slot]).wait()

    for k in range(1, n_col):
        arrived(rrecv, row_recv, lax.rem(c + k, n_col))

    @pl.when(row_edge)
    def _():
        for k in range(n_col):
            arrived(rrecv, row_recv, n_col + k)

    for k in range(n_row):
        arrived(crecv, col_recv, k)

    @pl.when(col_edge)
    def _():
        for k in range(n_row):
            arrived(crecv, col_recv, n_row + k)

    sums = jnp.sum(rrecv[...], axis=0) + jnp.sum(crecv[...], axis=0)
    res[pl.ds(0, 4, stride=2), :] = sums
    res[pl.ds(1, 4, stride=2), :] = pltpu.roll(sums, 64, 1)
    pooled = res[:, :64]
    center = jnp.mean(pooled, axis=1, keepdims=True)
    spread = jnp.mean((pooled - center) ** 2, axis=1, keepdims=True)
    normed = ((pooled - center) / jnp.sqrt(spread + EPSILON) * gain[...]).astype(BF16)
    out[...] = jnp.dot(normed, wp[...], preferred_element_type=F32).astype(BF16)

    for present, _, copy in copies:
        @pl.when(present)
        def _():
            copy.wait_send()

    for k in range(18):
        if k != n_col:
            @pl.when(has_up if k == 0 else has_down if k == 17 else r >= 0)
            def _():
                pltpu.make_async_copy(rsend.at[k], rsend.at[k], row_send.at[k]).wait()

    for k in range(10):
        tr, tc = col_target(k)

        @pl.when((has_left if k == 0 else has_right if k == 9 else r >= 0) & ((tr != r) | (tc != c)))
        def _():
            pltpu.make_async_copy(csend.at[k], csend.at[k], col_send.at[k]).wait()


def body(pair, tile_mask, w_first, b_first, w_second, b_second, norm_gain, w_proj):
    n_row, n_col = lax.axis_size("row"), lax.axis_size("col")
    hbm = pl.BlockSpec(memory_space=pltpu.HBM)
    return pl.pallas_call(
        functools.partial(kernel, n_row, n_col),
        out_shape=pltpu.VMEM((8, w_proj.shape[1]), BF16),
        in_specs=[hbm] * 8,
        out_specs=pl.BlockSpec(memory_space=pltpu.VMEM),
        scratch_shapes=[
            pltpu.SMEM(tile_mask.shape, jnp.int32),
            pltpu.VMEM(w_first.shape, BF16),
            pltpu.VMEM((1, 64), F32),
            pltpu.VMEM(w_second.shape, BF16),
            pltpu.VMEM((1, 64), F32),
            pltpu.VMEM((1, 64), F32),
            pltpu.VMEM(w_proj.shape, BF16),
            pltpu.VMEM((ROWS + 2 * EDGE, LANES + 256), BF16),
            pltpu.VMEM((16, LANES + 256), BF16),
            pltpu.VMEM((16, LANES + 256), BF16),
            pltpu.VMEM((ROWS, LANES), BF16),
            pltpu.VMEM((1536, 256), BF16),
            pltpu.VMEM((1152, 128), BF16),
            pltpu.VMEM((3, ROWS, 128), F32),
            pltpu.VMEM((ROWS, 128), F32),
            pltpu.VMEM((144, 128), F32),
            pltpu.VMEM((48, 128), F32),
            pltpu.VMEM((512, 128), F32),
            pltpu.VMEM((4, 64, 256), BF16),
            pltpu.VMEM((2, 64, 256), BF16),
            pltpu.VMEM((2, ROWS + 2 * EDGE, 128), BF16),
            pltpu.VMEM((2, ROWS, 128), F32),
            pltpu.VMEM((2, 32, 256), F32),
            pltpu.VMEM((112, 128), BF16),
            pltpu.VMEM((18, 4, 128), F32),
            pltpu.VMEM((10, 4, 128), F32),
            pltpu.VMEM((32, 4, 128), F32),
            pltpu.VMEM((16, 4, 128), F32),
            pltpu.VMEM((8, 128), F32),
            pltpu.SemaphoreType.REGULAR,
            pltpu.SemaphoreType.DMA((3,)),
            pltpu.SemaphoreType.DMA((7,)),
            pltpu.SemaphoreType.DMA((8,)),
            pltpu.SemaphoreType.DMA((8,)),
            pltpu.SemaphoreType.DMA((18,)),
            pltpu.SemaphoreType.DMA((32,)),
            pltpu.SemaphoreType.DMA((10,)),
            pltpu.SemaphoreType.DMA((16,)),
        ],
        compiler_params=pltpu.CompilerParams(
            collective_id=0, has_side_effects=True, vmem_limit_bytes=48 * 1024 * 1024
        ),
        name="block",
    )(
        *(pltpu.with_memory_space_constraint(v, pltpu.HBM) for v in (
        pair, tile_mask, w_first, b_first.reshape(1, -1), w_second, b_second.reshape(1, -1),
        norm_gain.reshape(1, -1), w_proj,
    )))


def solution(mesh):
    return jax.shard_map(
        body,
        mesh=mesh,
        in_specs=(P("row", "col"), P(), P(), P(), P(), P(), P(), P()),
        out_specs=P(("row", "col"), None),
        check_vma=False,
    )
```

```python
import functools

import jax
import jax.numpy as jnp
from jax import lax
from jax.experimental import pallas as pl
from jax.experimental.pallas import tpu as pltpu
from jax.sharding import PartitionSpec as P

TILE = 64
EPSILON = 1e-05
MESH = pl.DeviceIdType.MESH
F32 = jnp.float32
BF16 = jnp.bfloat16

ROWS = 128
PAIRS = 32
EDGE = 16
GROUPS = 16
OWN = 128
LANES = PAIRS * 128
SPLIT = 4


def elu(v):
    return jnp.where(v > 0, v, jnp.exp(jnp.minimum(v, 0.0)) - 1.0)


def kernel(
    n_row, n_col,
    pair, mask_in, w1_in, b1_in, w2_in, b2_in, gain_in, wp_in,
    out,
    mask, w1, b1, w2, b2, gain, wp, xe, xm, xp, hb, wt1, wt2, hs, xs, racc, cacc, csum, compact, landed, side, side_pre, edge_pre, gather, rsend, csend, rrecv, crecv, res,
    ready, known, load_sem, small_sem, halo_send, halo_recv, row_send, row_recv, col_send, col_recv,
):
    r = lax.axis_index("row")
    c = lax.axis_index("col")
    me = r * n_col + c
    n_all = n_row * n_col

    loads = [
        pltpu.make_async_copy(
            pair.at[pl.ds(start, size)], xe.at[pl.ds(EDGE + start, size), pl.ds(OWN, LANES)], load_sem.at[k]
        )
        for k, (start, size) in enumerate(((0, EDGE), (ROWS - EDGE, EDGE), (EDGE, ROWS - 2 * EDGE)))
    ]
    small = [(mask_in, mask), (w1_in, w1), (w2_in, w2), (b1_in, b1), (b2_in, b2), (gain_in, gain), (wp_in, wp)]
    small = [
        pltpu.make_async_copy(src, dst, small_sem.at[k]) for k, (src, dst) in enumerate(small)
    ]
    barrier = pltpu.get_barrier_semaphore()

    def greet(semaphore, tr, tc):
        pl.semaphore_signal(semaphore, inc=1, device_id=(tr, tc), device_id_type=MESH)

    up, down = lax.rem(r + n_row - 1, n_row), lax.rem(r + 1, n_row)
    left, right = lax.rem(c + n_col - 1, n_col), lax.rem(c + 1, n_col)
    above, below, whole = pl.ds(0, EDGE), pl.ds(EDGE + ROWS, EDGE), pl.ds(EDGE, ROWS)
    before, after = pl.ds(0, 128), pl.ds(OWN + LANES, 128)
    first, last = pl.ds(OWN, 128), pl.ds(OWN + LANES - 128, 128)
    top, bottom = pl.ds(EDGE, EDGE), pl.ds(ROWS, EDGE)
    inner, low, high = pl.ds(EDGE, ROWS), pl.ds(0, EDGE), pl.ds(EDGE + ROWS, EDGE)
    has_up, has_down, has_left, has_right = r > 0, r < n_row - 1, c > 0, c < n_col - 1
    halos = [
        (has_up, up, c, compact.at[0, pl.ds(16, 32)], landed.at[1, pl.ds(16, 32)]),
        (has_down, down, c, compact.at[3, pl.ds(16, 32)], landed.at[0, pl.ds(16, 32)]),
        (has_left, r, left, xe.at[whole, first], side.at[1, inner]),
        (has_right, r, right, xe.at[whole, last], side.at[0, inner]),
        (has_up & has_left, up, left, xe.at[top, first], side.at[1, high]),
        (has_up & has_right, up, right, xe.at[top, last], side.at[0, high]),
        (has_down & has_left, down, left, xe.at[bottom, first], side.at[1, low]),
        (has_down & has_right, down, right, xe.at[bottom, last], side.at[0, low]),
    ]
    near = (lax.rem(r + 2, n_row), lax.rem(r + n_row - 2, n_row))
    for present, tr, tc, _, _ in halos[:2] + halos[4:]:
        @pl.when(present)
        def _():
            greet(barrier, tr, tc)

    for k in (8, 7, 9, 6, 10, 5, 11, 4, 12, 3, 13, 2, 14, 1, 15):
        greet(barrier, r, lax.rem(c + k, n_col))
    for tr in near:
        greet(barrier, tr, c)
    for copy in loads + small:
        copy.start()
    part = lax.rem(me, 8)

    xe[above, :] = jnp.zeros((EDGE, xe.shape[1]), BF16)
    xe[below, :] = jnp.zeros((EDGE, xe.shape[1]), BF16)
    xe[whole, before] = jnp.zeros((ROWS, 128), BF16)
    xe[whole, after] = jnp.zeros((ROWS, 128), BF16)
    for k in range(2):
        landed[k, pl.ds(0, 16), :] = jnp.zeros((16, 256), BF16)
        landed[k, pl.ds(48, 16), :] = jnp.zeros((16, 256), BF16)
    for k in range(4):
        compact[k, pl.ds(0, 16), :] = jnp.zeros((16, 256), BF16)
        compact[k, pl.ds(48, 16), :] = jnp.zeros((16, 256), BF16)

    for k, present, place in ((0, has_up, low), (1, has_down, high)):
        @pl.when(jnp.logical_not(present))
        def _():
            landed[k, pl.ds(16, 32), :] = jnp.zeros((32, 256), BF16)
            side[:, place] = jnp.zeros((2, EDGE, 128), BF16)

    for k, present in ((0, has_left), (1, has_right)):
        @pl.when(jnp.logical_not(present))
        def _():
            side[k] = jnp.zeros((ROWS + 2 * EDGE, 128), BF16)

    row_edge = ((c == 0) & has_up) | ((c == n_col - 1) & has_down)
    col_edge = ((part == 0) & (me > 0)) | ((part == 7) & (me < n_all - 1))

    @pl.when(jnp.logical_not(row_edge))
    def _():
        rrecv[pl.ds(n_col, n_col)] = jnp.zeros((n_col, 4, 128), F32)

    @pl.when(jnp.logical_not(col_edge))
    def _():
        crecv[pl.ds(n_row, n_row)] = jnp.zeros((n_row, 4, 128), F32)

    i = lax.broadcasted_iota(jnp.int32, (64, 256), 0)
    j = lax.broadcasted_iota(jnp.int32, (64, 256), 1)
    for k in range(2):
        loads[k].wait()
        cells = jnp.concatenate(
            [xe[pl.ds(EDGE + (ROWS - EDGE) * k, EDGE), pl.ds(OWN + 256 * g, 256)] for g in range(GROUPS)], axis=0
        )
        row = (EDGE - 4) * k + (i // 32) * 2 + i % 2
        select = jnp.where(j == (i % 32 // 2) * 16 + row, 1.0, 0.0).astype(BF16)
        both = jnp.dot(select, cells, preferred_element_type=F32).astype(BF16)
        compact[2 * k, pl.ds(16, 32), :] = both[:32]
        compact[2 * k + 1, pl.ds(16, 32), :] = both[32:]

    loads[2].wait()
    beside = has_up.astype(jnp.int32) + has_down.astype(jnp.int32)
    corners = beside * (has_left.astype(jnp.int32) + has_right.astype(jnp.int32))
    pl.semaphore_wait(barrier, (n_col - 1) + beside + len(near) + corners)
    copies = []
    for k in (0, 1, 4, 5, 6, 7, 2, 3):
        present, tr, tc, src, dst = halos[k]
        copy = pltpu.make_async_remote_copy(
            src_ref=src, dst_ref=dst, send_sem=halo_send.at[k], recv_sem=halo_recv.at[k],
            device_id=(tr, tc), device_id_type=MESH,
        )
        copies.append((present, k, copy))

        @pl.when(present)
        def _():
            copy.start()

    for present, tr, tc, _, _ in halos[:2]:
        @pl.when(present)
        def _():
            greet(known, tr, tc)

    for tr in near:
        greet(known, tr, c)

    for copy in small:
        copy.wait()

    zero = jnp.zeros((64, 64), BF16)
    wt1[...] = jnp.zeros_like(wt1)
    for a in range(3):
        for b in range(3):
            w = w1[a, b]
            doubled = jnp.concatenate(
                [jnp.concatenate([w, zero], axis=1), jnp.concatenate([zero, w], axis=1)], axis=0
            )
            for n in range(2):
                wt1[pl.ds(a * 512 + (b + n) * 128, 128), pl.ds(n * 128, 128)] = doubled
            w = w2[a, b]
            wt2[pl.ds((a * 3 + b) * 128, 128), :] = jnp.concatenate(
                [jnp.concatenate([w, zero], axis=1), jnp.concatenate([zero, w], axis=1)], axis=0
            )
    bias_one = jnp.concatenate([b1[...]] * 4, axis=1)
    bias_two = jnp.concatenate([b2[...]] * 2, axis=1)

    def tile(t, v):
        ti = 2 * r - 1 + t
        tj = c + v
        ok = (ti >= 0) & (ti < 2 * n_row) & (tj >= 0) & (tj < n_col)
        value = mask[jnp.clip(ti, 0, 2 * n_row - 1), jnp.clip(tj, 0, n_col - 1)]
        return jnp.where(ok, value, 0).astype(F32)

    mt = [[tile(t, v) for v in (0, -1, 1)] for t in range(4)]

    def by_row(rows, v):
        return jnp.where(
            rows < 0, mt[0][v], jnp.where(rows < 64, mt[1][v], jnp.where(rows < 128, mt[2][v], mt[3][v]))
        )

    def expand(buffer, k):
        window = buffer[k]
        return jnp.concatenate([window[14:46, 128:], window[16:48], window[18:50, :128]], axis=1)

    def fold(parts):
        both = functools.reduce(jnp.add, parts)
        return both[:, :128] + both[:, 128:]

    def split(values):
        high_part = values.astype(BF16)
        return jnp.concatenate([high_part, (values - high_part.astype(F32)).astype(BF16)], axis=0)

    def rows_of(k):
        r0 = pl.multiple_of(16 * k, 16)
        window = xe[pl.ds(r0, 48), :]
        xm[...] = window[14:30]
        xp[...] = window[18:34]
        lhs = []
        for g in range(GROUPS):
            lanes = pl.ds(g * 256, 512)
            lhs.append(jnp.concatenate([xm[:, lanes], xe[pl.ds(EDGE + r0, 16), lanes], xp[:, lanes]], axis=1))
        pre = jnp.dot(jnp.concatenate(lhs, axis=0), wt1[...], preferred_element_type=F32) + bias_one
        side_pre[0, pl.ds(r0, 16), :] = pre[:16, :128]
        side_pre[1, pl.ds(r0, 16), :] = pre[-16:, 128:]
        h = elu(pre)
        parts = [h[16 * g : 16 * g + 16] for g in range(GROUPS)]
        for g, piece in enumerate(parts):
            hb[pl.ds(r0, 16), pl.ds(g * 256, 256)] = piece.astype(BF16)
        at_row = r0 + lax.broadcasted_iota(jnp.int32, (16, 128), 0)
        final = (at_row >= 2) & (at_row < ROWS - 2)
        for n, value in enumerate((parts[0][:, 128:], fold(parts[1:-1]), parts[-1][:, :128])):
            hs[n, pl.ds(r0, 16), :] = jnp.where(final, value, 0.0)
        cells = xe[pl.ds(EDGE + r0, 16), pl.ds(OWN, LANES)].astype(F32)
        xs[pl.ds(r0, 16), :] = functools.reduce(
            jnp.add, [cells[:, p * 128 : (p + 1) * 128] for p in range(PAIRS)]
        )

    pl.loop(0, SPLIT)(rows_of)

    pl.semaphore_wait(known, len(near) + beside)
    odd = lax.rem(c, 2)
    owner_row, edge_row = c // 2, c // 2 - 1 + 2 * odd
    edge_exists = (edge_row >= 0) & (edge_row < n_row)

    for n, tells in ((0, r == owner_row), (1, edge_exists & (r == edge_row))):
        @pl.when(tells)
        def _():
            for k in range(1, n_row):
                greet(ready.at[n], lax.rem(r + k, n_row), c)

    pl.loop(SPLIT, ROWS // 16)(rows_of)

    for k in range(2):
        lhs = jnp.concatenate([expand(compact, 2 * k), expand(compact, 2 * k + 1)], axis=1)
        edge_pre[k] = (
            jnp.dot(lhs, wt1[pl.ds(512 * (1 - k), 1024), :], preferred_element_type=F32) + bias_one
        )

    combos = [(a, v) for a in range(3) for v in range(3)]
    at = lax.broadcasted_iota(jnp.int32, (16, 128), 1)
    which = lax.broadcasted_iota(jnp.int32, (16, 128), 0)
    own_at = by_row(at, 0)
    pick = jnp.zeros((16, 128), F32)
    for k, (a, v) in enumerate(combos):
        pick = jnp.where(which == k, by_row(at - 4 * (a - 1), v), pick)
    pick = pick * own_at
    inside = jnp.where((at >= 2) & (at < ROWS - 2), pick, 0.0)
    weights = jnp.concatenate([inside, jnp.where(which == 9, own_at, 0.0)], axis=1).astype(BF16)
    pick = pick.astype(BF16)
    for g in range(GROUPS):
        cells = jnp.concatenate(
            [hb[:, pl.ds(g * 256, 256)], xe[pl.ds(EDGE, ROWS), pl.ds(OWN + g * 256, 256)]], axis=0
        )
        sums = jnp.dot(weights, cells, preferred_element_type=F32)
        csum[pl.ds(g * 32, 16), :] = sums[:, :128]
        csum[pl.ds(g * 32 + 16, 16), :] = sums[:, 128:]
    cacc[...] = jnp.zeros_like(cacc)
    cacc[pl.ds(8, PAIRS), :] = csum[pl.ds(9, PAIRS, stride=16), :] + bias_two * (
        64.0 * (mt[1][0] + mt[2][0])
    )

    i = lax.broadcasted_iota(jnp.int32, (112, 128), 0)
    j = lax.broadcasted_iota(jnp.int32, (112, 128), 1)
    lower = j // 64
    pair_at = j % 32 // 2 * 2 + j // 32 % 2
    by_column = (lower == i // 32) & (pair_at == i % 32) & (pair_at > 0) & (pair_at < PAIRS - 1)
    kind = (i - 64) // 16
    in_kind = ((kind == 0) & (pair_at >= 2) & (pair_at < PAIRS - 2)) | (
        (kind > 0) & (pair_at == jnp.where(kind == 1, 1, PAIRS - 2))
    )
    by_line = in_kind & (lower == (i // 8) % 2) & (j % 2 + 6 * lower == i % 8)
    gather[...] = jnp.where(((i < 64) & by_column) | ((i >= 64) & by_line), 1.0, 0.0).astype(BF16)

    sender = (has_down, has_up, has_right, has_left, has_down & has_right, has_down & has_left,
              has_up & has_right, has_up & has_left)
    for _, k, copy in copies:
        @pl.when(sender[k])
        def _():
            copy.wait_recv()

    edges = []
    for k in range(2):
        edges.append(jnp.dot(expand(landed, k), wt1[pl.ds(1024 * k, 512), :], preferred_element_type=F32))
    line = lax.broadcasted_iota(jnp.int32, (8, 128), 0)
    flat = []
    for k in range(2):
        window = side[k]
        lhs = jnp.concatenate([window[14:142], window[16:144], window[18:146]], axis=1)
        taps = jnp.concatenate([wt1[pl.ds(a * 512 + 256 * k, 128), pl.ds(0, 128)] for a in range(3)], axis=0)
        term = jnp.dot(lhs, taps, preferred_element_type=F32)
        value = side_pre[k] + term
        if k == 0:
            head, tail = edges[0][:8, :128], pltpu.roll(edges[1][:8, :128], 6, 0)
        else:
            head, tail = pltpu.roll(edges[0][24:, 128:], 2, 0), edges[1][24:, 128:]
        value = jnp.concatenate(
            [
                value[:8] + jnp.where(line < 2, head, 0.0),
                value[8:120],
                value[120:] + jnp.where(line >= 6, tail, 0.0),
            ],
            axis=0,
        )
        flat.append(elu(value))
    sums = jnp.dot(
        pick, jnp.concatenate([v.astype(BF16) for v in flat], axis=1), preferred_element_type=F32
    )
    csum[pl.ds(0, 16), :] = sums[:, :128]
    csum[pl.ds(16 * (PAIRS - 1), 16), :] = sums[:, 128:]
    edges = [elu(edge_pre[k] + edges[k]).astype(BF16) for k in range(2)]
    cells = jnp.concatenate([edges[0][:, :128], edges[0][:, 128:], edges[1][:, :128], edges[1][:, 128:]], axis=0)
    found = jnp.dot(gather[...], cells, preferred_element_type=F32)

    def column(a, v):
        upper = mt[1][0] * (mt[0][v] if a == 2 else mt[1][v])
        under = mt[2][0] * (mt[3][v] if a == 0 else mt[2][v])
        return csum[pl.ds(3 * a + v, PAIRS, stride=16), :] + upper * found[:32] + under * found[32:64]

    at_pair = lax.broadcasted_iota(jnp.int32, (PAIRS, 128), 0)
    for b in range(3):
        pieces = []
        for a in range(3):
            value = column(a, 0)
            if b == 0:
                value = jnp.where(at_pair >= PAIRS - 2, column(a, 2), value)
            if b == 2:
                value = jnp.where(at_pair < 2, column(a, 1), value)
            pieces.append(value)
        weights = jnp.concatenate([wt2[pl.ds((a * 3 + b) * 128, 128), :] for a in range(3)], axis=0)
        both = jnp.dot(split(jnp.concatenate(pieces, axis=1)), weights, preferred_element_type=F32)
        cacc[pl.ds(8 - 2 * (b - 1), PAIRS), :] += both[:PAIRS] + both[PAIRS:]
    columns = cacc[pl.ds(4, 40), :]
    for k in range(10):
        csend[k] = columns[4 * k : 4 * k + 4]

    def post(src, dst, send_sem, recv_sem, tr, tc):
        mine = (tr == r) & (tc == c)

        @pl.when(mine)
        def _():
            pltpu.make_async_copy(src, dst, recv_sem).start()

        @pl.when(jnp.logical_not(mine))
        def _():
            pltpu.make_async_remote_copy(
                src_ref=src, dst_ref=dst, send_sem=send_sem, recv_sem=recv_sem, device_id=(tr, tc),
                device_id_type=MESH,
            ).start()

    def col_target(k):
        target = lax.rem(8 * c - 1 + k + n_all, n_all)
        return target // n_col, lax.rem(target, n_col)

    for k, told in ((0, r != owner_row), (1, edge_exists & (r != edge_row))):
        @pl.when(told)
        def _():
            pl.semaphore_wait(ready.at[k], 1)

    for k in range(1, 9):
        post(csend.at[k], crecv.at[r], col_send.at[k], col_recv.at[r], *col_target(k))
    for k, present in ((0, has_left), (9, has_right)):
        @pl.when(present)
        def _():
            post(
                csend.at[k], crecv.at[n_row + r], col_send.at[k], col_recv.at[n_row + r], *col_target(k)
            )

    for k in range(2):
        hs[2 * k] += flat[k]
    for k, n in enumerate((1, 0, 2)):
        hs[n, pl.ds(0, 8), :] += found[64 + 16 * k : 72 + 16 * k]
        hs[n, pl.ds(ROWS - 8, 8), :] += found[72 + 16 * k : 80 + 16 * k]
    rows = lax.broadcasted_iota(jnp.int32, (ROWS, 128), 0)
    own = by_row(rows, 0)
    sum_l, sum_m, sum_r = (hs[k] * own for k in range(3))
    racc[...] = jnp.zeros_like(racc)
    racc[pl.ds(8, ROWS), :] = (xs[...] + 32.0 * bias_two) * own
    for a in range(3):
        out_rows = rows - 4 * (a - 1)
        m0, ml, mr = (by_row(out_rows, v) for v in range(3))
        lhs = split(
            jnp.concatenate(
                [
                    m0 * (sum_l + sum_m) + mr * sum_r,
                    m0 * (sum_l + sum_m + sum_r),
                    m0 * (sum_m + sum_r) + ml * sum_l,
                ],
                axis=1,
            )
        )
        both = jnp.dot(lhs, wt2[pl.ds(a * 384, 384), :], preferred_element_type=F32)
        racc[pl.ds(8 - 4 * (a - 1), ROWS), :] += both[:ROWS] + both[ROWS:]
    racc[...] = racc[...] + pltpu.roll(racc[...], 64, 1)
    half = lax.broadcasted_iota(jnp.int32, (72, 128), 1) < 64
    paired = jnp.where(half, racc[pl.ds(0, 72, stride=2), :], racc[pl.ds(1, 72, stride=2), :])
    for k in range(18):
        rsend[k] = paired[4 * k : 4 * k + 4]


    for k, present, tr, tc in ((0, has_up, up, n_col - 1), (17, has_down, down, 0)):
        @pl.when(present)
        def _():
            pltpu.make_async_remote_copy(
                src_ref=rsend.at[k], dst_ref=rrecv.at[n_col + c], send_sem=row_send.at[k],
                recv_sem=row_recv.at[n_col + c], device_id=(tr, tc), device_id_type=MESH,
            ).start()

    rrecv[c] = rsend[c + 1]
    for k in range(1, n_col):
        tc = lax.rem(c + k, n_col)
        pltpu.make_async_remote_copy(
            src_ref=rsend.at[tc + 1], dst_ref=rrecv.at[c], send_sem=row_send.at[k], recv_sem=row_recv.at[c],
            device_id=(r, tc), device_id_type=MESH,
        ).start()

    def arrived(buffer, sem, slot):
        pltpu.make_async_copy(buffer.at[slot], buffer.at[slot], sem.at[slot]).wait()

    for k in range(1, n_col):
        arrived(rrecv, row_recv, lax.rem(c + k, n_col))

    @pl.when(row_edge)
    def _():
        for k in range(n_col):
            arrived(rrecv, row_recv, n_col + k)

    for k in range(n_row):
        arrived(crecv, col_recv, k)

    @pl.when(col_edge)
    def _():
        for k in range(n_row):
            arrived(crecv, col_recv, n_row + k)

    sums = jnp.sum(rrecv[...], axis=0) + jnp.sum(crecv[...], axis=0)
    res[pl.ds(0, 4, stride=2), :] = sums
    res[pl.ds(1, 4, stride=2), :] = pltpu.roll(sums, 64, 1)
    pooled = res[:, :64]
    center = jnp.mean(pooled, axis=1, keepdims=True)
    spread = jnp.mean((pooled - center) ** 2, axis=1, keepdims=True)
    normed = ((pooled - center) / jnp.sqrt(spread + EPSILON) * gain[...]).astype(BF16)
    out[...] = jnp.dot(normed, wp[...], preferred_element_type=F32).astype(BF16)

    for present, _, copy in copies:
        @pl.when(present)
        def _():
            copy.wait_send()

    for k in range(18):
        if k != n_col:
            @pl.when(has_up if k == 0 else has_down if k == 17 else r >= 0)
            def _():
                pltpu.make_async_copy(rsend.at[k], rsend.at[k], row_send.at[k]).wait()

    for k in range(10):
        tr, tc = col_target(k)

        @pl.when((has_left if k == 0 else has_right if k == 9 else r >= 0) & ((tr != r) | (tc != c)))
        def _():
            pltpu.make_async_copy(csend.at[k], csend.at[k], col_send.at[k]).wait()


def body(pair, tile_mask, w_first, b_first, w_second, b_second, norm_gain, w_proj):
    n_row, n_col = lax.axis_size("row"), lax.axis_size("col")
    hbm = pl.BlockSpec(memory_space=pltpu.HBM)
    return pl.pallas_call(
        functools.partial(kernel, n_row, n_col),
        out_shape=pltpu.VMEM((8, w_proj.shape[1]), BF16),
        in_specs=[hbm] * 8,
        out_specs=pl.BlockSpec(memory_space=pltpu.VMEM),
        scratch_shapes=[
            pltpu.SMEM(tile_mask.shape, jnp.int32),
            pltpu.VMEM(w_first.shape, BF16),
            pltpu.VMEM((1, 64), F32),
            pltpu.VMEM(w_second.shape, BF16),
            pltpu.VMEM((1, 64), F32),
            pltpu.VMEM((1, 64), F32),
            pltpu.VMEM(w_proj.shape, BF16),
            pltpu.VMEM((ROWS + 2 * EDGE, LANES + 256), BF16),
            pltpu.VMEM((16, LANES + 256), BF16),
            pltpu.VMEM((16, LANES + 256), BF16),
            pltpu.VMEM((ROWS, LANES), BF16),
            pltpu.VMEM((1536, 256), BF16),
            pltpu.VMEM((1152, 128), BF16),
            pltpu.VMEM((3, ROWS, 128), F32),
            pltpu.VMEM((ROWS, 128), F32),
            pltpu.VMEM((144, 128), F32),
            pltpu.VMEM((48, 128), F32),
            pltpu.VMEM((512, 128), F32),
            pltpu.VMEM((4, 64, 256), BF16),
            pltpu.VMEM((2, 64, 256), BF16),
            pltpu.VMEM((2, ROWS + 2 * EDGE, 128), BF16),
            pltpu.VMEM((2, ROWS, 128), F32),
            pltpu.VMEM((2, 32, 256), F32),
            pltpu.VMEM((112, 128), BF16),
            pltpu.VMEM((18, 4, 128), F32),
            pltpu.VMEM((10, 4, 128), F32),
            pltpu.VMEM((32, 4, 128), F32),
            pltpu.VMEM((16, 4, 128), F32),
            pltpu.VMEM((8, 128), F32),
            pltpu.SemaphoreType.REGULAR((2,)),
            pltpu.SemaphoreType.REGULAR,
            pltpu.SemaphoreType.DMA((3,)),
            pltpu.SemaphoreType.DMA((7,)),
            pltpu.SemaphoreType.DMA((8,)),
            pltpu.SemaphoreType.DMA((8,)),
            pltpu.SemaphoreType.DMA((18,)),
            pltpu.SemaphoreType.DMA((32,)),
            pltpu.SemaphoreType.DMA((10,)),
            pltpu.SemaphoreType.DMA((16,)),
        ],
        compiler_params=pltpu.CompilerParams(
            collective_id=0, has_side_effects=True, vmem_limit_bytes=48 * 1024 * 1024
        ),
        name="block",
    )(
        *(pltpu.with_memory_space_constraint(v, pltpu.HBM) for v in (
        pair, tile_mask, w_first, b_first.reshape(1, -1), w_second, b_second.reshape(1, -1),
        norm_gain.reshape(1, -1), w_proj,
    )))


def solution(mesh):
    return jax.shard_map(
        body,
        mesh=mesh,
        in_specs=(P("row", "col"), P(), P(), P(), P(), P(), P(), P()),
        out_specs=P(("row", "col"), None),
        check_vma=False,
    )
```

```python
import functools

import jax
import jax.numpy as jnp
from jax import lax
from jax.experimental import pallas as pl
from jax.experimental.pallas import tpu as pltpu
from jax.sharding import PartitionSpec as P

TILE = 64
EPSILON = 1e-05
MESH = pl.DeviceIdType.MESH
F32 = jnp.float32
BF16 = jnp.bfloat16

ROWS = 128
PAIRS = 32
EDGE = 16
GROUPS = 16
OWN = 128
LANES = PAIRS * 128
SPLIT = 4


def elu(v):
    return jnp.where(v > 0, v, jnp.exp(jnp.minimum(v, 0.0)) - 1.0)


def kernel(
    n_row, n_col,
    pair, mask_in, w1_in, b1_in, w2_in, b2_in, gain_in, wp_in,
    out,
    mask, w1, b1, w2, b2, gain, wp, xe, xm, xp, hb, wt1, wt2, hs, xs, racc, cacc, csum, compact, landed, side, side_pre, edge_pre, gather, rsend, csend, rrecv, crecv, res,
    ready, known, load_sem, small_sem, halo_send, halo_recv, row_send, row_recv, col_send, col_recv,
):
    r = lax.axis_index("row")
    c = lax.axis_index("col")
    me = r * n_col + c
    n_all = n_row * n_col

    loads = [
        pltpu.make_async_copy(
            pair.at[pl.ds(start, size)], xe.at[pl.ds(EDGE + start, size), pl.ds(OWN, LANES)], load_sem.at[k]
        )
        for k, (start, size) in enumerate(((0, EDGE), (ROWS - EDGE, EDGE), (EDGE, ROWS - 2 * EDGE)))
    ]
    small = [(mask_in, mask), (w1_in, w1), (w2_in, w2), (b1_in, b1), (b2_in, b2), (gain_in, gain), (wp_in, wp)]
    small = [
        pltpu.make_async_copy(src, dst, small_sem.at[k]) for k, (src, dst) in enumerate(small)
    ]
    barrier = pltpu.get_barrier_semaphore()

    def greet(semaphore, tr, tc):
        pl.semaphore_signal(semaphore, inc=1, device_id=(tr, tc), device_id_type=MESH)

    up, down = lax.rem(r + n_row - 1, n_row), lax.rem(r + 1, n_row)
    left, right = lax.rem(c + n_col - 1, n_col), lax.rem(c + 1, n_col)
    above, below, whole = pl.ds(0, EDGE), pl.ds(EDGE + ROWS, EDGE), pl.ds(EDGE, ROWS)
    before, after = pl.ds(0, 128), pl.ds(OWN + LANES, 128)
    first, last = pl.ds(OWN, 128), pl.ds(OWN + LANES - 128, 128)
    top, bottom = pl.ds(EDGE, EDGE), pl.ds(ROWS, EDGE)
    inner, low, high = pl.ds(EDGE, ROWS), pl.ds(0, EDGE), pl.ds(EDGE + ROWS, EDGE)
    has_up, has_down, has_left, has_right = r > 0, r < n_row - 1, c > 0, c < n_col - 1
    halos = [
        (has_up, up, c, compact.at[0, pl.ds(16, 32)], landed.at[1, pl.ds(16, 32)]),
        (has_down, down, c, compact.at[3, pl.ds(16, 32)], landed.at[0, pl.ds(16, 32)]),
        (has_left, r, left, xe.at[whole, first], side.at[1, inner]),
        (has_right, r, right, xe.at[whole, last], side.at[0, inner]),
        (has_up & has_left, up, left, xe.at[top, first], side.at[1, high]),
        (has_up & has_right, up, right, xe.at[top, last], side.at[0, high]),
        (has_down & has_left, down, left, xe.at[bottom, first], side.at[1, low]),
        (has_down & has_right, down, right, xe.at[bottom, last], side.at[0, low]),
    ]
    near = (lax.rem(r + 2, n_row), lax.rem(r + n_row - 2, n_row))
    for present, tr, tc, _, _ in halos[:2] + halos[4:]:
        @pl.when(present)
        def _():
            greet(barrier, tr, tc)

    for k in (8, 7, 9, 6, 10, 5, 11, 4, 12, 3, 13, 2, 14, 1, 15):
        greet(barrier, r, lax.rem(c + k, n_col))
    for tr in near:
        greet(barrier, tr, c)
    for copy in loads + small:
        copy.start()
    part = lax.rem(me, 8)

    xe[above, :] = jnp.zeros((EDGE, xe.shape[1]), BF16)
    xe[below, :] = jnp.zeros((EDGE, xe.shape[1]), BF16)
    xe[whole, before] = jnp.zeros((ROWS, 128), BF16)
    xe[whole, after] = jnp.zeros((ROWS, 128), BF16)
    for k in range(2):
        landed[k, pl.ds(0, 16), :] = jnp.zeros((16, 256), BF16)
        landed[k, pl.ds(48, 16), :] = jnp.zeros((16, 256), BF16)
    for k in range(4):
        compact[k, pl.ds(0, 16), :] = jnp.zeros((16, 256), BF16)
        compact[k, pl.ds(48, 16), :] = jnp.zeros((16, 256), BF16)

    for k, present, place in ((0, has_up, low), (1, has_down, high)):
        @pl.when(jnp.logical_not(present))
        def _():
            landed[k, pl.ds(16, 32), :] = jnp.zeros((32, 256), BF16)
            side[:, place] = jnp.zeros((2, EDGE, 128), BF16)

    for k, present in ((0, has_left), (1, has_right)):
        @pl.when(jnp.logical_not(present))
        def _():
            side[k] = jnp.zeros((ROWS + 2 * EDGE, 128), BF16)

    row_edge = ((c == 0) & has_up) | ((c == n_col - 1) & has_down)
    col_edge = ((part == 0) & (me > 0)) | ((part == 7) & (me < n_all - 1))

    @pl.when(jnp.logical_not(row_edge))
    def _():
        rrecv[pl.ds(n_col, n_col)] = jnp.zeros((n_col, 4, 128), F32)

    @pl.when(jnp.logical_not(col_edge))
    def _():
        crecv[pl.ds(n_row, n_row)] = jnp.zeros((n_row, 4, 128), F32)

    i = lax.broadcasted_iota(jnp.int32, (64, 256), 0)
    j = lax.broadcasted_iota(jnp.int32, (64, 256), 1)
    for k in range(2):
        loads[k].wait()
        cells = jnp.concatenate(
            [xe[pl.ds(EDGE + (ROWS - EDGE) * k, EDGE), pl.ds(OWN + 256 * g, 256)] for g in range(GROUPS)], axis=0
        )
        row = (EDGE - 4) * k + (i // 32) * 2 + i % 2
        select = jnp.where(j == (i % 32 // 2) * 16 + row, 1.0, 0.0).astype(BF16)
        both = jnp.dot(select, cells, preferred_element_type=F32).astype(BF16)
        compact[2 * k, pl.ds(16, 32), :] = both[:32]
        compact[2 * k + 1, pl.ds(16, 32), :] = both[32:]

    for copy in small:
        copy.wait()

    zero = jnp.zeros((64, 64), BF16)
    wt1[...] = jnp.zeros_like(wt1)
    for a in range(3):
        for b in range(3):
            w = w1[a, b]
            doubled = jnp.concatenate(
                [jnp.concatenate([w, zero], axis=1), jnp.concatenate([zero, w], axis=1)], axis=0
            )
            for n in range(2):
                wt1[pl.ds(a * 512 + (b + n) * 128, 128), pl.ds(n * 128, 128)] = doubled
            w = w2[a, b]
            wt2[pl.ds((a * 3 + b) * 128, 128), :] = jnp.concatenate(
                [jnp.concatenate([w, zero], axis=1), jnp.concatenate([zero, w], axis=1)], axis=0
            )
    bias_one = jnp.concatenate([b1[...]] * 4, axis=1)
    bias_two = jnp.concatenate([b2[...]] * 2, axis=1)

    def tile(t, v):
        ti = 2 * r - 1 + t
        tj = c + v
        ok = (ti >= 0) & (ti < 2 * n_row) & (tj >= 0) & (tj < n_col)
        value = mask[jnp.clip(ti, 0, 2 * n_row - 1), jnp.clip(tj, 0, n_col - 1)]
        return jnp.where(ok, value, 0).astype(F32)

    mt = [[tile(t, v) for v in (0, -1, 1)] for t in range(4)]

    def by_row(rows, v):
        return jnp.where(
            rows < 0, mt[0][v], jnp.where(rows < 64, mt[1][v], jnp.where(rows < 128, mt[2][v], mt[3][v]))
        )

    i = lax.broadcasted_iota(jnp.int32, (112, 128), 0)
    j = lax.broadcasted_iota(jnp.int32, (112, 128), 1)
    lower = j // 64
    pair_at = j % 32 // 2 * 2 + j // 32 % 2
    by_column = (lower == i // 32) & (pair_at == i % 32) & (pair_at > 0) & (pair_at < PAIRS - 1)
    kind = (i - 64) // 16
    in_kind = ((kind == 0) & (pair_at >= 2) & (pair_at < PAIRS - 2)) | (
        (kind > 0) & (pair_at == jnp.where(kind == 1, 1, PAIRS - 2))
    )
    by_line = in_kind & (lower == (i // 8) % 2) & (j % 2 + 6 * lower == i % 8)
    gather[...] = jnp.where(((i < 64) & by_column) | ((i >= 64) & by_line), 1.0, 0.0).astype(BF16)

    def expand(buffer, k):
        window = buffer[k]
        return jnp.concatenate([window[14:46, 128:], window[16:48], window[18:50, :128]], axis=1)

    for k in range(2):
        lhs = jnp.concatenate([expand(compact, 2 * k), expand(compact, 2 * k + 1)], axis=1)
        edge_pre[k] = (
            jnp.dot(lhs, wt1[pl.ds(512 * (1 - k), 1024), :], preferred_element_type=F32) + bias_one
        )

    loads[2].wait()
    beside = has_up.astype(jnp.int32) + has_down.astype(jnp.int32)
    corners = beside * (has_left.astype(jnp.int32) + has_right.astype(jnp.int32))
    pl.semaphore_wait(barrier, (n_col - 1) + beside + len(near) + corners)
    copies = []
    for k in (0, 1, 4, 5, 6, 7, 2, 3):
        present, tr, tc, src, dst = halos[k]
        copy = pltpu.make_async_remote_copy(
            src_ref=src, dst_ref=dst, send_sem=halo_send.at[k], recv_sem=halo_recv.at[k],
            device_id=(tr, tc), device_id_type=MESH,
        )
        copies.append((present, k, copy))

        @pl.when(present)
        def _():
            copy.start()

    for present, tr, tc, _, _ in halos[:2]:
        @pl.when(present)
        def _():
            greet(known, tr, tc)

    for tr in near:
        greet(known, tr, c)

    def fold(parts):
        both = functools.reduce(jnp.add, parts)
        return both[:, :128] + both[:, 128:]

    def split(values):
        high_part = values.astype(BF16)
        return jnp.concatenate([high_part, (values - high_part.astype(F32)).astype(BF16)], axis=0)

    def rows_of(k):
        r0 = pl.multiple_of(16 * k, 16)
        window = xe[pl.ds(r0, 48), :]
        xm[...] = window[14:30]
        xp[...] = window[18:34]
        lhs = []
        for g in range(GROUPS):
            lanes = pl.ds(g * 256, 512)
            lhs.append(jnp.concatenate([xm[:, lanes], xe[pl.ds(EDGE + r0, 16), lanes], xp[:, lanes]], axis=1))
        pre = jnp.dot(jnp.concatenate(lhs, axis=0), wt1[...], preferred_element_type=F32) + bias_one
        side_pre[0, pl.ds(r0, 16), :] = pre[:16, :128]
        side_pre[1, pl.ds(r0, 16), :] = pre[-16:, 128:]
        h = elu(pre)
        parts = [h[16 * g : 16 * g + 16] for g in range(GROUPS)]
        for g, piece in enumerate(parts):
            hb[pl.ds(r0, 16), pl.ds(g * 256, 256)] = piece.astype(BF16)
        at_row = r0 + lax.broadcasted_iota(jnp.int32, (16, 128), 0)
        final = (at_row >= 2) & (at_row < ROWS - 2)
        for n, value in enumerate((parts[0][:, 128:], fold(parts[1:-1]), parts[-1][:, :128])):
            hs[n, pl.ds(r0, 16), :] = jnp.where(final, value, 0.0)
        cells = xe[pl.ds(EDGE + r0, 16), pl.ds(OWN, LANES)].astype(F32)
        xs[pl.ds(r0, 16), :] = functools.reduce(
            jnp.add, [cells[:, p * 128 : (p + 1) * 128] for p in range(PAIRS)]
        )

    pl.loop(0, SPLIT)(rows_of)

    pl.semaphore_wait(known, len(near) + beside)
    odd = lax.rem(c, 2)
    owner_row, edge_row = c // 2, c // 2 - 1 + 2 * odd
    edge_exists = (edge_row >= 0) & (edge_row < n_row)

    for n, tells in ((0, r == owner_row), (1, edge_exists & (r == edge_row))):
        @pl.when(tells)
        def _():
            for k in range(1, n_row):
                greet(ready.at[n], lax.rem(r + k, n_row), c)

    pl.loop(SPLIT, ROWS // 16)(rows_of)

    combos = [(a, v) for a in range(3) for v in range(3)]
    at = lax.broadcasted_iota(jnp.int32, (16, 128), 1)
    which = lax.broadcasted_iota(jnp.int32, (16, 128), 0)
    own_at = by_row(at, 0)
    pick = jnp.zeros((16, 128), F32)
    for k, (a, v) in enumerate(combos):
        pick = jnp.where(which == k, by_row(at - 4 * (a - 1), v), pick)
    pick = pick * own_at
    inside = jnp.where((at >= 2) & (at < ROWS - 2), pick, 0.0)
    weights = jnp.concatenate([inside, jnp.where(which == 9, own_at, 0.0)], axis=1).astype(BF16)
    pick = pick.astype(BF16)
    for g in range(GROUPS):
        cells = jnp.concatenate(
            [hb[:, pl.ds(g * 256, 256)], xe[pl.ds(EDGE, ROWS), pl.ds(OWN + g * 256, 256)]], axis=0
        )
        sums = jnp.dot(weights, cells, preferred_element_type=F32)
        csum[pl.ds(g * 32, 16), :] = sums[:, :128]
        csum[pl.ds(g * 32 + 16, 16), :] = sums[:, 128:]
    cacc[...] = jnp.zeros_like(cacc)
    cacc[pl.ds(8, PAIRS), :] = csum[pl.ds(9, PAIRS, stride=16), :] + bias_two * (
        64.0 * (mt[1][0] + mt[2][0])
    )

    sender = (has_down, has_up, has_right, has_left, has_down & has_right, has_down & has_left,
              has_up & has_right, has_up & has_left)
    for _, k, copy in copies:
        @pl.when(sender[k])
        def _():
            copy.wait_recv()

    edges = []
    for k in range(2):
        edges.append(jnp.dot(expand(landed, k), wt1[pl.ds(1024 * k, 512), :], preferred_element_type=F32))
    line = lax.broadcasted_iota(jnp.int32, (8, 128), 0)
    flat = []
    for k in range(2):
        window = side[k]
        lhs = jnp.concatenate([window[14:142], window[16:144], window[18:146]], axis=1)
        taps = jnp.concatenate([wt1[pl.ds(a * 512 + 256 * k, 128), pl.ds(0, 128)] for a in range(3)], axis=0)
        term = jnp.dot(lhs, taps, preferred_element_type=F32)
        value = side_pre[k] + term
        if k == 0:
            head, tail = edges[0][:8, :128], pltpu.roll(edges[1][:8, :128], 6, 0)
        else:
            head, tail = pltpu.roll(edges[0][24:, 128:], 2, 0), edges[1][24:, 128:]
        value = jnp.concatenate(
            [
                value[:8] + jnp.where(line < 2, head, 0.0),
                value[8:120],
                value[120:] + jnp.where(line >= 6, tail, 0.0),
            ],
            axis=0,
        )
        flat.append(elu(value))
    sums = jnp.dot(
        pick, jnp.concatenate([v.astype(BF16) for v in flat], axis=1), preferred_element_type=F32
    )
    csum[pl.ds(0, 16), :] = sums[:, :128]
    csum[pl.ds(16 * (PAIRS - 1), 16), :] = sums[:, 128:]
    edges = [elu(edge_pre[k] + edges[k]).astype(BF16) for k in range(2)]
    cells = jnp.concatenate([edges[0][:, :128], edges[0][:, 128:], edges[1][:, :128], edges[1][:, 128:]], axis=0)
    found = jnp.dot(gather[...], cells, preferred_element_type=F32)

    def column(a, v):
        upper = mt[1][0] * (mt[0][v] if a == 2 else mt[1][v])
        under = mt[2][0] * (mt[3][v] if a == 0 else mt[2][v])
        return csum[pl.ds(3 * a + v, PAIRS, stride=16), :] + upper * found[:32] + under * found[32:64]

    at_pair = lax.broadcasted_iota(jnp.int32, (PAIRS, 128), 0)
    for b in range(3):
        pieces = []
        for a in range(3):
            value = column(a, 0)
            if b == 0:
                value = jnp.where(at_pair >= PAIRS - 2, column(a, 2), value)
            if b == 2:
                value = jnp.where(at_pair < 2, column(a, 1), value)
            pieces.append(value)
        weights = jnp.concatenate([wt2[pl.ds((a * 3 + b) * 128, 128), :] for a in range(3)], axis=0)
        both = jnp.dot(split(jnp.concatenate(pieces, axis=1)), weights, preferred_element_type=F32)
        cacc[pl.ds(8 - 2 * (b - 1), PAIRS), :] += both[:PAIRS] + both[PAIRS:]
    columns = cacc[pl.ds(4, 40), :]
    for k in range(10):
        csend[k] = columns[4 * k : 4 * k + 4]

    def post(src, dst, send_sem, recv_sem, tr, tc):
        mine = (tr == r) & (tc == c)

        @pl.when(mine)
        def _():
            pltpu.make_async_copy(src, dst, recv_sem).start()

        @pl.when(jnp.logical_not(mine))
        def _():
            pltpu.make_async_remote_copy(
                src_ref=src, dst_ref=dst, send_sem=send_sem, recv_sem=recv_sem, device_id=(tr, tc),
                device_id_type=MESH,
            ).start()

    def col_target(k):
        target = lax.rem(8 * c - 1 + k + n_all, n_all)
        return target // n_col, lax.rem(target, n_col)

    for k, told in ((0, r != owner_row), (1, edge_exists & (r != edge_row))):
        @pl.when(told)
        def _():
            pl.semaphore_wait(ready.at[k], 1)

    for k in range(1, 9):
        post(csend.at[k], crecv.at[r], col_send.at[k], col_recv.at[r], *col_target(k))
    for k, present in ((0, has_left), (9, has_right)):
        @pl.when(present)
        def _():
            post(
                csend.at[k], crecv.at[n_row + r], col_send.at[k], col_recv.at[n_row + r], *col_target(k)
            )

    for k in range(2):
        hs[2 * k] += flat[k]
    for k, n in enumerate((1, 0, 2)):
        hs[n, pl.ds(0, 8), :] += found[64 + 16 * k : 72 + 16 * k]
        hs[n, pl.ds(ROWS - 8, 8), :] += found[72 + 16 * k : 80 + 16 * k]
    rows = lax.broadcasted_iota(jnp.int32, (ROWS, 128), 0)
    own = by_row(rows, 0)
    sum_l, sum_m, sum_r = (hs[k] * own for k in range(3))
    racc[...] = jnp.zeros_like(racc)
    racc[pl.ds(8, ROWS), :] = (xs[...] + 32.0 * bias_two) * own
    for a in range(3):
        out_rows = rows - 4 * (a - 1)
        m0, ml, mr = (by_row(out_rows, v) for v in range(3))
        lhs = split(
            jnp.concatenate(
                [
                    m0 * (sum_l + sum_m) + mr * sum_r,
                    m0 * (sum_l + sum_m + sum_r),
                    m0 * (sum_m + sum_r) + ml * sum_l,
                ],
                axis=1,
            )
        )
        both = jnp.dot(lhs, wt2[pl.ds(a * 384, 384), :], preferred_element_type=F32)
        racc[pl.ds(8 - 4 * (a - 1), ROWS), :] += both[:ROWS] + both[ROWS:]
    racc[...] = racc[...] + pltpu.roll(racc[...], 64, 1)
    half = lax.broadcasted_iota(jnp.int32, (72, 128), 1) < 64
    paired = jnp.where(half, racc[pl.ds(0, 72, stride=2), :], racc[pl.ds(1, 72, stride=2), :])
    for k in range(18):
        rsend[k] = paired[4 * k : 4 * k + 4]


    rrecv[c] = rsend[c + 1]
    for k in range(n_col):
        @pl.when(c != k)
        def _():
            pltpu.make_async_remote_copy(
                src_ref=rsend.at[k + 1], dst_ref=rrecv.at[c], send_sem=row_send.at[k + 1],
                recv_sem=row_recv.at[c], device_id=(r, k), device_id_type=MESH,
            ).start()


    for k, present, tr, tc in ((0, has_up, up, n_col - 1), (17, has_down, down, 0)):
        @pl.when(present)
        def _():
            pltpu.make_async_remote_copy(
                src_ref=rsend.at[k], dst_ref=rrecv.at[n_col + c], send_sem=row_send.at[k],
                recv_sem=row_recv.at[n_col + c], device_id=(tr, tc), device_id_type=MESH,
            ).start()

    def arrived(buffer, sem, slot):
        pltpu.make_async_copy(buffer.at[slot], buffer.at[slot], sem.at[slot]).wait()

    for k in range(1, n_col):
        arrived(rrecv, row_recv, lax.rem(c + k, n_col))

    @pl.when(row_edge)
    def _():
        for k in range(n_col):
            arrived(rrecv, row_recv, n_col + k)

    for k in range(n_row):
        arrived(crecv, col_recv, k)

    @pl.when(col_edge)
    def _():
        for k in range(n_row):
            arrived(crecv, col_recv, n_row + k)

    sums = jnp.sum(rrecv[...], axis=0) + jnp.sum(crecv[...], axis=0)
    res[pl.ds(0, 4, stride=2), :] = sums
    res[pl.ds(1, 4, stride=2), :] = pltpu.roll(sums, 64, 1)
    pooled = res[:, :64]
    center = jnp.mean(pooled, axis=1, keepdims=True)
    spread = jnp.mean((pooled - center) ** 2, axis=1, keepdims=True)
    normed = ((pooled - center) / jnp.sqrt(spread + EPSILON) * gain[...]).astype(BF16)
    out[...] = jnp.dot(normed, wp[...], preferred_element_type=F32).astype(BF16)

    for present, _, copy in copies:
        @pl.when(present)
        def _():
            copy.wait_send()

    for k in range(18):
        @pl.when(has_up if k == 0 else has_down if k == 17 else c != k - 1)
        def _():
            pltpu.make_async_copy(rsend.at[k], rsend.at[k], row_send.at[k]).wait()

    for k in range(10):
        tr, tc = col_target(k)

        @pl.when((has_left if k == 0 else has_right if k == 9 else r >= 0) & ((tr != r) | (tc != c)))
        def _():
            pltpu.make_async_copy(csend.at[k], csend.at[k], col_send.at[k]).wait()


def body(pair, tile_mask, w_first, b_first, w_second, b_second, norm_gain, w_proj):
    n_row, n_col = lax.axis_size("row"), lax.axis_size("col")
    hbm = pl.BlockSpec(memory_space=pltpu.HBM)
    return pl.pallas_call(
        functools.partial(kernel, n_row, n_col),
        out_shape=pltpu.VMEM((8, w_proj.shape[1]), BF16),
        in_specs=[hbm] * 8,
        out_specs=pl.BlockSpec(memory_space=pltpu.VMEM),
        scratch_shapes=[
            pltpu.SMEM(tile_mask.shape, jnp.int32),
            pltpu.VMEM(w_first.shape, BF16),
            pltpu.VMEM((1, 64), F32),
            pltpu.VMEM(w_second.shape, BF16),
            pltpu.VMEM((1, 64), F32),
            pltpu.VMEM((1, 64), F32),
            pltpu.VMEM(w_proj.shape, BF16),
            pltpu.VMEM((ROWS + 2 * EDGE, LANES + 256), BF16),
            pltpu.VMEM((16, LANES + 256), BF16),
            pltpu.VMEM((16, LANES + 256), BF16),
            pltpu.VMEM((ROWS, LANES), BF16),
            pltpu.VMEM((1536, 256), BF16),
            pltpu.VMEM((1152, 128), BF16),
            pltpu.VMEM((3, ROWS, 128), F32),
            pltpu.VMEM((ROWS, 128), F32),
            pltpu.VMEM((144, 128), F32),
            pltpu.VMEM((48, 128), F32),
            pltpu.VMEM((512, 128), F32),
            pltpu.VMEM((4, 64, 256), BF16),
            pltpu.VMEM((2, 64, 256), BF16),
            pltpu.VMEM((2, ROWS + 2 * EDGE, 128), BF16),
            pltpu.VMEM((2, ROWS, 128), F32),
            pltpu.VMEM((2, 32, 256), F32),
            pltpu.VMEM((112, 128), BF16),
            pltpu.VMEM((18, 4, 128), F32),
            pltpu.VMEM((10, 4, 128), F32),
            pltpu.VMEM((32, 4, 128), F32),
            pltpu.VMEM((16, 4, 128), F32),
            pltpu.VMEM((8, 128), F32),
            pltpu.SemaphoreType.REGULAR((2,)),
            pltpu.SemaphoreType.REGULAR,
            pltpu.SemaphoreType.DMA((3,)),
            pltpu.SemaphoreType.DMA((7,)),
            pltpu.SemaphoreType.DMA((8,)),
            pltpu.SemaphoreType.DMA((8,)),
            pltpu.SemaphoreType.DMA((18,)),
            pltpu.SemaphoreType.DMA((32,)),
            pltpu.SemaphoreType.DMA((10,)),
            pltpu.SemaphoreType.DMA((16,)),
        ],
        compiler_params=pltpu.CompilerParams(
            collective_id=0, has_side_effects=True, vmem_limit_bytes=48 * 1024 * 1024
        ),
        name="block",
    )(
        *(pltpu.with_memory_space_constraint(v, pltpu.HBM) for v in (
        pair, tile_mask, w_first, b_first.reshape(1, -1), w_second, b_second.reshape(1, -1),
        norm_gain.reshape(1, -1), w_proj,
    )))


def solution(mesh):
    return jax.shard_map(
        body,
        mesh=mesh,
        in_specs=(P("row", "col"), P(), P(), P(), P(), P(), P(), P()),
        out_specs=P(("row", "col"), None),
        check_vma=False,
    )
```

```python
import functools

import jax
import jax.numpy as jnp
from jax import lax
from jax.experimental import pallas as pl
from jax.experimental.pallas import tpu as pltpu
from jax.sharding import PartitionSpec as P

TILE = 64
EPSILON = 1e-05
MESH = pl.DeviceIdType.MESH
F32 = jnp.float32
BF16 = jnp.bfloat16

ROWS = 128
PAIRS = 32
EDGE = 16
GROUPS = 16
OWN = 128
LANES = PAIRS * 128
SPLIT = 4


def elu(v):
    return jnp.where(v > 0, v, jnp.exp(jnp.minimum(v, 0.0)) - 1.0)


def kernel(
    n_row, n_col,
    pair, mask_in, w1_in, b1_in, w2_in, b2_in, gain_in, wp_in,
    out,
    mask, w1, b1, w2, b2, gain, wp, xe, xm, xp, hb, wt1, wt2, hs, xs, racc, cacc, csum, compact, landed, side, side_pre, edge_pre, gather, rsend, csend, rrecv, crecv, res,
    ready, known, load_sem, small_sem, halo_send, halo_recv, row_send, row_recv, col_send, col_recv,
):
    r = lax.axis_index("row")
    c = lax.axis_index("col")
    me = r * n_col + c
    n_all = n_row * n_col

    loads = [
        pltpu.make_async_copy(
            pair.at[pl.ds(start, size)], xe.at[pl.ds(EDGE + start, size), pl.ds(OWN, LANES)], load_sem.at[k]
        )
        for k, (start, size) in enumerate(((0, EDGE), (ROWS - EDGE, EDGE), (EDGE, ROWS - 2 * EDGE)))
    ]
    small = [(mask_in, mask), (w1_in, w1), (w2_in, w2), (b1_in, b1), (b2_in, b2), (gain_in, gain), (wp_in, wp)]
    small = [
        pltpu.make_async_copy(src, dst, small_sem.at[k]) for k, (src, dst) in enumerate(small)
    ]
    barrier = pltpu.get_barrier_semaphore()

    def greet(semaphore, tr, tc):
        pl.semaphore_signal(semaphore, inc=1, device_id=(tr, tc), device_id_type=MESH)

    up, down = lax.rem(r + n_row - 1, n_row), lax.rem(r + 1, n_row)
    left, right = lax.rem(c + n_col - 1, n_col), lax.rem(c + 1, n_col)
    above, below, whole = pl.ds(0, EDGE), pl.ds(EDGE + ROWS, EDGE), pl.ds(EDGE, ROWS)
    before, after = pl.ds(0, 128), pl.ds(OWN + LANES, 128)
    first, last = pl.ds(OWN, 128), pl.ds(OWN + LANES - 128, 128)
    top, bottom = pl.ds(EDGE, EDGE), pl.ds(ROWS, EDGE)
    inner, low, high = pl.ds(EDGE, ROWS), pl.ds(0, EDGE), pl.ds(EDGE + ROWS, EDGE)
    has_up, has_down, has_left, has_right = r > 0, r < n_row - 1, c > 0, c < n_col - 1
    halos = [
        (has_up, up, c, compact.at[0, pl.ds(16, 32)], landed.at[1, pl.ds(16, 32)]),
        (has_down, down, c, compact.at[3, pl.ds(16, 32)], landed.at[0, pl.ds(16, 32)]),
        (has_left, r, left, xe.at[whole, first], side.at[1, inner]),
        (has_right, r, right, xe.at[whole, last], side.at[0, inner]),
        (has_up & has_left, up, left, xe.at[top, first], side.at[1, high]),
        (has_up & has_right, up, right, xe.at[top, last], side.at[0, high]),
        (has_down & has_left, down, left, xe.at[bottom, first], side.at[1, low]),
        (has_down & has_right, down, right, xe.at[bottom, last], side.at[0, low]),
    ]
    near = (lax.rem(r + 2, n_row), lax.rem(r + n_row - 2, n_row))
    for present, tr, tc, _, _ in halos[:2] + halos[4:]:
        @pl.when(present)
        def _():
            greet(barrier, tr, tc)

    for k in (8, 7, 9, 6, 10, 5, 11, 4, 12, 3, 13, 2, 14, 1, 15):
        greet(barrier, r, lax.rem(c + k, n_col))
    for tr in near:
        greet(barrier, tr, c)
    for copy in loads + small:
        copy.start()
    part = lax.rem(me, 8)

    xe[above, :] = jnp.zeros((EDGE, xe.shape[1]), BF16)
    xe[below, :] = jnp.zeros((EDGE, xe.shape[1]), BF16)
    xe[whole, before] = jnp.zeros((ROWS, 128), BF16)
    xe[whole, after] = jnp.zeros((ROWS, 128), BF16)
    for k in range(2):
        landed[k, pl.ds(0, 16), :] = jnp.zeros((16, 256), BF16)
        landed[k, pl.ds(48, 16), :] = jnp.zeros((16, 256), BF16)
    for k in range(4):
        compact[k, pl.ds(0, 16), :] = jnp.zeros((16, 256), BF16)
        compact[k, pl.ds(48, 16), :] = jnp.zeros((16, 256), BF16)

    for k, present, place in ((0, has_up, low), (1, has_down, high)):
        @pl.when(jnp.logical_not(present))
        def _():
            landed[k, pl.ds(16, 32), :] = jnp.zeros((32, 256), BF16)
            side[:, place] = jnp.zeros((2, EDGE, 128), BF16)

    for k, present in ((0, has_left), (1, has_right)):
        @pl.when(jnp.logical_not(present))
        def _():
            side[k] = jnp.zeros((ROWS + 2 * EDGE, 128), BF16)

    row_edge = ((c == 0) & has_up) | ((c == n_col - 1) & has_down)
    col_edge = ((part == 0) & (me > 0)) | ((part == 7) & (me < n_all - 1))

    @pl.when(jnp.logical_not(row_edge))
    def _():
        rrecv[pl.ds(n_col, n_col)] = jnp.zeros((n_col, 4, 128), F32)

    @pl.when(jnp.logical_not(col_edge))
    def _():
        crecv[pl.ds(n_row, n_row)] = jnp.zeros((n_row, 4, 128), F32)

    i = lax.broadcasted_iota(jnp.int32, (64, 256), 0)
    j = lax.broadcasted_iota(jnp.int32, (64, 256), 1)
    for k in range(2):
        loads[k].wait()
        cells = jnp.concatenate(
            [xe[pl.ds(EDGE + (ROWS - EDGE) * k, EDGE), pl.ds(OWN + 256 * g, 256)] for g in range(GROUPS)], axis=0
        )
        row = (EDGE - 4) * k + (i // 32) * 2 + i % 2
        select = jnp.where(j == (i % 32 // 2) * 16 + row, 1.0, 0.0).astype(BF16)
        both = jnp.dot(select, cells, preferred_element_type=F32).astype(BF16)
        compact[2 * k, pl.ds(16, 32), :] = both[:32]
        compact[2 * k + 1, pl.ds(16, 32), :] = both[32:]

    for copy in small:
        copy.wait()

    zero = jnp.zeros((64, 64), BF16)
    wt1[...] = jnp.zeros_like(wt1)
    for a in range(3):
        for b in range(3):
            w = w1[a, b]
            doubled = jnp.concatenate(
                [jnp.concatenate([w, zero], axis=1), jnp.concatenate([zero, w], axis=1)], axis=0
            )
            for n in range(2):
                wt1[pl.ds(a * 512 + (b + n) * 128, 128), pl.ds(n * 128, 128)] = doubled
            w = w2[a, b]
            wt2[pl.ds((a * 3 + b) * 128, 128), :] = jnp.concatenate(
                [jnp.concatenate([w, zero], axis=1), jnp.concatenate([zero, w], axis=1)], axis=0
            )
    bias_one = jnp.concatenate([b1[...]] * 4, axis=1)
    bias_two = jnp.concatenate([b2[...]] * 2, axis=1)

    def tile(t, v):
        ti = 2 * r - 1 + t
        tj = c + v
        ok = (ti >= 0) & (ti < 2 * n_row) & (tj >= 0) & (tj < n_col)
        value = mask[jnp.clip(ti, 0, 2 * n_row - 1), jnp.clip(tj, 0, n_col - 1)]
        return jnp.where(ok, value, 0).astype(F32)

    mt = [[tile(t, v) for v in (0, -1, 1)] for t in range(4)]

    def by_row(rows, v):
        return jnp.where(
            rows < 0, mt[0][v], jnp.where(rows < 64, mt[1][v], jnp.where(rows < 128, mt[2][v], mt[3][v]))
        )

    i = lax.broadcasted_iota(jnp.int32, (112, 128), 0)
    j = lax.broadcasted_iota(jnp.int32, (112, 128), 1)
    lower = j // 64
    pair_at = j % 32 // 2 * 2 + j // 32 % 2
    by_column = (lower == i // 32) & (pair_at == i % 32) & (pair_at > 0) & (pair_at < PAIRS - 1)
    kind = (i - 64) // 16
    in_kind = ((kind == 0) & (pair_at >= 2) & (pair_at < PAIRS - 2)) | (
        (kind > 0) & (pair_at == jnp.where(kind == 1, 1, PAIRS - 2))
    )
    by_line = in_kind & (lower == (i // 8) % 2) & (j % 2 + 6 * lower == i % 8)
    gather[...] = jnp.where(((i < 64) & by_column) | ((i >= 64) & by_line), 1.0, 0.0).astype(BF16)

    def expand(buffer, k):
        window = buffer[k]
        return jnp.concatenate([window[14:46, 128:], window[16:48], window[18:50, :128]], axis=1)

    for k in range(2):
        lhs = jnp.concatenate([expand(compact, 2 * k), expand(compact, 2 * k + 1)], axis=1)
        edge_pre[k] = (
            jnp.dot(lhs, wt1[pl.ds(512 * (1 - k), 1024), :], preferred_element_type=F32) + bias_one
        )

    loads[2].wait()

    @pl.loop(0, ROWS // 16)
    def _(k):
        r0 = pl.multiple_of(16 * k, 16)
        cells = xe[pl.ds(EDGE + r0, 16), pl.ds(OWN, LANES)].astype(F32)
        xs[pl.ds(r0, 16), :] = functools.reduce(
            jnp.add, [cells[:, p * 128 : (p + 1) * 128] for p in range(PAIRS)]
        )

    beside = has_up.astype(jnp.int32) + has_down.astype(jnp.int32)
    corners = beside * (has_left.astype(jnp.int32) + has_right.astype(jnp.int32))
    pl.semaphore_wait(barrier, (n_col - 1) + beside + len(near) + corners)
    copies = []
    for k in (0, 1, 4, 5, 6, 7, 2, 3):
        present, tr, tc, src, dst = halos[k]
        copy = pltpu.make_async_remote_copy(
            src_ref=src, dst_ref=dst, send_sem=halo_send.at[k], recv_sem=halo_recv.at[k],
            device_id=(tr, tc), device_id_type=MESH,
        )
        copies.append((present, k, copy))

        @pl.when(present)
        def _():
            copy.start()

    for present, tr, tc, _, _ in halos[:2]:
        @pl.when(present)
        def _():
            greet(known, tr, tc)

    for tr in near:
        greet(known, tr, c)

    def fold(parts):
        both = functools.reduce(jnp.add, parts)
        return both[:, :128] + both[:, 128:]

    def split(values):
        high_part = values.astype(BF16)
        return jnp.concatenate([high_part, (values - high_part.astype(F32)).astype(BF16)], axis=0)

    def rows_of(k):
        r0 = pl.multiple_of(16 * k, 16)
        window = xe[pl.ds(r0, 48), :]
        xm[...] = window[14:30]
        xp[...] = window[18:34]
        lhs = []
        for g in range(GROUPS):
            lanes = pl.ds(g * 256, 512)
            lhs.append(jnp.concatenate([xm[:, lanes], xe[pl.ds(EDGE + r0, 16), lanes], xp[:, lanes]], axis=1))
        pre = jnp.dot(jnp.concatenate(lhs, axis=0), wt1[...], preferred_element_type=F32) + bias_one
        side_pre[0, pl.ds(r0, 16), :] = pre[:16, :128]
        side_pre[1, pl.ds(r0, 16), :] = pre[-16:, 128:]
        h = elu(pre)
        parts = [h[16 * g : 16 * g + 16] for g in range(GROUPS)]
        for g, piece in enumerate(parts):
            hb[pl.ds(r0, 16), pl.ds(g * 256, 256)] = piece.astype(BF16)
        at_row = r0 + lax.broadcasted_iota(jnp.int32, (16, 128), 0)
        final = (at_row >= 2) & (at_row < ROWS - 2)
        for n, value in enumerate((parts[0][:, 128:], fold(parts[1:-1]), parts[-1][:, :128])):
            hs[n, pl.ds(r0, 16), :] = jnp.where(final, value, 0.0)

    pl.loop(0, SPLIT)(rows_of)

    pl.semaphore_wait(known, len(near) + beside)
    odd = lax.rem(c, 2)
    owner_row, edge_row = c // 2, c // 2 - 1 + 2 * odd
    edge_exists = (edge_row >= 0) & (edge_row < n_row)

    for n, tells in ((0, r == owner_row), (1, edge_exists & (r == edge_row))):
        @pl.when(tells)
        def _():
            for k in range(1, n_row):
                greet(ready.at[n], lax.rem(r + k, n_row), c)

    pl.loop(SPLIT, ROWS // 16)(rows_of)

    combos = [(a, v) for a in range(3) for v in range(3)]
    at = lax.broadcasted_iota(jnp.int32, (16, 128), 1)
    which = lax.broadcasted_iota(jnp.int32, (16, 128), 0)
    own_at = by_row(at, 0)
    pick = jnp.zeros((16, 128), F32)
    for k, (a, v) in enumerate(combos):
        pick = jnp.where(which == k, by_row(at - 4 * (a - 1), v), pick)
    pick = pick * own_at
    inside = jnp.where((at >= 2) & (at < ROWS - 2), pick, 0.0)
    weights = jnp.concatenate([inside, jnp.where(which == 9, own_at, 0.0)], axis=1).astype(BF16)
    pick = pick.astype(BF16)
    for g in range(GROUPS):
        cells = jnp.concatenate(
            [hb[:, pl.ds(g * 256, 256)], xe[pl.ds(EDGE, ROWS), pl.ds(OWN + g * 256, 256)]], axis=0
        )
        sums = jnp.dot(weights, cells, preferred_element_type=F32)
        csum[pl.ds(g * 32, 16), :] = sums[:, :128]
        csum[pl.ds(g * 32 + 16, 16), :] = sums[:, 128:]
    cacc[...] = jnp.zeros_like(cacc)
    cacc[pl.ds(8, PAIRS), :] = csum[pl.ds(9, PAIRS, stride=16), :] + bias_two * (
        64.0 * (mt[1][0] + mt[2][0])
    )

    sender = (has_down, has_up, has_right, has_left, has_down & has_right, has_down & has_left,
              has_up & has_right, has_up & has_left)
    for _, k, copy in copies:
        @pl.when(sender[k])
        def _():
            copy.wait_recv()

    edges = []
    for k in range(2):
        edges.append(jnp.dot(expand(landed, k), wt1[pl.ds(1024 * k, 512), :], preferred_element_type=F32))
    line = lax.broadcasted_iota(jnp.int32, (8, 128), 0)
    flat = []
    for k in range(2):
        window = side[k]
        lhs = jnp.concatenate([window[14:142], window[16:144], window[18:146]], axis=1)
        taps = jnp.concatenate([wt1[pl.ds(a * 512 + 256 * k, 128), pl.ds(0, 128)] for a in range(3)], axis=0)
        term = jnp.dot(lhs, taps, preferred_element_type=F32)
        value = side_pre[k] + term
        if k == 0:
            head, tail = edges[0][:8, :128], pltpu.roll(edges[1][:8, :128], 6, 0)
        else:
            head, tail = pltpu.roll(edges[0][24:, 128:], 2, 0), edges[1][24:, 128:]
        value = jnp.concatenate(
            [
                value[:8] + jnp.where(line < 2, head, 0.0),
                value[8:120],
                value[120:] + jnp.where(line >= 6, tail, 0.0),
            ],
            axis=0,
        )
        flat.append(elu(value))
    sums = jnp.dot(
        pick, jnp.concatenate([v.astype(BF16) for v in flat], axis=1), preferred_element_type=F32
    )
    csum[pl.ds(0, 16), :] = sums[:, :128]
    csum[pl.ds(16 * (PAIRS - 1), 16), :] = sums[:, 128:]
    edges = [elu(edge_pre[k] + edges[k]).astype(BF16) for k in range(2)]
    cells = jnp.concatenate([edges[0][:, :128], edges[0][:, 128:], edges[1][:, :128], edges[1][:, 128:]], axis=0)
    found = jnp.dot(gather[...], cells, preferred_element_type=F32)

    def column(a, v):
        upper = mt[1][0] * (mt[0][v] if a == 2 else mt[1][v])
        under = mt[2][0] * (mt[3][v] if a == 0 else mt[2][v])
        return csum[pl.ds(3 * a + v, PAIRS, stride=16), :] + upper * found[:32] + under * found[32:64]

    at_pair = lax.broadcasted_iota(jnp.int32, (PAIRS, 128), 0)
    for b in range(3):
        pieces = []
        for a in range(3):
            value = column(a, 0)
            if b == 0:
                value = jnp.where(at_pair >= PAIRS - 2, column(a, 2), value)
            if b == 2:
                value = jnp.where(at_pair < 2, column(a, 1), value)
            pieces.append(value)
        weights = jnp.concatenate([wt2[pl.ds((a * 3 + b) * 128, 128), :] for a in range(3)], axis=0)
        both = jnp.dot(split(jnp.concatenate(pieces, axis=1)), weights, preferred_element_type=F32)
        cacc[pl.ds(8 - 2 * (b - 1), PAIRS), :] += both[:PAIRS] + both[PAIRS:]
    columns = cacc[pl.ds(4, 40), :]
    for k in range(10):
        csend[k] = columns[4 * k : 4 * k + 4]

    def post(src, dst, send_sem, recv_sem, tr, tc):
        mine = (tr == r) & (tc == c)

        @pl.when(mine)
        def _():
            pltpu.make_async_copy(src, dst, recv_sem).start()

        @pl.when(jnp.logical_not(mine))
        def _():
            pltpu.make_async_remote_copy(
                src_ref=src, dst_ref=dst, send_sem=send_sem, recv_sem=recv_sem, device_id=(tr, tc),
                device_id_type=MESH,
            ).start()

    def col_target(k):
        target = lax.rem(8 * c - 1 + k + n_all, n_all)
        return target // n_col, lax.rem(target, n_col)

    for k, told in ((0, r != owner_row), (1, edge_exists & (r != edge_row))):
        @pl.when(told)
        def _():
            pl.semaphore_wait(ready.at[k], 1)

    for k in range(1, 9):
        post(csend.at[k], crecv.at[r], col_send.at[k], col_recv.at[r], *col_target(k))
    for k, present in ((0, has_left), (9, has_right)):
        @pl.when(present)
        def _():
            post(
                csend.at[k], crecv.at[n_row + r], col_send.at[k], col_recv.at[n_row + r], *col_target(k)
            )

    for k in range(2):
        hs[2 * k] += flat[k]
    for k, n in enumerate((1, 0, 2)):
        hs[n, pl.ds(0, 8), :] += found[64 + 16 * k : 72 + 16 * k]
        hs[n, pl.ds(ROWS - 8, 8), :] += found[72 + 16 * k : 80 + 16 * k]
    rows = lax.broadcasted_iota(jnp.int32, (ROWS, 128), 0)
    own = by_row(rows, 0)
    sum_l, sum_m, sum_r = (hs[k] * own for k in range(3))
    racc[...] = jnp.zeros_like(racc)
    racc[pl.ds(8, ROWS), :] = (xs[...] + 32.0 * bias_two) * own
    for a in range(3):
        out_rows = rows - 4 * (a - 1)
        m0, ml, mr = (by_row(out_rows, v) for v in range(3))
        lhs = split(
            jnp.concatenate(
                [
                    m0 * (sum_l + sum_m) + mr * sum_r,
                    m0 * (sum_l + sum_m + sum_r),
                    m0 * (sum_m + sum_r) + ml * sum_l,
                ],
                axis=1,
            )
        )
        both = jnp.dot(lhs, wt2[pl.ds(a * 384, 384), :], preferred_element_type=F32)
        racc[pl.ds(8 - 4 * (a - 1), ROWS), :] += both[:ROWS] + both[ROWS:]
    racc[...] = racc[...] + pltpu.roll(racc[...], 64, 1)
    half = lax.broadcasted_iota(jnp.int32, (72, 128), 1) < 64
    paired = jnp.where(half, racc[pl.ds(0, 72, stride=2), :], racc[pl.ds(1, 72, stride=2), :])
    for k in range(18):
        rsend[k] = paired[4 * k : 4 * k + 4]


    rrecv[c] = rsend[c + 1]
    for k in range(n_col):
        @pl.when(c != k)
        def _():
            pltpu.make_async_remote_copy(
                src_ref=rsend.at[k + 1], dst_ref=rrecv.at[c], send_sem=row_send.at[k + 1],
                recv_sem=row_recv.at[c], device_id=(r, k), device_id_type=MESH,
            ).start()


    for k, present, tr, tc in ((0, has_up, up, n_col - 1), (17, has_down, down, 0)):
        @pl.when(present)
        def _():
            pltpu.make_async_remote_copy(
                src_ref=rsend.at[k], dst_ref=rrecv.at[n_col + c], send_sem=row_send.at[k],
                recv_sem=row_recv.at[n_col + c], device_id=(tr, tc), device_id_type=MESH,
            ).start()

    def arrived(buffer, sem, slot):
        pltpu.make_async_copy(buffer.at[slot], buffer.at[slot], sem.at[slot]).wait()

    for k in range(1, n_col):
        arrived(rrecv, row_recv, lax.rem(c + k, n_col))

    @pl.when(row_edge)
    def _():
        for k in range(n_col):
            arrived(rrecv, row_recv, n_col + k)

    for k in range(n_row):
        arrived(crecv, col_recv, k)

    @pl.when(col_edge)
    def _():
        for k in range(n_row):
            arrived(crecv, col_recv, n_row + k)

    sums = jnp.sum(rrecv[...], axis=0) + jnp.sum(crecv[...], axis=0)
    res[pl.ds(0, 4, stride=2), :] = sums
    res[pl.ds(1, 4, stride=2), :] = pltpu.roll(sums, 64, 1)
    pooled = res[:, :64]
    center = jnp.mean(pooled, axis=1, keepdims=True)
    spread = jnp.mean((pooled - center) ** 2, axis=1, keepdims=True)
    normed = ((pooled - center) / jnp.sqrt(spread + EPSILON) * gain[...]).astype(BF16)
    out[...] = jnp.dot(normed, wp[...], preferred_element_type=F32).astype(BF16)

    for present, _, copy in copies:
        @pl.when(present)
        def _():
            copy.wait_send()

    for k in range(18):
        @pl.when(has_up if k == 0 else has_down if k == 17 else c != k - 1)
        def _():
            pltpu.make_async_copy(rsend.at[k], rsend.at[k], row_send.at[k]).wait()

    for k in range(10):
        tr, tc = col_target(k)

        @pl.when((has_left if k == 0 else has_right if k == 9 else r >= 0) & ((tr != r) | (tc != c)))
        def _():
            pltpu.make_async_copy(csend.at[k], csend.at[k], col_send.at[k]).wait()


def body(pair, tile_mask, w_first, b_first, w_second, b_second, norm_gain, w_proj):
    n_row, n_col = lax.axis_size("row"), lax.axis_size("col")
    hbm = pl.BlockSpec(memory_space=pltpu.HBM)
    return pl.pallas_call(
        functools.partial(kernel, n_row, n_col),
        out_shape=pltpu.VMEM((8, w_proj.shape[1]), BF16),
        in_specs=[hbm] * 8,
        out_specs=pl.BlockSpec(memory_space=pltpu.VMEM),
        scratch_shapes=[
            pltpu.SMEM(tile_mask.shape, jnp.int32),
            pltpu.VMEM(w_first.shape, BF16),
            pltpu.VMEM((1, 64), F32),
            pltpu.VMEM(w_second.shape, BF16),
            pltpu.VMEM((1, 64), F32),
            pltpu.VMEM((1, 64), F32),
            pltpu.VMEM(w_proj.shape, BF16),
            pltpu.VMEM((ROWS + 2 * EDGE, LANES + 256), BF16),
            pltpu.VMEM((16, LANES + 256), BF16),
            pltpu.VMEM((16, LANES + 256), BF16),
            pltpu.VMEM((ROWS, LANES), BF16),
            pltpu.VMEM((1536, 256), BF16),
            pltpu.VMEM((1152, 128), BF16),
            pltpu.VMEM((3, ROWS, 128), F32),
            pltpu.VMEM((ROWS, 128), F32),
            pltpu.VMEM((144, 128), F32),
            pltpu.VMEM((48, 128), F32),
            pltpu.VMEM((512, 128), F32),
            pltpu.VMEM((4, 64, 256), BF16),
            pltpu.VMEM((2, 64, 256), BF16),
            pltpu.VMEM((2, ROWS + 2 * EDGE, 128), BF16),
            pltpu.VMEM((2, ROWS, 128), F32),
            pltpu.VMEM((2, 32, 256), F32),
            pltpu.VMEM((112, 128), BF16),
            pltpu.VMEM((18, 4, 128), F32),
            pltpu.VMEM((10, 4, 128), F32),
            pltpu.VMEM((32, 4, 128), F32),
            pltpu.VMEM((16, 4, 128), F32),
            pltpu.VMEM((8, 128), F32),
            pltpu.SemaphoreType.REGULAR((2,)),
            pltpu.SemaphoreType.REGULAR,
            pltpu.SemaphoreType.DMA((3,)),
            pltpu.SemaphoreType.DMA((7,)),
            pltpu.SemaphoreType.DMA((8,)),
            pltpu.SemaphoreType.DMA((8,)),
            pltpu.SemaphoreType.DMA((18,)),
            pltpu.SemaphoreType.DMA((32,)),
            pltpu.SemaphoreType.DMA((10,)),
            pltpu.SemaphoreType.DMA((16,)),
        ],
        compiler_params=pltpu.CompilerParams(
            collective_id=0, has_side_effects=True, vmem_limit_bytes=48 * 1024 * 1024
        ),
        name="block",
    )(
        *(pltpu.with_memory_space_constraint(v, pltpu.HBM) for v in (
        pair, tile_mask, w_first, b_first.reshape(1, -1), w_second, b_second.reshape(1, -1),
        norm_gain.reshape(1, -1), w_proj,
    )))


def solution(mesh):
    return jax.shard_map(
        body,
        mesh=mesh,
        in_specs=(P("row", "col"), P(), P(), P(), P(), P(), P(), P()),
        out_specs=P(("row", "col"), None),
        check_vma=False,
    )
```

```python
import functools

import jax
import jax.numpy as jnp
from jax import lax
from jax.experimental import pallas as pl
from jax.experimental.pallas import tpu as pltpu
from jax.sharding import PartitionSpec as P

TILE = 64
EPSILON = 1e-05
MESH = pl.DeviceIdType.MESH
F32 = jnp.float32
BF16 = jnp.bfloat16

ROWS = 128
PAIRS = 32
EDGE = 16
GROUPS = 16
OWN = 128
LANES = PAIRS * 128
SPLIT = 4


def elu(v):
    return jnp.where(v > 0, v, jnp.exp(jnp.minimum(v, 0.0)) - 1.0)


def kernel(
    n_row, n_col,
    pair, mask_in, w1_in, b1_in, w2_in, b2_in, gain_in, wp_in,
    out,
    mask, w1, b1, w2, b2, gain, wp, xe, xm, xp, hb, wt1, wt2, hs, xs, racc, cacc, csum, compact, landed, side, side_pre, edge_pre, gather, rsend, csend, rrecv, crecv, res,
    ready, known, load_sem, small_sem, halo_send, halo_recv, row_send, row_recv, col_send, col_recv,
):
    r = lax.axis_index("row")
    c = lax.axis_index("col")
    me = r * n_col + c
    n_all = n_row * n_col

    loads = [
        pltpu.make_async_copy(
            pair.at[pl.ds(start, size)], xe.at[pl.ds(EDGE + start, size), pl.ds(OWN, LANES)], load_sem.at[k]
        )
        for k, (start, size) in enumerate(((0, EDGE), (ROWS - EDGE, EDGE), (EDGE, ROWS - 2 * EDGE)))
    ]
    small = [(mask_in, mask), (w1_in, w1), (w2_in, w2), (b1_in, b1), (b2_in, b2), (gain_in, gain), (wp_in, wp)]
    small = [
        pltpu.make_async_copy(src, dst, small_sem.at[k]) for k, (src, dst) in enumerate(small)
    ]
    barrier = pltpu.get_barrier_semaphore()

    def greet(semaphore, tr, tc):
        pl.semaphore_signal(semaphore, inc=1, device_id=(tr, tc), device_id_type=MESH)

    up, down = lax.rem(r + n_row - 1, n_row), lax.rem(r + 1, n_row)
    left, right = lax.rem(c + n_col - 1, n_col), lax.rem(c + 1, n_col)
    above, below, whole = pl.ds(0, EDGE), pl.ds(EDGE + ROWS, EDGE), pl.ds(EDGE, ROWS)
    before, after = pl.ds(0, 128), pl.ds(OWN + LANES, 128)
    first, last = pl.ds(OWN, 128), pl.ds(OWN + LANES - 128, 128)
    top, bottom = pl.ds(EDGE, EDGE), pl.ds(ROWS, EDGE)
    inner, low, high = pl.ds(EDGE, ROWS), pl.ds(0, EDGE), pl.ds(EDGE + ROWS, EDGE)
    has_up, has_down, has_left, has_right = r > 0, r < n_row - 1, c > 0, c < n_col - 1
    halos = [
        (has_up, up, c, compact.at[0, pl.ds(16, 32)], landed.at[1, pl.ds(16, 32)]),
        (has_down, down, c, compact.at[3, pl.ds(16, 32)], landed.at[0, pl.ds(16, 32)]),
        (has_left, r, left, xe.at[whole, first], side.at[1, inner]),
        (has_right, r, right, xe.at[whole, last], side.at[0, inner]),
        (has_up & has_left, up, left, xe.at[top, first], side.at[1, high]),
        (has_up & has_right, up, right, xe.at[top, last], side.at[0, high]),
        (has_down & has_left, down, left, xe.at[bottom, first], side.at[1, low]),
        (has_down & has_right, down, right, xe.at[bottom, last], side.at[0, low]),
    ]
    near = (lax.rem(r + 2, n_row), lax.rem(r + n_row - 2, n_row))
    for present, tr, tc, _, _ in halos[:2] + halos[4:]:
        @pl.when(present)
        def _():
            greet(barrier, tr, tc)

    for k in (8, 7, 9, 6, 10, 5, 11, 4, 12, 3, 13, 2, 14, 1, 15):
        greet(barrier, r, lax.rem(c + k, n_col))
    for tr in near:
        greet(barrier, tr, c)
    for copy in loads + small:
        copy.start()
    part = lax.rem(me, 8)

    xe[above, :] = jnp.zeros((EDGE, xe.shape[1]), BF16)
    xe[below, :] = jnp.zeros((EDGE, xe.shape[1]), BF16)
    xe[whole, before] = jnp.zeros((ROWS, 128), BF16)
    xe[whole, after] = jnp.zeros((ROWS, 128), BF16)
    for k in range(2):
        landed[k, pl.ds(0, 16), :] = jnp.zeros((16, 256), BF16)
        landed[k, pl.ds(48, 16), :] = jnp.zeros((16, 256), BF16)
    for k in range(4):
        compact[k, pl.ds(0, 16), :] = jnp.zeros((16, 256), BF16)
        compact[k, pl.ds(48, 16), :] = jnp.zeros((16, 256), BF16)

    for k, present, place in ((0, has_up, low), (1, has_down, high)):
        @pl.when(jnp.logical_not(present))
        def _():
            landed[k, pl.ds(16, 32), :] = jnp.zeros((32, 256), BF16)
            side[:, place] = jnp.zeros((2, EDGE, 128), BF16)

    for k, present in ((0, has_left), (1, has_right)):
        @pl.when(jnp.logical_not(present))
        def _():
            side[k] = jnp.zeros((ROWS + 2 * EDGE, 128), BF16)

    row_edge = ((c == 0) & has_up) | ((c == n_col - 1) & has_down)
    col_edge = ((part == 0) & (me > 0)) | ((part == 7) & (me < n_all - 1))

    @pl.when(jnp.logical_not(row_edge))
    def _():
        rrecv[pl.ds(n_col, n_col)] = jnp.zeros((n_col, 4, 128), F32)

    @pl.when(jnp.logical_not(col_edge))
    def _():
        crecv[pl.ds(n_row, n_row)] = jnp.zeros((n_row, 4, 128), F32)

    i = lax.broadcasted_iota(jnp.int32, (64, 256), 0)
    j = lax.broadcasted_iota(jnp.int32, (64, 256), 1)
    for k in range(2):
        loads[k].wait()
        cells = jnp.concatenate(
            [xe[pl.ds(EDGE + (ROWS - EDGE) * k, EDGE), pl.ds(OWN + 256 * g, 256)] for g in range(GROUPS)], axis=0
        )
        row = (EDGE - 4) * k + (i // 32) * 2 + i % 2
        select = jnp.where(j == (i % 32 // 2) * 16 + row, 1.0, 0.0).astype(BF16)
        both = jnp.dot(select, cells, preferred_element_type=F32).astype(BF16)
        compact[2 * k, pl.ds(16, 32), :] = both[:32]
        compact[2 * k + 1, pl.ds(16, 32), :] = both[32:]

    for copy in small:
        copy.wait()

    zero = jnp.zeros((64, 64), BF16)
    wt1[...] = jnp.zeros_like(wt1)
    for a in range(3):
        for b in range(3):
            w = w1[a, b]
            doubled = jnp.concatenate(
                [jnp.concatenate([w, zero], axis=1), jnp.concatenate([zero, w], axis=1)], axis=0
            )
            for n in range(2):
                wt1[pl.ds(a * 512 + (b + n) * 128, 128), pl.ds(n * 128, 128)] = doubled
            w = w2[a, b]
            wt2[pl.ds((a * 3 + b) * 128, 128), :] = jnp.concatenate(
                [jnp.concatenate([w, zero], axis=1), jnp.concatenate([zero, w], axis=1)], axis=0
            )
    bias_one = jnp.concatenate([b1[...]] * 4, axis=1)
    bias_two = jnp.concatenate([b2[...]] * 2, axis=1)

    def tile(t, v):
        ti = 2 * r - 1 + t
        tj = c + v
        ok = (ti >= 0) & (ti < 2 * n_row) & (tj >= 0) & (tj < n_col)
        value = mask[jnp.clip(ti, 0, 2 * n_row - 1), jnp.clip(tj, 0, n_col - 1)]
        return jnp.where(ok, value, 0).astype(F32)

    mt = [[tile(t, v) for v in (0, -1, 1)] for t in range(4)]

    def by_row(rows, v):
        return jnp.where(
            rows < 0, mt[0][v], jnp.where(rows < 64, mt[1][v], jnp.where(rows < 128, mt[2][v], mt[3][v]))
        )

    i = lax.broadcasted_iota(jnp.int32, (112, 128), 0)
    j = lax.broadcasted_iota(jnp.int32, (112, 128), 1)
    lower = j // 64
    pair_at = j % 32 // 2 * 2 + j // 32 % 2
    by_column = (lower == i // 32) & (pair_at == i % 32) & (pair_at > 0) & (pair_at < PAIRS - 1)
    kind = (i - 64) // 16
    in_kind = ((kind == 0) & (pair_at >= 2) & (pair_at < PAIRS - 2)) | (
        (kind > 0) & (pair_at == jnp.where(kind == 1, 1, PAIRS - 2))
    )
    by_line = in_kind & (lower == (i // 8) % 2) & (j % 2 + 6 * lower == i % 8)
    gather[...] = jnp.where(((i < 64) & by_column) | ((i >= 64) & by_line), 1.0, 0.0).astype(BF16)

    def expand(buffer, k):
        window = buffer[k]
        return jnp.concatenate([window[14:46, 128:], window[16:48], window[18:50, :128]], axis=1)

    for k in range(2):
        lhs = jnp.concatenate([expand(compact, 2 * k), expand(compact, 2 * k + 1)], axis=1)
        edge_pre[k] = (
            jnp.dot(lhs, wt1[pl.ds(512 * (1 - k), 1024), :], preferred_element_type=F32) + bias_one
        )

    loads[2].wait()
    combos = [(a, v) for a in range(3) for v in range(3)]
    at = lax.broadcasted_iota(jnp.int32, (16, 128), 1)
    which = lax.broadcasted_iota(jnp.int32, (16, 128), 0)
    own_at = by_row(at, 0)
    pick = jnp.zeros((16, 128), F32)
    for k, (a, v) in enumerate(combos):
        pick = jnp.where(which == k, by_row(at - 4 * (a - 1), v), pick)
    pick = pick * own_at
    inside = jnp.where((at >= 2) & (at < ROWS - 2), pick, 0.0)
    inside = inside.astype(BF16)
    pick = pick.astype(BF16)
    for g in range(GROUPS):
        sums = jnp.dot(
            own_at.astype(BF16), xe[pl.ds(EDGE, ROWS), pl.ds(OWN + g * 256, 256)], preferred_element_type=F32
        )
        csum[pl.ds(g * 32, 16), :] = sums[:, :128]
        csum[pl.ds(g * 32 + 16, 16), :] = sums[:, 128:]
    cacc[...] = jnp.zeros_like(cacc)
    cacc[pl.ds(8, PAIRS), :] = csum[pl.ds(0, PAIRS, stride=16), :] + bias_two * (
        64.0 * (mt[1][0] + mt[2][0])
    )


    @pl.loop(0, ROWS // 16)
    def _(k):
        r0 = pl.multiple_of(16 * k, 16)
        cells = xe[pl.ds(EDGE + r0, 16), pl.ds(OWN, LANES)].astype(F32)
        xs[pl.ds(r0, 16), :] = functools.reduce(
            jnp.add, [cells[:, p * 128 : (p + 1) * 128] for p in range(PAIRS)]
        )

    beside = has_up.astype(jnp.int32) + has_down.astype(jnp.int32)
    corners = beside * (has_left.astype(jnp.int32) + has_right.astype(jnp.int32))
    pl.semaphore_wait(barrier, (n_col - 1) + beside + len(near) + corners)
    copies = []
    for k in (0, 1, 4, 5, 6, 7, 2, 3):
        present, tr, tc, src, dst = halos[k]
        copy = pltpu.make_async_remote_copy(
            src_ref=src, dst_ref=dst, send_sem=halo_send.at[k], recv_sem=halo_recv.at[k],
            device_id=(tr, tc), device_id_type=MESH,
        )
        copies.append((present, k, copy))

        @pl.when(present)
        def _():
            copy.start()

    for present, tr, tc, _, _ in halos[:2]:
        @pl.when(present)
        def _():
            greet(known, tr, tc)

    for tr in near:
        greet(known, tr, c)

    def fold(parts):
        both = functools.reduce(jnp.add, parts)
        return both[:, :128] + both[:, 128:]

    def split(values):
        high_part = values.astype(BF16)
        return jnp.concatenate([high_part, (values - high_part.astype(F32)).astype(BF16)], axis=0)

    def rows_of(k):
        r0 = pl.multiple_of(16 * k, 16)
        window = xe[pl.ds(r0, 48), :]
        xm[...] = window[14:30]
        xp[...] = window[18:34]
        lhs = []
        for g in range(GROUPS):
            lanes = pl.ds(g * 256, 512)
            lhs.append(jnp.concatenate([xm[:, lanes], xe[pl.ds(EDGE + r0, 16), lanes], xp[:, lanes]], axis=1))
        pre = jnp.dot(jnp.concatenate(lhs, axis=0), wt1[...], preferred_element_type=F32) + bias_one
        side_pre[0, pl.ds(r0, 16), :] = pre[:16, :128]
        side_pre[1, pl.ds(r0, 16), :] = pre[-16:, 128:]
        h = elu(pre)
        parts = [h[16 * g : 16 * g + 16] for g in range(GROUPS)]
        for g, piece in enumerate(parts):
            hb[pl.ds(r0, 16), pl.ds(g * 256, 256)] = piece.astype(BF16)
        at_row = r0 + lax.broadcasted_iota(jnp.int32, (16, 128), 0)
        final = (at_row >= 2) & (at_row < ROWS - 2)
        for n, value in enumerate((parts[0][:, 128:], fold(parts[1:-1]), parts[-1][:, :128])):
            hs[n, pl.ds(r0, 16), :] = jnp.where(final, value, 0.0)

    pl.loop(0, SPLIT)(rows_of)

    pl.semaphore_wait(known, len(near) + beside)
    odd = lax.rem(c, 2)
    owner_row, edge_row = c // 2, c // 2 - 1 + 2 * odd
    edge_exists = (edge_row >= 0) & (edge_row < n_row)

    for n, tells in ((0, r == owner_row), (1, edge_exists & (r == edge_row))):
        @pl.when(tells)
        def _():
            for k in range(1, n_row):
                greet(ready.at[n], lax.rem(r + k, n_row), c)

    pl.loop(SPLIT, ROWS // 16)(rows_of)

    for g in range(GROUPS):
        sums = jnp.dot(inside, hb[:, pl.ds(g * 256, 256)], preferred_element_type=F32)
        csum[pl.ds(g * 32, 16), :] = sums[:, :128]
        csum[pl.ds(g * 32 + 16, 16), :] = sums[:, 128:]

    sender = (has_down, has_up, has_right, has_left, has_down & has_right, has_down & has_left,
              has_up & has_right, has_up & has_left)
    for _, k, copy in copies:
        @pl.when(sender[k])
        def _():
            copy.wait_recv()

    edges = []
    for k in range(2):
        edges.append(jnp.dot(expand(landed, k), wt1[pl.ds(1024 * k, 512), :], preferred_element_type=F32))
    line = lax.broadcasted_iota(jnp.int32, (8, 128), 0)
    flat = []
    for k in range(2):
        window = side[k]
        lhs = jnp.concatenate([window[14:142], window[16:144], window[18:146]], axis=1)
        taps = jnp.concatenate([wt1[pl.ds(a * 512 + 256 * k, 128), pl.ds(0, 128)] for a in range(3)], axis=0)
        term = jnp.dot(lhs, taps, preferred_element_type=F32)
        value = side_pre[k] + term
        if k == 0:
            head, tail = edges[0][:8, :128], pltpu.roll(edges[1][:8, :128], 6, 0)
        else:
            head, tail = pltpu.roll(edges[0][24:, 128:], 2, 0), edges[1][24:, 128:]
        value = jnp.concatenate(
            [
                value[:8] + jnp.where(line < 2, head, 0.0),
                value[8:120],
                value[120:] + jnp.where(line >= 6, tail, 0.0),
            ],
            axis=0,
        )
        flat.append(elu(value))
    sums = jnp.dot(
        pick, jnp.concatenate([v.astype(BF16) for v in flat], axis=1), preferred_element_type=F32
    )
    csum[pl.ds(0, 16), :] = sums[:, :128]
    csum[pl.ds(16 * (PAIRS - 1), 16), :] = sums[:, 128:]
    edges = [elu(edge_pre[k] + edges[k]).astype(BF16) for k in range(2)]
    cells = jnp.concatenate([edges[0][:, :128], edges[0][:, 128:], edges[1][:, :128], edges[1][:, 128:]], axis=0)
    found = jnp.dot(gather[...], cells, preferred_element_type=F32)

    def column(a, v):
        upper = mt[1][0] * (mt[0][v] if a == 2 else mt[1][v])
        under = mt[2][0] * (mt[3][v] if a == 0 else mt[2][v])
        return csum[pl.ds(3 * a + v, PAIRS, stride=16), :] + upper * found[:32] + under * found[32:64]

    at_pair = lax.broadcasted_iota(jnp.int32, (PAIRS, 128), 0)
    for b in range(3):
        pieces = []
        for a in range(3):
            value = column(a, 0)
            if b == 0:
                value = jnp.where(at_pair >= PAIRS - 2, column(a, 2), value)
            if b == 2:
                value = jnp.where(at_pair < 2, column(a, 1), value)
            pieces.append(value)
        weights = jnp.concatenate([wt2[pl.ds((a * 3 + b) * 128, 128), :] for a in range(3)], axis=0)
        both = jnp.dot(split(jnp.concatenate(pieces, axis=1)), weights, preferred_element_type=F32)
        cacc[pl.ds(8 - 2 * (b - 1), PAIRS), :] += both[:PAIRS] + both[PAIRS:]
    columns = cacc[pl.ds(4, 40), :]
    for k in range(10):
        csend[k] = columns[4 * k : 4 * k + 4]

    def post(src, dst, send_sem, recv_sem, tr, tc):
        mine = (tr == r) & (tc == c)

        @pl.when(mine)
        def _():
            pltpu.make_async_copy(src, dst, recv_sem).start()

        @pl.when(jnp.logical_not(mine))
        def _():
            pltpu.make_async_remote_copy(
                src_ref=src, dst_ref=dst, send_sem=send_sem, recv_sem=recv_sem, device_id=(tr, tc),
                device_id_type=MESH,
            ).start()

    def col_target(k):
        target = lax.rem(8 * c - 1 + k + n_all, n_all)
        return target // n_col, lax.rem(target, n_col)

    for k, told in ((0, r != owner_row), (1, edge_exists & (r != edge_row))):
        @pl.when(told)
        def _():
            pl.semaphore_wait(ready.at[k], 1)

    for k in range(1, 9):
        post(csend.at[k], crecv.at[r], col_send.at[k], col_recv.at[r], *col_target(k))
    for k, present in ((0, has_left), (9, has_right)):
        @pl.when(present)
        def _():
            post(
                csend.at[k], crecv.at[n_row + r], col_send.at[k], col_recv.at[n_row + r], *col_target(k)
            )

    for k in range(2):
        hs[2 * k] += flat[k]
    for k, n in enumerate((1, 0, 2)):
        hs[n, pl.ds(0, 8), :] += found[64 + 16 * k : 72 + 16 * k]
        hs[n, pl.ds(ROWS - 8, 8), :] += found[72 + 16 * k : 80 + 16 * k]
    rows = lax.broadcasted_iota(jnp.int32, (ROWS, 128), 0)
    own = by_row(rows, 0)
    sum_l, sum_m, sum_r = (hs[k] * own for k in range(3))
    racc[...] = jnp.zeros_like(racc)
    racc[pl.ds(8, ROWS), :] = (xs[...] + 32.0 * bias_two) * own
    for a in range(3):
        out_rows = rows - 4 * (a - 1)
        m0, ml, mr = (by_row(out_rows, v) for v in range(3))
        lhs = split(
            jnp.concatenate(
                [
                    m0 * (sum_l + sum_m) + mr * sum_r,
                    m0 * (sum_l + sum_m + sum_r),
                    m0 * (sum_m + sum_r) + ml * sum_l,
                ],
                axis=1,
            )
        )
        both = jnp.dot(lhs, wt2[pl.ds(a * 384, 384), :], preferred_element_type=F32)
        racc[pl.ds(8 - 4 * (a - 1), ROWS), :] += both[:ROWS] + both[ROWS:]
    racc[...] = racc[...] + pltpu.roll(racc[...], 64, 1)
    half = lax.broadcasted_iota(jnp.int32, (72, 128), 1) < 64
    paired = jnp.where(half, racc[pl.ds(0, 72, stride=2), :], racc[pl.ds(1, 72, stride=2), :])
    for k in range(18):
        rsend[k] = paired[4 * k : 4 * k + 4]


    rrecv[c] = rsend[c + 1]
    for k in range(n_col):
        @pl.when(c != k)
        def _():
            pltpu.make_async_remote_copy(
                src_ref=rsend.at[k + 1], dst_ref=rrecv.at[c], send_sem=row_send.at[k + 1],
                recv_sem=row_recv.at[c], device_id=(r, k), device_id_type=MESH,
            ).start()


    for k, present, tr, tc in ((0, has_up, up, n_col - 1), (17, has_down, down, 0)):
        @pl.when(present)
        def _():
            pltpu.make_async_remote_copy(
                src_ref=rsend.at[k], dst_ref=rrecv.at[n_col + c], send_sem=row_send.at[k],
                recv_sem=row_recv.at[n_col + c], device_id=(tr, tc), device_id_type=MESH,
            ).start()

    def arrived(buffer, sem, slot):
        pltpu.make_async_copy(buffer.at[slot], buffer.at[slot], sem.at[slot]).wait()

    for k in range(1, n_col):
        arrived(rrecv, row_recv, lax.rem(c + k, n_col))

    @pl.when(row_edge)
    def _():
        for k in range(n_col):
            arrived(rrecv, row_recv, n_col + k)

    for k in range(n_row):
        arrived(crecv, col_recv, k)

    @pl.when(col_edge)
    def _():
        for k in range(n_row):
            arrived(crecv, col_recv, n_row + k)

    sums = jnp.sum(rrecv[...], axis=0) + jnp.sum(crecv[...], axis=0)
    res[pl.ds(0, 4, stride=2), :] = sums
    res[pl.ds(1, 4, stride=2), :] = pltpu.roll(sums, 64, 1)
    pooled = res[:, :64]
    center = jnp.mean(pooled, axis=1, keepdims=True)
    spread = jnp.mean((pooled - center) ** 2, axis=1, keepdims=True)
    normed = ((pooled - center) / jnp.sqrt(spread + EPSILON) * gain[...]).astype(BF16)
    out[...] = jnp.dot(normed, wp[...], preferred_element_type=F32).astype(BF16)

    for present, _, copy in copies:
        @pl.when(present)
        def _():
            copy.wait_send()

    for k in range(18):
        @pl.when(has_up if k == 0 else has_down if k == 17 else c != k - 1)
        def _():
            pltpu.make_async_copy(rsend.at[k], rsend.at[k], row_send.at[k]).wait()

    for k in range(10):
        tr, tc = col_target(k)

        @pl.when((has_left if k == 0 else has_right if k == 9 else r >= 0) & ((tr != r) | (tc != c)))
        def _():
            pltpu.make_async_copy(csend.at[k], csend.at[k], col_send.at[k]).wait()


def body(pair, tile_mask, w_first, b_first, w_second, b_second, norm_gain, w_proj):
    n_row, n_col = lax.axis_size("row"), lax.axis_size("col")
    hbm = pl.BlockSpec(memory_space=pltpu.HBM)
    return pl.pallas_call(
        functools.partial(kernel, n_row, n_col),
        out_shape=pltpu.VMEM((8, w_proj.shape[1]), BF16),
        in_specs=[hbm] * 8,
        out_specs=pl.BlockSpec(memory_space=pltpu.VMEM),
        scratch_shapes=[
            pltpu.SMEM(tile_mask.shape, jnp.int32),
            pltpu.VMEM(w_first.shape, BF16),
            pltpu.VMEM((1, 64), F32),
            pltpu.VMEM(w_second.shape, BF16),
            pltpu.VMEM((1, 64), F32),
            pltpu.VMEM((1, 64), F32),
            pltpu.VMEM(w_proj.shape, BF16),
            pltpu.VMEM((ROWS + 2 * EDGE, LANES + 256), BF16),
            pltpu.VMEM((16, LANES + 256), BF16),
            pltpu.VMEM((16, LANES + 256), BF16),
            pltpu.VMEM((ROWS, LANES), BF16),
            pltpu.VMEM((1536, 256), BF16),
            pltpu.VMEM((1152, 128), BF16),
            pltpu.VMEM((3, ROWS, 128), F32),
            pltpu.VMEM((ROWS, 128), F32),
            pltpu.VMEM((144, 128), F32),
            pltpu.VMEM((48, 128), F32),
            pltpu.VMEM((512, 128), F32),
            pltpu.VMEM((4, 64, 256), BF16),
            pltpu.VMEM((2, 64, 256), BF16),
            pltpu.VMEM((2, ROWS + 2 * EDGE, 128), BF16),
            pltpu.VMEM((2, ROWS, 128), F32),
            pltpu.VMEM((2, 32, 256), F32),
            pltpu.VMEM((112, 128), BF16),
            pltpu.VMEM((18, 4, 128), F32),
            pltpu.VMEM((10, 4, 128), F32),
            pltpu.VMEM((32, 4, 128), F32),
            pltpu.VMEM((16, 4, 128), F32),
            pltpu.VMEM((8, 128), F32),
            pltpu.SemaphoreType.REGULAR((2,)),
            pltpu.SemaphoreType.REGULAR,
            pltpu.SemaphoreType.DMA((3,)),
            pltpu.SemaphoreType.DMA((7,)),
            pltpu.SemaphoreType.DMA((8,)),
            pltpu.SemaphoreType.DMA((8,)),
            pltpu.SemaphoreType.DMA((18,)),
            pltpu.SemaphoreType.DMA((32,)),
            pltpu.SemaphoreType.DMA((10,)),
            pltpu.SemaphoreType.DMA((16,)),
        ],
        compiler_params=pltpu.CompilerParams(
            collective_id=0, has_side_effects=True, vmem_limit_bytes=48 * 1024 * 1024
        ),
        name="block",
    )(
        *(pltpu.with_memory_space_constraint(v, pltpu.HBM) for v in (
        pair, tile_mask, w_first, b_first.reshape(1, -1), w_second, b_second.reshape(1, -1),
        norm_gain.reshape(1, -1), w_proj,
    )))


def solution(mesh):
    return jax.shard_map(
        body,
        mesh=mesh,
        in_specs=(P("row", "col"), P(), P(), P(), P(), P(), P(), P()),
        out_specs=P(("row", "col"), None),
        check_vma=False,
    )
```

```python
import functools

import jax
import jax.numpy as jnp
from jax import lax
from jax.experimental import pallas as pl
from jax.experimental.pallas import tpu as pltpu
from jax.sharding import PartitionSpec as P

TILE = 64
EPSILON = 1e-05
MESH = pl.DeviceIdType.MESH
F32 = jnp.float32
BF16 = jnp.bfloat16

ROWS = 128
PAIRS = 32
EDGE = 16
GROUPS = 16
OWN = 128
LANES = PAIRS * 128
SPLIT = 5


def elu(v):
    return jnp.where(v > 0, v, jnp.exp(jnp.minimum(v, 0.0)) - 1.0)


def kernel(
    n_row, n_col,
    pair, mask_in, w1_in, b1_in, w2_in, b2_in, gain_in, wp_in,
    out,
    mask, w1, b1, w2, b2, gain, wp, xe, xm, xp, hb, wt1, wt2, hs, xs, racc, cacc, csum, compact, landed, side, side_pre, edge_pre, gather, rsend, csend, rrecv, crecv, res,
    ready, known, load_sem, small_sem, halo_send, halo_recv, row_send, row_recv, col_send, col_recv,
):
    r = lax.axis_index("row")
    c = lax.axis_index("col")
    me = r * n_col + c
    n_all = n_row * n_col

    loads = [
        pltpu.make_async_copy(
            pair.at[pl.ds(start, size)], xe.at[pl.ds(EDGE + start, size), pl.ds(OWN, LANES)], load_sem.at[k]
        )
        for k, (start, size) in enumerate(((0, EDGE), (ROWS - EDGE, EDGE), (EDGE, ROWS - 2 * EDGE)))
    ]
    small = [(mask_in, mask), (w1_in, w1), (w2_in, w2), (b1_in, b1), (b2_in, b2), (gain_in, gain), (wp_in, wp)]
    small = [
        pltpu.make_async_copy(src, dst, small_sem.at[k]) for k, (src, dst) in enumerate(small)
    ]
    barrier = pltpu.get_barrier_semaphore()

    def greet(semaphore, tr, tc):
        pl.semaphore_signal(semaphore, inc=1, device_id=(tr, tc), device_id_type=MESH)

    up, down = lax.rem(r + n_row - 1, n_row), lax.rem(r + 1, n_row)
    left, right = lax.rem(c + n_col - 1, n_col), lax.rem(c + 1, n_col)
    above, below, whole = pl.ds(0, EDGE), pl.ds(EDGE + ROWS, EDGE), pl.ds(EDGE, ROWS)
    before, after = pl.ds(0, 128), pl.ds(OWN + LANES, 128)
    first, last = pl.ds(OWN, 128), pl.ds(OWN + LANES - 128, 128)
    top, bottom = pl.ds(EDGE, EDGE), pl.ds(ROWS, EDGE)
    inner, low, high = pl.ds(EDGE, ROWS), pl.ds(0, EDGE), pl.ds(EDGE + ROWS, EDGE)
    has_up, has_down, has_left, has_right = r > 0, r < n_row - 1, c > 0, c < n_col - 1
    halos = [
        (has_up, up, c, compact.at[0, pl.ds(16, 32)], landed.at[1, pl.ds(16, 32)]),
        (has_down, down, c, compact.at[3, pl.ds(16, 32)], landed.at[0, pl.ds(16, 32)]),
        (has_left, r, left, xe.at[whole, first], side.at[1, inner]),
        (has_right, r, right, xe.at[whole, last], side.at[0, inner]),
        (has_up & has_left, up, left, xe.at[top, first], side.at[1, high]),
        (has_up & has_right, up, right, xe.at[top, last], side.at[0, high]),
        (has_down & has_left, down, left, xe.at[bottom, first], side.at[1, low]),
        (has_down & has_right, down, right, xe.at[bottom, last], side.at[0, low]),
    ]
    near = (lax.rem(r + 2, n_row), lax.rem(r + n_row - 2, n_row))
    for present, tr, tc, _, _ in halos[:2] + halos[4:]:
        @pl.when(present)
        def _():
            greet(barrier, tr, tc)

    for k in (8, 7, 9, 6, 10, 5, 11, 4, 12, 3, 13, 2, 14, 1, 15):
        greet(barrier, r, lax.rem(c + k, n_col))
    for tr in near:
        greet(barrier, tr, c)
    for copy in loads + small:
        copy.start()
    part = lax.rem(me, 8)

    xe[above, :] = jnp.zeros((EDGE, xe.shape[1]), BF16)
    xe[below, :] = jnp.zeros((EDGE, xe.shape[1]), BF16)
    xe[whole, before] = jnp.zeros((ROWS, 128), BF16)
    xe[whole, after] = jnp.zeros((ROWS, 128), BF16)
    for k in range(2):
        landed[k, pl.ds(0, 16), :] = jnp.zeros((16, 256), BF16)
        landed[k, pl.ds(48, 16), :] = jnp.zeros((16, 256), BF16)
    for k in range(4):
        compact[k, pl.ds(0, 16), :] = jnp.zeros((16, 256), BF16)
        compact[k, pl.ds(48, 16), :] = jnp.zeros((16, 256), BF16)

    for k, present, place in ((0, has_up, low), (1, has_down, high)):
        @pl.when(jnp.logical_not(present))
        def _():
            landed[k, pl.ds(16, 32), :] = jnp.zeros((32, 256), BF16)
            side[:, place] = jnp.zeros((2, EDGE, 128), BF16)

    for k, present in ((0, has_left), (1, has_right)):
        @pl.when(jnp.logical_not(present))
        def _():
            side[k] = jnp.zeros((ROWS + 2 * EDGE, 128), BF16)

    row_edge = ((c == 0) & has_up) | ((c == n_col - 1) & has_down)
    col_edge = ((part == 0) & (me > 0)) | ((part == 7) & (me < n_all - 1))

    @pl.when(jnp.logical_not(row_edge))
    def _():
        rrecv[pl.ds(n_col, n_col)] = jnp.zeros((n_col, 4, 128), F32)

    @pl.when(jnp.logical_not(col_edge))
    def _():
        crecv[pl.ds(n_row, n_row)] = jnp.zeros((n_row, 4, 128), F32)

    i = lax.broadcasted_iota(jnp.int32, (64, 256), 0)
    j = lax.broadcasted_iota(jnp.int32, (64, 256), 1)
    for k in range(2):
        loads[k].wait()
        cells = jnp.concatenate(
            [xe[pl.ds(EDGE + (ROWS - EDGE) * k, EDGE), pl.ds(OWN + 256 * g, 256)] for g in range(GROUPS)], axis=0
        )
        row = (EDGE - 4) * k + (i // 32) * 2 + i % 2
        select = jnp.where(j == (i % 32 // 2) * 16 + row, 1.0, 0.0).astype(BF16)
        both = jnp.dot(select, cells, preferred_element_type=F32).astype(BF16)
        compact[2 * k, pl.ds(16, 32), :] = both[:32]
        compact[2 * k + 1, pl.ds(16, 32), :] = both[32:]

    for copy in small:
        copy.wait()

    zero = jnp.zeros((64, 64), BF16)
    wt1[...] = jnp.zeros_like(wt1)
    for a in range(3):
        for b in range(3):
            w = w1[a, b]
            doubled = jnp.concatenate(
                [jnp.concatenate([w, zero], axis=1), jnp.concatenate([zero, w], axis=1)], axis=0
            )
            for n in range(2):
                wt1[pl.ds(a * 512 + (b + n) * 128, 128), pl.ds(n * 128, 128)] = doubled
            w = w2[a, b]
            wt2[pl.ds((a * 3 + b) * 128, 128), :] = jnp.concatenate(
                [jnp.concatenate([w, zero], axis=1), jnp.concatenate([zero, w], axis=1)], axis=0
            )
    bias_one = jnp.concatenate([b1[...]] * 4, axis=1)
    bias_two = jnp.concatenate([b2[...]] * 2, axis=1)

    def tile(t, v):
        ti = 2 * r - 1 + t
        tj = c + v
        ok = (ti >= 0) & (ti < 2 * n_row) & (tj >= 0) & (tj < n_col)
        value = mask[jnp.clip(ti, 0, 2 * n_row - 1), jnp.clip(tj, 0, n_col - 1)]
        return jnp.where(ok, value, 0).astype(F32)

    mt = [[tile(t, v) for v in (0, -1, 1)] for t in range(4)]

    def by_row(rows, v):
        return jnp.where(
            rows < 0, mt[0][v], jnp.where(rows < 64, mt[1][v], jnp.where(rows < 128, mt[2][v], mt[3][v]))
        )

    i = lax.broadcasted_iota(jnp.int32, (112, 128), 0)
    j = lax.broadcasted_iota(jnp.int32, (112, 128), 1)
    lower = j // 64
    pair_at = j % 32 // 2 * 2 + j // 32 % 2
    by_column = (lower == i // 32) & (pair_at == i % 32) & (pair_at > 0) & (pair_at < PAIRS - 1)
    kind = (i - 64) // 16
    in_kind = ((kind == 0) & (pair_at >= 2) & (pair_at < PAIRS - 2)) | (
        (kind > 0) & (pair_at == jnp.where(kind == 1, 1, PAIRS - 2))
    )
    by_line = in_kind & (lower == (i // 8) % 2) & (j % 2 + 6 * lower == i % 8)
    gather[...] = jnp.where(((i < 64) & by_column) | ((i >= 64) & by_line), 1.0, 0.0).astype(BF16)

    def expand(buffer, k):
        window = buffer[k]
        return jnp.concatenate([window[14:46, 128:], window[16:48], window[18:50, :128]], axis=1)

    for k in range(2):
        lhs = jnp.concatenate([expand(compact, 2 * k), expand(compact, 2 * k + 1)], axis=1)
        edge_pre[k] = (
            jnp.dot(lhs, wt1[pl.ds(512 * (1 - k), 1024), :], preferred_element_type=F32) + bias_one
        )

    loads[2].wait()

    @pl.loop(0, ROWS // 16)
    def _(k):
        r0 = pl.multiple_of(16 * k, 16)
        cells = xe[pl.ds(EDGE + r0, 16), pl.ds(OWN, LANES)].astype(F32)
        xs[pl.ds(r0, 16), :] = functools.reduce(
            jnp.add, [cells[:, p * 128 : (p + 1) * 128] for p in range(PAIRS)]
        )

    beside = has_up.astype(jnp.int32) + has_down.astype(jnp.int32)
    corners = beside * (has_left.astype(jnp.int32) + has_right.astype(jnp.int32))
    pl.semaphore_wait(barrier, (n_col - 1) + beside + len(near) + corners)
    copies = []
    for k in (0, 1, 4, 5, 6, 7, 2, 3):
        present, tr, tc, src, dst = halos[k]
        copy = pltpu.make_async_remote_copy(
            src_ref=src, dst_ref=dst, send_sem=halo_send.at[k], recv_sem=halo_recv.at[k],
            device_id=(tr, tc), device_id_type=MESH,
        )
        copies.append((present, k, copy))

        @pl.when(present)
        def _():
            copy.start()

    for present, tr, tc, _, _ in halos[:2]:
        @pl.when(present)
        def _():
            greet(known, tr, tc)

    for tr in near:
        greet(known, tr, c)

    def fold(parts):
        both = functools.reduce(jnp.add, parts)
        return both[:, :128] + both[:, 128:]

    def split(values):
        high_part = values.astype(BF16)
        return jnp.concatenate([high_part, (values - high_part.astype(F32)).astype(BF16)], axis=0)

    def rows_of(k):
        r0 = pl.multiple_of(16 * k, 16)
        window = xe[pl.ds(r0, 48), :]
        xm[...] = window[14:30]
        xp[...] = window[18:34]
        lhs = []
        for g in range(GROUPS):
            lanes = pl.ds(g * 256, 512)
            lhs.append(jnp.concatenate([xm[:, lanes], xe[pl.ds(EDGE + r0, 16), lanes], xp[:, lanes]], axis=1))
        pre = jnp.dot(jnp.concatenate(lhs, axis=0), wt1[...], preferred_element_type=F32) + bias_one
        side_pre[0, pl.ds(r0, 16), :] = pre[:16, :128]
        side_pre[1, pl.ds(r0, 16), :] = pre[-16:, 128:]
        h = elu(pre)
        parts = [h[16 * g : 16 * g + 16] for g in range(GROUPS)]
        for g, piece in enumerate(parts):
            hb[pl.ds(r0, 16), pl.ds(g * 256, 256)] = piece.astype(BF16)
        at_row = r0 + lax.broadcasted_iota(jnp.int32, (16, 128), 0)
        final = (at_row >= 2) & (at_row < ROWS - 2)
        for n, value in enumerate((parts[0][:, 128:], fold(parts[1:-1]), parts[-1][:, :128])):
            hs[n, pl.ds(r0, 16), :] = jnp.where(final, value, 0.0)

    pl.loop(0, SPLIT)(rows_of)

    pl.semaphore_wait(known, len(near) + beside)
    odd = lax.rem(c, 2)
    owner_row, edge_row = c // 2, c // 2 - 1 + 2 * odd
    edge_exists = (edge_row >= 0) & (edge_row < n_row)

    for n, tells in ((0, r == owner_row), (1, edge_exists & (r == edge_row))):
        @pl.when(tells)
        def _():
            for k in range(1, n_row):
                greet(ready.at[n], lax.rem(r + k, n_row), c)

    pl.loop(SPLIT, ROWS // 16)(rows_of)

    combos = [(a, v) for a in range(3) for v in range(3)]
    at = lax.broadcasted_iota(jnp.int32, (16, 128), 1)
    which = lax.broadcasted_iota(jnp.int32, (16, 128), 0)
    own_at = by_row(at, 0)
    pick = jnp.zeros((16, 128), F32)
    for k, (a, v) in enumerate(combos):
        pick = jnp.where(which == k, by_row(at - 4 * (a - 1), v), pick)
    pick = pick * own_at
    inside = jnp.where((at >= 2) & (at < ROWS - 2), pick, 0.0)
    weights = jnp.concatenate([inside, jnp.where(which == 9, own_at, 0.0)], axis=1).astype(BF16)
    pick = pick.astype(BF16)
    for g in range(GROUPS):
        cells = jnp.concatenate(
            [hb[:, pl.ds(g * 256, 256)], xe[pl.ds(EDGE, ROWS), pl.ds(OWN + g * 256, 256)]], axis=0
        )
        sums = jnp.dot(weights, cells, preferred_element_type=F32)
        csum[pl.ds(g * 32, 16), :] = sums[:, :128]
        csum[pl.ds(g * 32 + 16, 16), :] = sums[:, 128:]
    cacc[...] = jnp.zeros_like(cacc)
    cacc[pl.ds(8, PAIRS), :] = csum[pl.ds(9, PAIRS, stride=16), :] + bias_two * (
        64.0 * (mt[1][0] + mt[2][0])
    )

    sender = (has_down, has_up, has_right, has_left, has_down & has_right, has_down & has_left,
              has_up & has_right, has_up & has_left)
    for _, k, copy in copies:
        @pl.when(sender[k])
        def _():
            copy.wait_recv()

    edges = []
    for k in range(2):
        edges.append(jnp.dot(expand(landed, k), wt1[pl.ds(1024 * k, 512), :], preferred_element_type=F32))
    line = lax.broadcasted_iota(jnp.int32, (8, 128), 0)
    flat = []
    for k in range(2):
        window = side[k]
        lhs = jnp.concatenate([window[14:142], window[16:144], window[18:146]], axis=1)
        taps = jnp.concatenate([wt1[pl.ds(a * 512 + 256 * k, 128), pl.ds(0, 128)] for a in range(3)], axis=0)
        term = jnp.dot(lhs, taps, preferred_element_type=F32)
        value = side_pre[k] + term
        if k == 0:
            head, tail = edges[0][:8, :128], pltpu.roll(edges[1][:8, :128], 6, 0)
        else:
            head, tail = pltpu.roll(edges[0][24:, 128:], 2, 0), edges[1][24:, 128:]
        value = jnp.concatenate(
            [
                value[:8] + jnp.where(line < 2, head, 0.0),
                value[8:120],
                value[120:] + jnp.where(line >= 6, tail, 0.0),
            ],
            axis=0,
        )
        flat.append(elu(value))
    sums = jnp.dot(
        pick, jnp.concatenate([v.astype(BF16) for v in flat], axis=1), preferred_element_type=F32
    )
    csum[pl.ds(0, 16), :] = sums[:, :128]
    csum[pl.ds(16 * (PAIRS - 1), 16), :] = sums[:, 128:]
    edges = [elu(edge_pre[k] + edges[k]).astype(BF16) for k in range(2)]
    cells = jnp.concatenate([edges[0][:, :128], edges[0][:, 128:], edges[1][:, :128], edges[1][:, 128:]], axis=0)
    found = jnp.dot(gather[...], cells, preferred_element_type=F32)

    def column(a, v):
        upper = mt[1][0] * (mt[0][v] if a == 2 else mt[1][v])
        under = mt[2][0] * (mt[3][v] if a == 0 else mt[2][v])
        return csum[pl.ds(3 * a + v, PAIRS, stride=16), :] + upper * found[:32] + under * found[32:64]

    at_pair = lax.broadcasted_iota(jnp.int32, (PAIRS, 128), 0)
    for b in range(3):
        pieces = []
        for a in range(3):
            value = column(a, 0)
            if b == 0:
                value = jnp.where(at_pair >= PAIRS - 2, column(a, 2), value)
            if b == 2:
                value = jnp.where(at_pair < 2, column(a, 1), value)
            pieces.append(value)
        weights = jnp.concatenate([wt2[pl.ds((a * 3 + b) * 128, 128), :] for a in range(3)], axis=0)
        both = jnp.dot(split(jnp.concatenate(pieces, axis=1)), weights, preferred_element_type=F32)
        cacc[pl.ds(8 - 2 * (b - 1), PAIRS), :] += both[:PAIRS] + both[PAIRS:]
    columns = cacc[pl.ds(4, 40), :]
    for k in range(10):
        csend[k] = columns[4 * k : 4 * k + 4]

    def post(src, dst, send_sem, recv_sem, tr, tc):
        mine = (tr == r) & (tc == c)

        @pl.when(mine)
        def _():
            pltpu.make_async_copy(src, dst, recv_sem).start()

        @pl.when(jnp.logical_not(mine))
        def _():
            pltpu.make_async_remote_copy(
                src_ref=src, dst_ref=dst, send_sem=send_sem, recv_sem=recv_sem, device_id=(tr, tc),
                device_id_type=MESH,
            ).start()

    def col_target(k):
        target = lax.rem(8 * c - 1 + k + n_all, n_all)
        return target // n_col, lax.rem(target, n_col)

    for k, told in ((0, r != owner_row), (1, edge_exists & (r != edge_row))):
        @pl.when(told)
        def _():
            pl.semaphore_wait(ready.at[k], 1)

    for k in range(1, 9):
        post(csend.at[k], crecv.at[r], col_send.at[k], col_recv.at[r], *col_target(k))
    for k, present in ((0, has_left), (9, has_right)):
        @pl.when(present)
        def _():
            post(
                csend.at[k], crecv.at[n_row + r], col_send.at[k], col_recv.at[n_row + r], *col_target(k)
            )

    for k in range(2):
        hs[2 * k] += flat[k]
    for k, n in enumerate((1, 0, 2)):
        hs[n, pl.ds(0, 8), :] += found[64 + 16 * k : 72 + 16 * k]
        hs[n, pl.ds(ROWS - 8, 8), :] += found[72 + 16 * k : 80 + 16 * k]
    rows = lax.broadcasted_iota(jnp.int32, (ROWS, 128), 0)
    own = by_row(rows, 0)
    sum_l, sum_m, sum_r = (hs[k] * own for k in range(3))
    racc[...] = jnp.zeros_like(racc)
    racc[pl.ds(8, ROWS), :] = (xs[...] + 32.0 * bias_two) * own
    for a in range(3):
        out_rows = rows - 4 * (a - 1)
        m0, ml, mr = (by_row(out_rows, v) for v in range(3))
        lhs = split(
            jnp.concatenate(
                [
                    m0 * (sum_l + sum_m) + mr * sum_r,
                    m0 * (sum_l + sum_m + sum_r),
                    m0 * (sum_m + sum_r) + ml * sum_l,
                ],
                axis=1,
            )
        )
        both = jnp.dot(lhs, wt2[pl.ds(a * 384, 384), :], preferred_element_type=F32)
        racc[pl.ds(8 - 4 * (a - 1), ROWS), :] += both[:ROWS] + both[ROWS:]
    racc[...] = racc[...] + pltpu.roll(racc[...], 64, 1)
    half = lax.broadcasted_iota(jnp.int32, (72, 128), 1) < 64
    paired = jnp.where(half, racc[pl.ds(0, 72, stride=2), :], racc[pl.ds(1, 72, stride=2), :])
    for k in range(18):
        rsend[k] = paired[4 * k : 4 * k + 4]


    rrecv[c] = rsend[c + 1]
    for k in range(n_col):
        @pl.when(c != k)
        def _():
            pltpu.make_async_remote_copy(
                src_ref=rsend.at[k + 1], dst_ref=rrecv.at[c], send_sem=row_send.at[k + 1],
                recv_sem=row_recv.at[c], device_id=(r, k), device_id_type=MESH,
            ).start()


    for k, present, tr, tc in ((0, has_up, up, n_col - 1), (17, has_down, down, 0)):
        @pl.when(present)
        def _():
            pltpu.make_async_remote_copy(
                src_ref=rsend.at[k], dst_ref=rrecv.at[n_col + c], send_sem=row_send.at[k],
                recv_sem=row_recv.at[n_col + c], device_id=(tr, tc), device_id_type=MESH,
            ).start()

    def arrived(buffer, sem, slot):
        pltpu.make_async_copy(buffer.at[slot], buffer.at[slot], sem.at[slot]).wait()

    for k in range(1, n_col):
        arrived(rrecv, row_recv, lax.rem(c + k, n_col))

    @pl.when(row_edge)
    def _():
        for k in range(n_col):
            arrived(rrecv, row_recv, n_col + k)

    for k in range(n_row):
        arrived(crecv, col_recv, k)

    @pl.when(col_edge)
    def _():
        for k in range(n_row):
            arrived(crecv, col_recv, n_row + k)

    sums = jnp.sum(rrecv[...], axis=0) + jnp.sum(crecv[...], axis=0)
    res[pl.ds(0, 4, stride=2), :] = sums
    res[pl.ds(1, 4, stride=2), :] = pltpu.roll(sums, 64, 1)
    pooled = res[:, :64]
    center = jnp.mean(pooled, axis=1, keepdims=True)
    spread = jnp.mean((pooled - center) ** 2, axis=1, keepdims=True)
    normed = ((pooled - center) / jnp.sqrt(spread + EPSILON) * gain[...]).astype(BF16)
    out[...] = jnp.dot(normed, wp[...], preferred_element_type=F32).astype(BF16)

    for present, _, copy in copies:
        @pl.when(present)
        def _():
            copy.wait_send()

    for k in range(18):
        @pl.when(has_up if k == 0 else has_down if k == 17 else c != k - 1)
        def _():
            pltpu.make_async_copy(rsend.at[k], rsend.at[k], row_send.at[k]).wait()

    for k in range(10):
        tr, tc = col_target(k)

        @pl.when((has_left if k == 0 else has_right if k == 9 else r >= 0) & ((tr != r) | (tc != c)))
        def _():
            pltpu.make_async_copy(csend.at[k], csend.at[k], col_send.at[k]).wait()


def body(pair, tile_mask, w_first, b_first, w_second, b_second, norm_gain, w_proj):
    n_row, n_col = lax.axis_size("row"), lax.axis_size("col")
    hbm = pl.BlockSpec(memory_space=pltpu.HBM)
    return pl.pallas_call(
        functools.partial(kernel, n_row, n_col),
        out_shape=pltpu.VMEM((8, w_proj.shape[1]), BF16),
        in_specs=[hbm] * 8,
        out_specs=pl.BlockSpec(memory_space=pltpu.VMEM),
        scratch_shapes=[
            pltpu.SMEM(tile_mask.shape, jnp.int32),
            pltpu.VMEM(w_first.shape, BF16),
            pltpu.VMEM((1, 64), F32),
            pltpu.VMEM(w_second.shape, BF16),
            pltpu.VMEM((1, 64), F32),
            pltpu.VMEM((1, 64), F32),
            pltpu.VMEM(w_proj.shape, BF16),
            pltpu.VMEM((ROWS + 2 * EDGE, LANES + 256), BF16),
            pltpu.VMEM((16, LANES + 256), BF16),
            pltpu.VMEM((16, LANES + 256), BF16),
            pltpu.VMEM((ROWS, LANES), BF16),
            pltpu.VMEM((1536, 256), BF16),
            pltpu.VMEM((1152, 128), BF16),
            pltpu.VMEM((3, ROWS, 128), F32),
            pltpu.VMEM((ROWS, 128), F32),
            pltpu.VMEM((144, 128), F32),
            pltpu.VMEM((48, 128), F32),
            pltpu.VMEM((512, 128), F32),
            pltpu.VMEM((4, 64, 256), BF16),
            pltpu.VMEM((2, 64, 256), BF16),
            pltpu.VMEM((2, ROWS + 2 * EDGE, 128), BF16),
            pltpu.VMEM((2, ROWS, 128), F32),
            pltpu.VMEM((2, 32, 256), F32),
            pltpu.VMEM((112, 128), BF16),
            pltpu.VMEM((18, 4, 128), F32),
            pltpu.VMEM((10, 4, 128), F32),
            pltpu.VMEM((32, 4, 128), F32),
            pltpu.VMEM((16, 4, 128), F32),
            pltpu.VMEM((8, 128), F32),
            pltpu.SemaphoreType.REGULAR((2,)),
            pltpu.SemaphoreType.REGULAR,
            pltpu.SemaphoreType.DMA((3,)),
            pltpu.SemaphoreType.DMA((7,)),
            pltpu.SemaphoreType.DMA((8,)),
            pltpu.SemaphoreType.DMA((8,)),
            pltpu.SemaphoreType.DMA((18,)),
            pltpu.SemaphoreType.DMA((32,)),
            pltpu.SemaphoreType.DMA((10,)),
            pltpu.SemaphoreType.DMA((16,)),
        ],
        compiler_params=pltpu.CompilerParams(
            collective_id=0, has_side_effects=True, vmem_limit_bytes=48 * 1024 * 1024
        ),
        name="block",
    )(
        *(pltpu.with_memory_space_constraint(v, pltpu.HBM) for v in (
        pair, tile_mask, w_first, b_first.reshape(1, -1), w_second, b_second.reshape(1, -1),
        norm_gain.reshape(1, -1), w_proj,
    )))


def solution(mesh):
    return jax.shard_map(
        body,
        mesh=mesh,
        in_specs=(P("row", "col"), P(), P(), P(), P(), P(), P(), P()),
        out_specs=P(("row", "col"), None),
        check_vma=False,
    )
```
